32 devices in a mesh: dp: 16 (over z, y, core), section: 2 (over x).
Axes of the slice: x: 2, y: 2, z: 4, core: 2. Of those that a mesh axis runs over, the one named last changes fastest.
Arguments:
- layer_inputs: bfloat16 [2, 2048, 4096], P('section', 'dp'), may hold values from -6 to 6
- top_grad: bfloat16 [2048, 4096], P('dp'), may hold values from -2.5 to 2.5
- value_grads: bfloat16 [2, 2048, 128], P('section', 'dp'), may hold values from -6 to 6
- weights: bfloat16 [2, 4096, 128], P('section'), may hold values from -0.09375 to 0.09375
- norm_gains: float32 [2, 4096], P('section'), may hold values from 0.5 to 1.5
- counts: int32 [128], P('dp'), may hold values from 1 to 16, as said below
Outputs:
- input_grads: bfloat16 [2, 2048, 4096], P('section', 'dp')
- weight_grads: float32 [2, 528384], P('section', 'dp')
The draws below stay inside these ranges and needn't reach their ends.
Inputs may be any that keep to these rules, and one draw needn't show every extreme that they name: Entry m of a device's block of counts belongs to its m-th micro-batch; slots at or past the count are padding. Some micro-batch holds 16 live slots and some holds 1.
All inputs are finite; a program needn't handle non-finite values.
Results may differ from the reference program's by a relative error of at most 0.0034.
Values may be sent and summed in bfloat16 or wider, within the bound.
No kernel may reach another device: no remote copies, remote signals or barrier semaphores. Data moves between devices by JAX's collectives and lax.ppermute only.
A program may use at most 64 MiB of HBM per device.

```python
import math
import jax
import jax.numpy as jnp
from jax import lax

D = 4096
R = 128
MB_ROWS = 16
MICRO = 8
SECTIONS = 2
TOKENS = 2048


def draw_counts(key, part):
    total = TOKENS // MB_ROWS
    key_list = jax.random.split(key, 4)
    device_level = jax.random.randint(key_list[0], (total // MICRO,), MB_ROWS // 2, MB_ROWS + 1)
    level = jnp.repeat(device_level, MICRO, total_repeat_length=total)
    raw_draw = jax.random.randint(key_list[1], (total,), 0, 1 << 20) % level + 1
    high_spot = jax.random.randint(key_list[2], (), 0, total)
    low_spot = (high_spot + 1 + jax.random.randint(key_list[3], (), 0, total - 1)) % total
    position = jnp.arange(total)
    raw_draw = jnp.where(position == high_spot, MB_ROWS, raw_draw)
    raw_draw = jnp.where(position == low_spot, 1, raw_draw)
    return raw_draw.astype(jnp.int32)


def block_scale(key, extent, shards, low, top_value):
    def one(dim, blocks):
        steps = jax.random.uniform(jax.random.fold_in(jax.random.fold_in(key, 6), dim), (blocks,), jnp.float32, low / len(shards), top_value / len(shards))
        return jnp.repeat(jnp.exp(steps), extent[dim] // blocks).reshape((-1,) + (1,) * (len(extent) - dim - 1))

    gain = one(*shards[0])
    for cut in shards[1:]:
        gain = gain * one(*cut)
    return gain


def centred(stream_key, shape, deviation, bound, pieces=(), kind=jnp.bfloat16):
    loudness = block_scale(stream_key, shape, pieces, -0.22, 0.18) if pieces else 1.0
    entries = jax.random.normal(stream_key, shape, jnp.float32) * deviation * loudness
    return jnp.minimum(jnp.maximum(entries, -bound), bound).astype(kind)


def setup_inputs(seed: int = 0) -> dict:
    streams_of = jax.random.split(jax.random.key(seed), 7)
    layer_inputs = centred(streams_of[0], (SECTIONS, TOKENS, D), 1.0, 6.0, ((0, 2), (1, 16)))
    top_grad = centred(streams_of[1], (TOKENS, D), 0.35, 2.5, ((0, 16),))
    value_grads = centred(streams_of[2], (SECTIONS, TOKENS, R), 1.0, 6.0, ((0, 2), (1, 16)))
    weights = centred(streams_of[3], (SECTIONS, D, R), D ** -0.5, 0.09375, ((0, 2),))
    norm_gains = jnp.clip(1.0 + 0.1 * jax.random.normal(streams_of[4], (SECTIONS, D), jnp.float32), 0.5, 1.5)
    counts = draw_counts(jax.random.fold_in(streams_of[6], 71), 0)
    return {"layer_inputs": layer_inputs, "top_grad": top_grad, "value_grads": value_grads, "weights": weights, "norm_gains": norm_gains, "counts": counts}


eps_norm = 1e-05

def reference(layer_inputs, top_grad, value_grads, weights, norm_gains, counts):
    slot_index = jnp.arange(MB_ROWS, dtype=jnp.int32)
    live = (slot_index[None, :] < counts[:, None]).reshape(TOKENS)
    factor = 1.0 / math.sqrt(TOKENS)
    carried = top_grad
    grads_list = [None] * SECTIONS
    packs_list = [None] * SECTIONS
    for layer in reversed(range(SECTIONS)):
        inputs_wide = layer_inputs[layer].astype(jnp.float32)
        scale = lax.rsqrt(lax.optimization_barrier(jnp.mean(inputs_wide * inputs_wide, axis=1, keepdims=True)) + eps_norm)
        unit = inputs_wide * scale
        gain_row = norm_gains[layer].astype(jnp.float32)
        normed = (unit * gain_row).astype(jnp.bfloat16)
        masked = jnp.where(live[:, None], value_grads[layer], jnp.zeros((), value_grads.dtype))
        back = lax.dot_general(masked, weights[layer], (((1,), (1,)), ((), ())), preferred_element_type=jnp.float32)
        branch = scale * (gain_row * back - unit * lax.optimization_barrier(jnp.mean(unit * gain_row * back, axis=1, keepdims=True)))
        carried = (carried.astype(jnp.float32) + branch).astype(jnp.bfloat16)
        grads_list[layer] = carried
        weight_term = lax.dot_general(normed, masked, (((0,), (0,)), ((), ())), preferred_element_type=jnp.float32)
        gain_term = lax.optimization_barrier(jnp.sum(unit * back, axis=0))
        packs_list[layer] = jnp.concatenate([gain_term, weight_term.reshape(-1)]) * factor
    return (jnp.stack(grads_list), jnp.stack(packs_list))
```

```python
import functools
import math

import jax
import jax.numpy as jnp
from jax import lax
from jax.experimental import pallas as pl
from jax.experimental.pallas import tpu as pltpu
from jax.sharding import PartitionSpec as P

eps_norm = 1e-05
lanes = 128
tile_width = 512
pair = 2
f32 = jnp.float32
bf16 = jnp.bfloat16
contract_last = (((1,), (1,)), ((), ()))
contract_rows = (((0,), (0,)), ((), ()))


def branch_kernel(first, slots, counts, x, top, v, w, gain, sent, branch, normed, masked, gain_out, back):
    rows, width = sent.shape
    slot = lax.broadcasted_iota(jnp.int32, (slots, v.shape[2]), 0)
    pieces = []
    for k in range(rows // slots):
        piece = v[0, k * slots : (k + 1) * slots, :]
        pieces.append(jnp.where(slot < counts[first + k], piece, jnp.zeros_like(piece)))
    values = jnp.concatenate(pieces, axis=0)
    masked[...] = values
    squares = jnp.zeros((rows, lanes), f32)
    products = jnp.zeros((rows, lanes), f32)
    tiles = [pl.ds(at, tile_width) for at in range(0, width, tile_width)]
    for cut in tiles:
        wide = x[0, :, cut].astype(f32)
        here = lax.dot_general(values, w[0, cut, :], contract_last, preferred_element_type=f32)
        back[:, cut] = here
        square = wide * wide
        product = wide * here * gain[:, cut]
        for at in range(0, tile_width, lanes):
            squares += square[:, at : at + lanes]
            products += product[:, at : at + lanes]
    scale = lax.rsqrt(jnp.sum(squares, axis=1, keepdims=True) / width + eps_norm)
    pull = scale * jnp.sum(products, axis=1, keepdims=True) / width
    for cut in tiles:
        unit = x[0, :, cut].astype(f32) * scale
        here = back[:, cut]
        scaled = gain[:, cut]
        gain_out[:, cut] = jnp.sum(unit * here, axis=0, keepdims=True)
        normed[:, cut] = (unit * scaled).astype(bf16)
        own = scale * (scaled * here - unit * pull)
        branch[:, cut] = own
        sent[:, cut] = (top[:, cut].astype(f32) + own).astype(bf16)


def branch_chunk(chunk, rows, slots, counts, x, top, v, w, gain):
    width = x.shape[2]
    depth = v.shape[2]
    first = chunk * rows // slots
    return pl.pallas_call(
        functools.partial(branch_kernel, first, slots),
        grid=(1,),
        in_specs=[
            pl.BlockSpec(memory_space=pltpu.SMEM),
            pl.BlockSpec((1, rows, width), lambda i: (0, chunk, 0)),
            pl.BlockSpec((rows, width), lambda i: (chunk, 0)),
            pl.BlockSpec((1, rows, depth), lambda i: (0, chunk, 0)),
            pl.BlockSpec(w.shape, lambda i: (0, 0, 0)),
            pl.BlockSpec(gain.shape, lambda i: (0, 0)),
        ],
        out_specs=[
            pl.BlockSpec((rows, width), lambda i: (0, 0)),
            pl.BlockSpec((rows, width), lambda i: (0, 0)),
            pl.BlockSpec((rows, width), lambda i: (0, 0)),
            pl.BlockSpec((rows, depth), lambda i: (0, 0)),
            pl.BlockSpec((1, width), lambda i: (0, 0)),
        ],
        out_shape=[
            jax.ShapeDtypeStruct((rows, width), bf16),
            jax.ShapeDtypeStruct((rows, width), f32),
            jax.ShapeDtypeStruct((rows, width), bf16),
            jax.ShapeDtypeStruct((rows, depth), bf16),
            jax.ShapeDtypeStruct((1, width), f32),
        ],
        scratch_shapes=[pltpu.VMEM((rows, width), f32)],
        compiler_params=pltpu.CompilerParams(vmem_limit_bytes=32 << 20),
        cost_estimate=pl.CostEstimate(flops=2 * rows * width * depth, bytes_accessed=4 << 20, transcendentals=0),
    )(counts, x, top, v, w, gain)


def finish_kernel(start, is_last, top, received, branch, *rest):
    out = rest[-1]
    rows, width = branch.shape
    last = is_last[0] == 1
    for at in range(0, width, tile_width):
        cut = pl.ds(at, tile_width)
        incoming = jnp.where(last, top[:, cut].astype(f32), received[:, cut].astype(f32))
        out[0, :, cut] = (incoming + branch[:, cut]).astype(bf16)


def finish_chunk(chunk, is_last, top, received, branch, previous):
    rows, width = branch.shape
    in_specs = [
        pl.BlockSpec(memory_space=pltpu.SMEM),
        pl.BlockSpec((rows, width), lambda i: (chunk, 0)),
        pl.BlockSpec((rows, width), lambda i: (0, 0)),
        pl.BlockSpec((rows, width), lambda i: (0, 0)),
    ]
    operands = [is_last, top, received, branch]
    aliases = {}
    if previous is not None:
        in_specs.append(pl.BlockSpec(memory_space=pl.ANY))
        operands.append(previous)
        aliases = {4: 0}
    return pl.pallas_call(
        functools.partial(finish_kernel, chunk),
        grid=(1,),
        in_specs=in_specs,
        out_specs=pl.BlockSpec((1, rows, width), lambda i: (0, chunk, 0)),
        out_shape=jax.ShapeDtypeStruct((1,) + top.shape, bf16),
        input_output_aliases=aliases,
        compiler_params=pltpu.CompilerParams(vmem_limit_bytes=32 << 20),
        cost_estimate=pl.CostEstimate(flops=rows * width, bytes_accessed=8 * rows * width, transcendentals=0),
    )(*operands)


def terms_kernel(chunks, owned_rows, core, *refs):
    normed = refs[:chunks]
    masked = refs[chunks : 2 * chunks]
    gains = refs[2 * chunks : 3 * chunks]
    keep, give, total = refs[3 * chunks :]
    width = normed[0].shape[1]
    values = jnp.concatenate([m[...] for m in masked], axis=0)
    gain_rows = width // lanes
    gain_sum = sum(g[...] for g in gains)
    for k in range(gain_rows):
        total[k : k + 1, :] = gain_sum[:, k * lanes : (k + 1) * lanes]
    for at in range(0, width, tile_width):
        cut = pl.ds(at, tile_width)
        tall = jnp.concatenate([n[:, cut] for n in normed], axis=0)
        total[gain_rows + at : gain_rows + at + tile_width, :] = lax.dot_general(
            tall, values, contract_rows, preferred_element_type=f32
        )
    even_core = core[0] == 0
    padded = keep.shape[1]
    for j in range(keep.shape[0]):
        even = total[2 * j * owned_rows : 2 * j * owned_rows + owned_rows, :]
        odd = total[(2 * j + 1) * owned_rows : (2 * j + 2) * owned_rows, :]
        keep[j, :owned_rows, :] = jnp.where(even_core, even, odd)
        give[j, :owned_rows, :] = jnp.where(even_core, odd, even)
        if padded > owned_rows:
            blank = jnp.zeros((padded - owned_rows, lanes), f32)
            keep[j, owned_rows:, :] = blank
            give[j, owned_rows:, :] = blank


def pair_terms(core, normed, masked, gains, owned_rows, owners):
    chunks = len(normed)
    depth = masked[0].shape[1]
    width = normed[0].shape[1]
    padded = -(-owned_rows // 16) * 16
    half = jax.ShapeDtypeStruct((owners // pair, padded, lanes), f32)
    everywhere = pl.BlockSpec(memory_space=pltpu.VMEM)
    return pl.pallas_call(
        functools.partial(terms_kernel, chunks, owned_rows),
        in_specs=[pl.BlockSpec(memory_space=pltpu.SMEM)] + [everywhere] * (3 * chunks),
        out_specs=[everywhere, everywhere],
        out_shape=[half, half],
        scratch_shapes=[pltpu.VMEM((owners * owned_rows, lanes), f32)],
        compiler_params=pltpu.CompilerParams(vmem_limit_bytes=32 << 20),
        cost_estimate=pl.CostEstimate(
            flops=2 * depth * width * depth, bytes_accessed=6 << 20, transcendentals=0
        ),
    )(core, *normed, *masked, *gains)


def weight_owned(normed, masked, gains, factor):
    owners = lax.axis_size("dp")
    width = normed[0].shape[1]
    depth = masked[0].shape[1]
    elements = width + width * depth
    owned = elements // owners
    if depth != lanes or owned % lanes or owners % pair:
        weight_term = lax.dot_general(
            jnp.concatenate(normed, axis=0),
            jnp.concatenate(masked, axis=0),
            contract_rows,
            preferred_element_type=f32,
        )
        flat = jnp.concatenate([sum(gains).reshape(-1), weight_term.reshape(-1)]) * factor
        return lax.psum_scatter(flat, "dp", scatter_dimension=0, tiled=True)
    core = (lax.axis_index("dp") % pair).astype(jnp.int32).reshape(1)
    keep, give = pair_terms(core, normed, masked, gains, owned // lanes, owners)
    taken = lax.ppermute(give, "dp", [(i, i ^ 1) for i in range(owners)])
    chip = (keep + taken).astype(bf16)
    groups = [[i for i in range(owners) if i % pair == c] for c in range(pair)]
    landed = lax.all_to_all(chip, "dp", 0, 0, axis_index_groups=groups, tiled=True)
    total = jnp.sum(landed.astype(f32), axis=0) * factor
    return total[: owned // lanes].reshape(owned)


def shards(layer_inputs, top_grad, value_grads, weights, norm_gains, counts):
    row_count = layer_inputs.shape[1]
    micro_count = counts.shape[0]
    slots = row_count // micro_count
    factor = 1.0 / math.sqrt(row_count * lax.axis_size("dp"))
    sections = lax.axis_size("section")
    section_here = lax.axis_index("section")
    is_last = (section_here == sections - 1).astype(jnp.int32).reshape(1)
    chunks = 4 if micro_count % 4 == 0 else 1
    rows = row_count // chunks
    sent, branch, normed, masked, gains = zip(
        *[
            branch_chunk(c, rows, slots, counts, layer_inputs, top_grad, value_grads, weights, norm_gains)
            for c in range(chunks)
        ]
    )
    received = list(sent)
    for hop in range(sections - 1):
        target = sections - 2 - hop
        for c in range(chunks):
            outgoing = sent[c] if hop == 0 else (received[c].astype(f32) + branch[c]).astype(bf16)
            landed = lax.ppermute(outgoing, "section", [(target + 1, target)])
            received[c] = landed if hop == 0 else jnp.where(section_here == target, landed, received[c])
    owned = weight_owned(normed, masked, gains, factor)
    result = None
    for c in range(chunks):
        result = finish_chunk(c, is_last, top_grad, received[c], branch[c], result)
    return (result, owned[None, :])


def solution(mesh):
    placed = (
        P("section", "dp", None),
        P("dp", None),
        P("section", "dp", None),
        P("section", None, None),
        P("section", None),
        P("dp"),
    )
    return jax.shard_map(
        shards,
        mesh=mesh,
        in_specs=placed,
        out_specs=(P("section", "dp", None), P("section", "dp")),
        check_vma=False,
    )
```

```python
import functools
import math

import jax
import jax.numpy as jnp
from jax import lax
from jax.experimental import pallas as pl
from jax.experimental.pallas import tpu as pltpu
from jax.sharding import PartitionSpec as P

eps_norm = 1e-05
lanes = 128
sublanes = 8
pack_rows = 16
tile_width = 512
pair = 2
f32 = jnp.float32
bf16 = jnp.bfloat16
contract_last = (((1,), (1,)), ((), ()))
contract_rows = (((0,), (0,)), ((), ()))
small_cost = pl.CostEstimate(flops=1 << 20, bytes_accessed=1 << 16, transcendentals=0)
roomy = pltpu.CompilerParams(vmem_limit_bytes=32 << 20)
near = pl.BlockSpec(memory_space=pltpu.VMEM)
scalar = pl.BlockSpec(memory_space=pltpu.SMEM)


def far(array):
    return pltpu.with_memory_space_constraint(array, pltpu.HBM)


def cuts(width, step):
    return [pl.ds(at, step) for at in range(0, width, step)]


def one_hot(counts, micro_count, slots, low, size):
    slot = lax.broadcasted_iota(jnp.int32, (slots, size), 0)
    column = lax.broadcasted_iota(jnp.int32, (slots, size), 1) + low
    start = jnp.int32(0)
    pieces = []
    for m in range(micro_count):
        hit = (slot < counts[m]) & (slot + start == column)
        pieces.append(jnp.where(hit, 1.0, 0.0))
        start = start + counts[m]
    return jnp.concatenate(pieces, axis=0).astype(bf16)


def branch_kernel(
    counts_far, x_far, top_far, v_far, w_far, gain_far,
    sent, packed, branch, normed, masked, gain_out,
    counts, x, top, v, w, gain, back, gain_part, ready,
):
    rows, width = sent.shape
    micro_count = counts.shape[0]
    slots = rows // micro_count
    fetches = [
        pltpu.make_async_copy(v_far.at[0], v, ready.at[0]),
        pltpu.make_async_copy(counts_far, counts, ready.at[1]),
        pltpu.make_async_copy(w_far.at[0], w, ready.at[2]),
        pltpu.make_async_copy(x_far.at[0], x, ready.at[3]),
        pltpu.make_async_copy(gain_far, gain, ready.at[4]),
        pltpu.make_async_copy(top_far, top, ready.at[5]),
    ]
    for fetch in fetches:
        fetch.start()
    fetches[0].wait()
    fetches[1].wait()
    slot = lax.broadcasted_iota(jnp.int32, (slots, v.shape[1]), 0)
    for m in range(micro_count):
        piece = v[m * slots : (m + 1) * slots, :]
        masked[m * slots : (m + 1) * slots, :] = jnp.where(slot < counts[m], piece, jnp.zeros_like(piece))
    gather = one_hot(counts, micro_count, slots, 0, packed.shape[0])
    values = masked[...]
    fetches[2].wait()
    for cut in cuts(width, tile_width):
        back[:, cut] = lax.dot_general(values, w[cut, :], contract_last, preferred_element_type=f32)
    fetches[3].wait()
    fetches[4].wait()
    fetches[5].wait()
    for at in range(0, rows, 32):
        part = slice(at, at + 32)
        squares = jnp.zeros((32, lanes), f32)
        products = jnp.zeros((32, lanes), f32)
        for cut in cuts(width, lanes):
            wide = x[part, cut].astype(f32)
            squares += wide * wide
            products += wide * back[part, cut] * gain[:, cut]
        scale = lax.rsqrt(jnp.sum(squares, axis=1, keepdims=True) / width + eps_norm)
        pull = scale * jnp.sum(products, axis=1, keepdims=True) / width
        for cut in cuts(width, 2 * lanes):
            unit = x[part, cut].astype(f32) * scale
            here = back[part, cut]
            scaled = gain[:, cut]
            product = (unit * here).reshape(32 // sublanes, sublanes, 2 * lanes).sum(axis=0)
            if at:
                product += gain_part[:, cut]
            gain_part[:, cut] = product
            normed[part, cut] = (unit * scaled).astype(bf16)
            own = scale * (scaled * here - unit * pull)
            branch[part, cut] = own
            sent[part, cut] = (top[part, cut].astype(f32) + own).astype(bf16)
    for cut in cuts(width, tile_width):
        packed[:, cut] = lax.dot_general(
            gather, sent[:, cut], contract_rows, preferred_element_type=f32
        ).astype(bf16)
    for cut in cuts(width, tile_width):
        gain_out[:, cut] = jnp.sum(gain_part[:, cut], axis=0, keepdims=True)


def branch_rows(room, counts, x, top, v, w, gain):
    rows, width = top.shape
    depth = v.shape[2]
    return pl.pallas_call(
        branch_kernel,
        in_specs=[pl.BlockSpec(memory_space=pltpu.HBM)] * 6,
        out_specs=[near] * 6,
        out_shape=[
            jax.ShapeDtypeStruct((rows, width), bf16),
            jax.ShapeDtypeStruct((room, width), bf16),
            jax.ShapeDtypeStruct((rows, width), f32),
            jax.ShapeDtypeStruct((rows, width), bf16),
            jax.ShapeDtypeStruct((rows, depth), bf16),
            jax.ShapeDtypeStruct((1, width), f32),
        ],
        scratch_shapes=[
            pltpu.SMEM(counts.shape, jnp.int32),
            pltpu.VMEM((rows, width), bf16),
            pltpu.VMEM((rows, width), bf16),
            pltpu.VMEM((rows, depth), bf16),
            pltpu.VMEM((width, depth), bf16),
            pltpu.VMEM((1, width), f32),
            pltpu.VMEM((rows, width), f32),
            pltpu.VMEM((sublanes, width), f32),
            pltpu.SemaphoreType.DMA((6,)),
        ],
        compiler_params=roomy,
        cost_estimate=small_cost,
    )(*[far(a) for a in (counts, x, top, v, w, gain)])


def pack_kernel(low, counts, sent, packed):
    micro_count = counts.shape[0]
    gather = one_hot(counts, micro_count, sent.shape[0] // micro_count, low, packed.shape[0])
    for cut in cuts(sent.shape[1], tile_width):
        packed[:, cut] = lax.dot_general(
            gather, sent[:, cut], contract_rows, preferred_element_type=f32
        ).astype(bf16)


def pack(low, room, counts, sent):
    return pl.pallas_call(
        functools.partial(pack_kernel, low),
        in_specs=[scalar, near],
        out_specs=near,
        out_shape=jax.ShapeDtypeStruct((room, sent.shape[1]), bf16),
        compiler_params=roomy,
        cost_estimate=small_cost,
    )(counts, sent)


def receive_kernel(low, counts, is_target, received, branch, sent, out_far, out, done):
    rows, width = sent.shape
    micro_count = counts.shape[0]
    slots = rows // micro_count
    scatter = one_hot(counts, micro_count, slots, low, received.shape[0])
    covered = jnp.sum(scatter.astype(f32), axis=1, keepdims=True) * is_target[0].astype(f32) > 0.5
    step = 1024 if width % 1024 == 0 else width
    writes = []
    for k, wide_cut in enumerate(cuts(width, step)):
        for at in range(k * step, (k + 1) * step, tile_width if step % tile_width == 0 else step):
            cut = pl.ds(at, tile_width if step % tile_width == 0 else step)
            incoming = jnp.dot(scatter, received[:, cut], preferred_element_type=f32)
            updated = (incoming + branch[:, cut]).astype(bf16)
            out[:, cut] = jnp.where(covered, updated, sent[:, cut])
        write = pltpu.make_async_copy(out.at[:, wide_cut], out_far.at[:, wide_cut], done.at[k])
        write.start()
        writes.append(write)
    for write in writes:
        write.wait()


def receive(low, counts, is_target, received, branch, sent):
    rows, width = sent.shape
    pieces = width // 1024 if width % 1024 == 0 else 1
    return pl.pallas_call(
        functools.partial(receive_kernel, low),
        in_specs=[scalar, scalar, near, near, near],
        out_specs=pl.BlockSpec(memory_space=pltpu.HBM),
        out_shape=pltpu.HBM((rows, width), bf16),
        scratch_shapes=[pltpu.VMEM((rows, width), bf16), pltpu.SemaphoreType.DMA((pieces,))],
        compiler_params=roomy,
        cost_estimate=small_cost,
    )(counts, is_target, received, branch, sent)


def terms_kernel(owned_rows, core, normed, masked, gain, keep, give, total):
    width = normed.shape[1]
    values = masked[...]
    gain_rows = width // lanes
    for k in range(gain_rows):
        total[k : k + 1, :] = gain[:, k * lanes : (k + 1) * lanes]
    for at in range(0, width, tile_width):
        total[gain_rows + at : gain_rows + at + tile_width, :] = lax.dot_general(
            normed[:, at : at + tile_width], values, contract_rows, preferred_element_type=f32
        )
    even_core = core[0] == 0
    padded = keep.shape[1]
    for j in range(keep.shape[0]):
        even = total[2 * j * owned_rows : (2 * j + 1) * owned_rows, :]
        odd = total[(2 * j + 1) * owned_rows : (2 * j + 2) * owned_rows, :]
        keep[j, :owned_rows, :] = jnp.where(even_core, even, odd)
        give[j, :owned_rows, :] = jnp.where(even_core, odd, even)
        if padded > owned_rows:
            blank = jnp.zeros((padded - owned_rows, lanes), f32)
            keep[j, owned_rows:, :] = blank
            give[j, owned_rows:, :] = blank


def pair_terms(core, normed, masked, gain, owned_rows, owners):
    padded = -(-owned_rows // pack_rows) * pack_rows
    half = jax.ShapeDtypeStruct((owners // pair, padded, lanes), f32)
    return pl.pallas_call(
        functools.partial(terms_kernel, owned_rows),
        in_specs=[scalar, near, near, near],
        out_specs=[near, near],
        out_shape=[half, half],
        scratch_shapes=[pltpu.VMEM((owners * owned_rows, lanes), f32)],
        compiler_params=roomy,
        cost_estimate=small_cost,
    )(core, normed, masked, gain)


def merge_kernel(side, keep, taken, hold, give):
    mine = side[0]
    for k in range(hold.shape[0]):
        here = 2 * k + mine
        there = 2 * k + 1 - mine
        hold[k] = keep[here] + taken[here]
        give[k] = (keep[there] + taken[there]).astype(bf16)


def merge_terms(side, keep, taken):
    half = (keep.shape[0] // 2,) + keep.shape[1:]
    return pl.pallas_call(
        merge_kernel,
        in_specs=[scalar, near, near],
        out_specs=[near, near],
        out_shape=[jax.ShapeDtypeStruct(half, f32), jax.ShapeDtypeStruct(half, bf16)],
        compiler_params=roomy,
        cost_estimate=small_cost,
    )(side, keep, taken)


def split_kernel(place, hold, taken, own, *parts):
    count = hold.shape[0]
    own[...] = hold[place[0]] + taken[place[0]].astype(f32)
    for k in range(1, count):
        at = lax.rem(place[0] + k, count)
        parts[k - 1][...] = (hold[at] + taken[at].astype(f32)).astype(bf16)


def split_terms(place, hold, taken):
    count = hold.shape[0]
    return pl.pallas_call(
        split_kernel,
        in_specs=[scalar, near, near],
        out_specs=[near] * count,
        out_shape=[jax.ShapeDtypeStruct(hold.shape[1:], f32)]
        + [jax.ShapeDtypeStruct(hold.shape[1:], bf16)] * (count - 1),
        compiler_params=roomy,
        cost_estimate=small_cost,
    )(place, hold, taken)


def total_kernel(owned_rows, factor, own, *rest):
    out = rest[-1]
    total = own[...]
    for part in rest[:-1]:
        total += part[...].astype(f32)
    total = total * factor
    for k in range(owned_rows):
        out[:, k * lanes : (k + 1) * lanes] = total[k : k + 1, :]


def total_terms(owned_rows, factor, own, landed):
    return pl.pallas_call(
        functools.partial(total_kernel, owned_rows, factor),
        in_specs=[near] * (1 + len(landed)),
        out_specs=near,
        out_shape=jax.ShapeDtypeStruct((1, owned_rows * lanes), f32),
        compiler_params=roomy,
        cost_estimate=small_cost,
    )(own, *landed)


def plane_sum(owners, owned_rows, factor, spot, keep, taken):
    quad = 2 * pair
    hold, give = merge_terms((spot // pair % 2).reshape(1), keep, taken)
    across = lax.ppermute(give, "dp", [(i, i ^ pair) for i in range(owners)])
    own, *parts = split_terms((spot // quad).reshape(1), hold, across)
    landed = []
    for k, part in enumerate(parts):
        landed.append(lax.ppermute(part, "dp", [(i, (i + quad * (k + 1)) % owners) for i in range(owners)]))
    return total_terms(owned_rows, factor, own, landed)


def weight_owned(normed, masked, gain, factor):
    owners = lax.axis_size("dp")
    width = normed.shape[1]
    depth = masked.shape[1]
    owned = (width + width * depth) // owners
    if depth != lanes or owned % lanes or owners % (2 * pair):
        weight_term = lax.dot_general(normed, masked, contract_rows, preferred_element_type=f32)
        flat = jnp.concatenate([gain.reshape(-1), weight_term.reshape(-1)]) * factor
        return lax.psum_scatter(flat, "dp", scatter_dimension=0, tiled=True)[None, :]
    spot = lax.axis_index("dp").astype(jnp.int32)
    keep, give = pair_terms((spot % pair).reshape(1), normed, masked, gain, owned // lanes, owners)
    taken = lax.ppermute(give, "dp", [(i, i ^ 1) for i in range(owners)])
    return plane_sum(owners, owned // lanes, factor, spot, keep, taken)


def shards(layer_inputs, top_grad, value_grads, weights, norm_gains, counts):
    rows = layer_inputs.shape[1]
    factor = 1.0 / math.sqrt(rows * lax.axis_size("dp"))
    sections = lax.axis_size("section")
    section_here = lax.axis_index("section")
    room = -(-rows * 3 // 4 // pack_rows) * pack_rows
    spare = rows - room
    sent, packed, branch, normed, masked, gain = branch_rows(
        room, counts, layer_inputs, top_grad, value_grads, weights, norm_gains
    )
    result = sent
    overflow = jnp.sum(counts) > room
    for hop in range(sections - 1):
        target = sections - 2 - hop
        is_target = (section_here == target).astype(jnp.int32).reshape(1)
        if hop:
            packed = pack(0, room, counts, result)
        hops = [(target + 1, target)]
        before = result
        landed = lax.ppermute(packed, "section", hops)
        result = receive(0, counts, is_target, landed, branch, before)

        def rest(result):
            landed = lax.ppermute(pack(room, spare, counts, before), "section", hops)
            return receive(room, counts, is_target, landed, branch, result)

        result = lax.cond(overflow, rest, lambda result: result, result)
    owned = weight_owned(normed, masked, gain, factor)
    return (result[None], owned)


def solution(mesh):
    placed = (
        P("section", "dp", None),
        P("dp", None),
        P("section", "dp", None),
        P("section", None, None),
        P("section", None),
        P("dp"),
    )
    return jax.shard_map(
        shards,
        mesh=mesh,
        in_specs=placed,
        out_specs=(P("section", "dp", None), P("section", "dp")),
        check_vma=False,
    )
```

```python
import functools
import math

import jax
import jax.numpy as jnp
from jax import lax
from jax.experimental import pallas as pl
from jax.experimental.pallas import tpu as pltpu
from jax.sharding import PartitionSpec as P

eps_norm = 1e-05
lanes = 128
sublanes = 8
pack_rows = 16
tile_width = 512
pair = 2
f32 = jnp.float32
bf16 = jnp.bfloat16
contract_last = (((1,), (1,)), ((), ()))
contract_rows = (((0,), (0,)), ((), ()))
small_cost = pl.CostEstimate(flops=1 << 20, bytes_accessed=1 << 16, transcendentals=0)
roomy = pltpu.CompilerParams(vmem_limit_bytes=32 << 20)
near = pl.BlockSpec(memory_space=pltpu.VMEM)
scalar = pl.BlockSpec(memory_space=pltpu.SMEM)


def far(array):
    return pltpu.with_memory_space_constraint(array, pltpu.HBM)


def cuts(width, step):
    return [pl.ds(at, step) for at in range(0, width, step)]


def one_hot(counts, micro_count, slots, low, size):
    slot = lax.broadcasted_iota(jnp.int32, (slots, size), 0)
    column = lax.broadcasted_iota(jnp.int32, (slots, size), 1) + low
    start = jnp.int32(0)
    pieces = []
    for m in range(micro_count):
        hit = (slot < counts[m]) & (slot + start == column)
        pieces.append(jnp.where(hit, 1.0, 0.0))
        start = start + counts[m]
    return jnp.concatenate(pieces, axis=0).astype(bf16)


def branch_kernel(
    low, counts_far, x_far, top_far, v_far, w_far, gain_far,
    sent, packed, branch, scatter, more, normed, masked, gain_out,
    counts, x, top, v, w, gain, back, gain_part, ready,
):
    rows, width = sent.shape
    micro_count = counts.shape[0]
    slots = rows // micro_count
    fetches = [
        pltpu.make_async_copy(v_far.at[0], v, ready.at[0]),
        pltpu.make_async_copy(counts_far, counts, ready.at[1]),
        pltpu.make_async_copy(w_far.at[0], w, ready.at[2]),
        pltpu.make_async_copy(x_far.at[0], x, ready.at[3]),
        pltpu.make_async_copy(gain_far, gain, ready.at[4]),
        pltpu.make_async_copy(top_far, top, ready.at[5]),
    ]
    for fetch in fetches:
        fetch.start()
    fetches[0].wait()
    fetches[1].wait()
    slot = lax.broadcasted_iota(jnp.int32, (slots, v.shape[1]), 0)
    for m in range(micro_count):
        piece = v[m * slots : (m + 1) * slots, :]
        masked[m * slots : (m + 1) * slots, :] = jnp.where(slot < counts[m], piece, jnp.zeros_like(piece))
    live = jnp.int32(0)
    for m in range(micro_count):
        live += counts[m]
    more[0] = (live > low + packed.shape[0]).astype(jnp.int32)
    gather = one_hot(counts, micro_count, slots, low, packed.shape[0])
    scatter[...] = gather
    values = masked[...]
    fetches[2].wait()
    for cut in cuts(width, tile_width):
        back[:, cut] = lax.dot_general(values, w[cut, :], contract_last, preferred_element_type=f32)
    fetches[3].wait()
    fetches[4].wait()
    fetches[5].wait()
    for at in range(0, rows, 32):
        part = slice(at, at + 32)
        squares = jnp.zeros((32, lanes), f32)
        products = jnp.zeros((32, lanes), f32)
        for cut in cuts(width, lanes):
            wide = x[part, cut].astype(f32)
            squares += wide * wide
            products += wide * back[part, cut] * gain[:, cut]
        scale = lax.rsqrt(jnp.sum(squares, axis=1, keepdims=True) / width + eps_norm)
        pull = scale * jnp.sum(products, axis=1, keepdims=True) / width
        for cut in cuts(width, 2 * lanes):
            unit = x[part, cut].astype(f32) * scale
            here = back[part, cut]
            scaled = gain[:, cut]
            product = (unit * here).reshape(32 // sublanes, sublanes, 2 * lanes).sum(axis=0)
            if at:
                product += gain_part[:, cut]
            gain_part[:, cut] = product
            normed[part, cut] = (unit * scaled).astype(bf16)
            own = scale * (scaled * here - unit * pull)
            branch[part, cut] = own
            sent[part, cut] = (top[part, cut].astype(f32) + own).astype(bf16)
    for cut in cuts(width, tile_width):
        packed[:, cut] = lax.dot_general(
            gather, sent[:, cut], contract_rows, preferred_element_type=f32
        ).astype(bf16)
    for cut in cuts(width, tile_width):
        gain_out[:, cut] = jnp.sum(gain_part[:, cut], axis=0, keepdims=True)


def branch_rows(low, room, counts, x, top, v, w, gain):
    rows, width = top.shape
    depth = v.shape[2]
    return pl.pallas_call(
        functools.partial(branch_kernel, low),
        in_specs=[pl.BlockSpec(memory_space=pltpu.HBM)] * 6,
        out_specs=[near] * 4 + [scalar] + [near] * 3,
        out_shape=[
            jax.ShapeDtypeStruct((rows, width), bf16),
            jax.ShapeDtypeStruct((room, width), bf16),
            jax.ShapeDtypeStruct((rows, width), f32),
            jax.ShapeDtypeStruct((rows, room), bf16),
            jax.ShapeDtypeStruct((1,), jnp.int32),
            jax.ShapeDtypeStruct((rows, width), bf16),
            jax.ShapeDtypeStruct((rows, depth), bf16),
            jax.ShapeDtypeStruct((1, width), f32),
        ],
        scratch_shapes=[
            pltpu.SMEM(counts.shape, jnp.int32),
            pltpu.VMEM((rows, width), bf16),
            pltpu.VMEM((rows, width), bf16),
            pltpu.VMEM((rows, depth), bf16),
            pltpu.VMEM((width, depth), bf16),
            pltpu.VMEM((1, width), f32),
            pltpu.VMEM((rows, width), f32),
            pltpu.VMEM((sublanes, width), f32),
            pltpu.SemaphoreType.DMA((6,)),
        ],
        compiler_params=roomy,
        cost_estimate=small_cost,
    )(*[far(a) for a in (counts, x, top, v, w, gain)])


def pack_kernel(gather, sent, packed):
    for cut in cuts(sent.shape[1], tile_width):
        packed[:, cut] = lax.dot_general(
            gather[...], sent[:, cut], contract_rows, preferred_element_type=f32
        ).astype(bf16)


def pack(gather, sent):
    return pl.pallas_call(
        pack_kernel,
        in_specs=[near, near],
        out_specs=near,
        out_shape=jax.ShapeDtypeStruct((gather.shape[1], sent.shape[1]), bf16),
        compiler_params=roomy,
        cost_estimate=small_cost,
    )(gather, sent)


def receive_kernel(target, step, scatter, received, branch, sent, more, *rest):
    out_far, more_out, out, done = rest[-4:]
    rows, width = sent.shape
    place = scatter[...]
    here = (lax.axis_index("section") == target).astype(f32)
    covered = jnp.sum(place.astype(f32), axis=1, keepdims=True) * here > 0.5
    writes = []
    for k, wide_cut in enumerate(cuts(width, step)):
        for at in range(k * step, (k + 1) * step, tile_width):
            cut = pl.ds(at, tile_width)
            incoming = jnp.dot(place, received[:, cut], preferred_element_type=f32)
            updated = (incoming + branch[:, cut]).astype(bf16)
            out[:, cut] = jnp.where(covered, updated, sent[:, cut])
        write = pltpu.make_async_copy(out.at[:, wide_cut], out_far.at[0, :, wide_cut], done.at[k])
        write.start()
        writes.append(write)
    for write in writes:
        write.wait()


def receive(target, scatter, received, branch, sent, more, after):
    rows, width = sent.shape
    step = 2 * tile_width if width % (2 * tile_width) == 0 else tile_width
    away = pl.BlockSpec(memory_space=pltpu.HBM)
    return pl.pallas_call(
        functools.partial(receive_kernel, target, step),
        in_specs=[near, near, near, near] + [away] * (1 + len(after)),
        out_specs=[away, away],
        out_shape=[pltpu.HBM((1, rows, width), bf16), pltpu.HBM(more.shape, more.dtype)],
        input_output_aliases={4: 1},
        scratch_shapes=[pltpu.VMEM((rows, width), bf16), pltpu.SemaphoreType.DMA((width // step,))],
        compiler_params=roomy,
        cost_estimate=small_cost,
    )(scatter, received, branch, sent, more, *[far(a) for a in after])


def terms_kernel(owned_rows, normed, masked, gain, keep, give, total):
    width = normed.shape[1]
    values = masked[...]
    gain_rows = width // lanes
    for k in range(gain_rows):
        total[k : k + 1, :] = gain[:, k * lanes : (k + 1) * lanes]
    for at in range(0, width, tile_width):
        total[gain_rows + at : gain_rows + at + tile_width, :] = lax.dot_general(
            normed[:, at : at + tile_width], values, contract_rows, preferred_element_type=f32
        )
    even_core = lax.axis_index("dp") % pair == 0
    padded = keep.shape[1]
    for j in range(keep.shape[0]):
        even = total[2 * j * owned_rows : (2 * j + 1) * owned_rows, :]
        odd = total[(2 * j + 1) * owned_rows : (2 * j + 2) * owned_rows, :]
        keep[j, :owned_rows, :] = jnp.where(even_core, even, odd)
        give[j, :owned_rows, :] = jnp.where(even_core, odd, even)
        if padded > owned_rows:
            blank = jnp.zeros((padded - owned_rows, lanes), f32)
            keep[j, owned_rows:, :] = blank
            give[j, owned_rows:, :] = blank


def pair_terms(normed, masked, gain, owned_rows, owners):
    padded = -(-owned_rows // pack_rows) * pack_rows
    half = jax.ShapeDtypeStruct((owners // pair, padded, lanes), f32)
    return pl.pallas_call(
        functools.partial(terms_kernel, owned_rows),
        in_specs=[near, near, near],
        out_specs=[near, near],
        out_shape=[half, half],
        scratch_shapes=[pltpu.VMEM((owners * owned_rows, lanes), f32)],
        compiler_params=roomy,
        cost_estimate=small_cost,
    )(normed, masked, gain)


def merge_kernel(keep, taken, hold, give):
    mine = lax.axis_index("dp") // pair % 2
    for k in range(hold.shape[0]):
        here = 2 * k + mine
        there = 2 * k + 1 - mine
        hold[k] = keep[here] + taken[here]
        give[k] = (keep[there] + taken[there]).astype(bf16)


def merge_terms(keep, taken):
    half = (keep.shape[0] // 2,) + keep.shape[1:]
    return pl.pallas_call(
        merge_kernel,
        in_specs=[near, near],
        out_specs=[near, near],
        out_shape=[jax.ShapeDtypeStruct(half, f32), jax.ShapeDtypeStruct(half, bf16)],
        compiler_params=roomy,
        cost_estimate=small_cost,
    )(keep, taken)


def split_kernel(hold, taken, own, *parts):
    count = hold.shape[0]
    place = lax.axis_index("dp") // (2 * pair)
    own[...] = hold[place] + taken[place].astype(f32)
    for k in range(1, count):
        at = lax.rem(place + k, count)
        parts[k - 1][...] = (hold[at] + taken[at].astype(f32)).astype(bf16)


def split_terms(hold, taken):
    count = hold.shape[0]
    return pl.pallas_call(
        split_kernel,
        in_specs=[near, near],
        out_specs=[near] * count,
        out_shape=[jax.ShapeDtypeStruct(hold.shape[1:], f32)]
        + [jax.ShapeDtypeStruct(hold.shape[1:], bf16)] * (count - 1),
        compiler_params=roomy,
        cost_estimate=small_cost,
    )(hold, taken)


def total_kernel(owned_rows, factor, own, *rest):
    out = rest[-1]
    total = own[...]
    for part in rest[:-1]:
        total += part[...].astype(f32)
    total = total * factor
    for k in range(owned_rows):
        out[:, k * lanes : (k + 1) * lanes] = total[k : k + 1, :]


def total_terms(owned_rows, factor, own, landed):
    return pl.pallas_call(
        functools.partial(total_kernel, owned_rows, factor),
        in_specs=[near] * (1 + len(landed)),
        out_specs=near,
        out_shape=jax.ShapeDtypeStruct((1, owned_rows * lanes), f32),
        compiler_params=roomy,
        cost_estimate=small_cost,
    )(own, *landed)


def plane_sum(owners, owned_rows, factor, keep, taken):
    quad = 2 * pair
    hold, give = merge_terms(keep, taken)
    across = lax.ppermute(give, "dp", [(i, i ^ pair) for i in range(owners)])
    own, *parts = split_terms(hold, across)
    landed = []
    for k, part in enumerate(parts):
        landed.append(lax.ppermute(part, "dp", [(i, (i + quad * (k + 1)) % owners) for i in range(owners)]))
    return total_terms(owned_rows, factor, own, landed)


def weight_owned(normed, masked, gain, factor):
    owners = lax.axis_size("dp")
    width = normed.shape[1]
    depth = masked.shape[1]
    owned = (width + width * depth) // owners
    if depth != lanes or owned % lanes or owners % (2 * pair):
        weight_term = lax.dot_general(normed, masked, contract_rows, preferred_element_type=f32)
        flat = jnp.concatenate([gain.reshape(-1), weight_term.reshape(-1)]) * factor
        return lax.psum_scatter(flat, "dp", scatter_dimension=0, tiled=True)[None, :]
    keep, give = pair_terms(normed, masked, gain, owned // lanes, owners)
    taken = lax.ppermute(give, "dp", [(i, i ^ 1) for i in range(owners)])
    return plane_sum(owners, owned // lanes, factor, keep, taken)


def shards(layer_inputs, top_grad, value_grads, weights, norm_gains, counts):
    rows = layer_inputs.shape[1]
    factor = 1.0 / math.sqrt(rows * lax.axis_size("dp"))
    sections = lax.axis_size("section")
    room = -(-rows * 3 // 4 // pack_rows) * pack_rows
    spare = rows - room
    inputs = (counts, layer_inputs, top_grad, value_grads, weights, norm_gains)
    result, packed, branch, scatter, more, normed, masked, gain = branch_rows(0, room, *inputs)
    owned = weight_owned(normed, masked, gain, factor)
    for hop in range(sections - 1):
        target = sections - 2 - hop
        hops = [(target + 1, target)]
        before = result
        if hop:
            packed = pack(scatter, before)
        landed = lax.ppermute(packed, "section", hops)
        updated, more = receive(target, scatter, landed, branch, before, more, (owned,))

        def rest(updated):
            sent, packed, branch, scatter, more, *_ = branch_rows(room, spare, *inputs)
            if hop:
                packed = pack(scatter, before)
            landed = lax.ppermute(packed, "section", hops)
            return receive(target, scatter, landed, branch, updated[0], more, ())[0]

        updated = lax.cond(more.reshape(()) > 0, rest, lambda updated: updated, updated)
        result = updated[0]
    return (result[None], owned)


def solution(mesh):
    placed = (
        P("section", "dp", None),
        P("dp", None),
        P("section", "dp", None),
        P("section", None, None),
        P("section", None),
        P("dp"),
    )
    return jax.shard_map(
        shards,
        mesh=mesh,
        in_specs=placed,
        out_specs=(P("section", "dp", None), P("section", "dp")),
        check_vma=False,
    )
```

```python
import functools
import math

import jax
import jax.numpy as jnp
from jax import lax
from jax.experimental import pallas as pl
from jax.experimental.pallas import tpu as pltpu
from jax.sharding import PartitionSpec as P

eps_norm = 1e-05
lanes = 128
sublanes = 8
pack_rows = 16
tile_width = 512
pair = 2
f32 = jnp.float32
bf16 = jnp.bfloat16
contract_last = (((1,), (1,)), ((), ()))
contract_rows = (((0,), (0,)), ((), ()))
small_cost = pl.CostEstimate(flops=1 << 20, bytes_accessed=1 << 16, transcendentals=0)
roomy = pltpu.CompilerParams(vmem_limit_bytes=32 << 20)
near = pl.BlockSpec(memory_space=pltpu.VMEM)
scalar = pl.BlockSpec(memory_space=pltpu.SMEM)


def far(array):
    return pltpu.with_memory_space_constraint(array, pltpu.HBM)


def cuts(width, step):
    return [pl.ds(at, step) for at in range(0, width, step)]


def one_hot(counts, micro_count, slots, low, size):
    slot = lax.broadcasted_iota(jnp.int32, (slots, size), 0)
    column = lax.broadcasted_iota(jnp.int32, (slots, size), 1) + low
    start = jnp.int32(0)
    pieces = []
    for m in range(micro_count):
        hit = (slot < counts[m]) & (slot + start == column)
        pieces.append(jnp.where(hit, 1.0, 0.0))
        start = start + counts[m]
    return jnp.concatenate(pieces, axis=0).astype(bf16)


def branch_kernel(
    low, counts_far, x_far, top_far, v_far, w_far, gain_far,
    packed, addend, scatter, more, normed, masked, gain_out,
    counts, x, top, v, w, gain, back, gain_part, sent, ready,
):
    rows, width = addend.shape
    micro_count = counts.shape[0]
    slots = rows // micro_count
    fetches = [
        pltpu.make_async_copy(v_far.at[0], v, ready.at[0]),
        pltpu.make_async_copy(counts_far, counts, ready.at[1]),
        pltpu.make_async_copy(w_far.at[0], w, ready.at[2]),
        pltpu.make_async_copy(x_far.at[0], x, ready.at[3]),
        pltpu.make_async_copy(gain_far, gain, ready.at[4]),
        pltpu.make_async_copy(top_far, top, ready.at[5]),
    ]
    for fetch in fetches:
        fetch.start()
    fetches[0].wait()
    fetches[1].wait()
    slot = lax.broadcasted_iota(jnp.int32, (slots, v.shape[1]), 0)
    for m in range(micro_count):
        piece = v[m * slots : (m + 1) * slots, :]
        masked[m * slots : (m + 1) * slots, :] = jnp.where(slot < counts[m], piece, jnp.zeros_like(piece))
    live = jnp.int32(0)
    for m in range(micro_count):
        live += counts[m]
    more[0] = (live > low + packed.shape[0]).astype(jnp.int32)
    gather = one_hot(counts, micro_count, slots, low, packed.shape[0])
    receives = lax.axis_index("section") < lax.axis_size("section") - 1
    scatter[...] = jnp.where(receives, gather.astype(f32), 0.0).astype(bf16)
    values = masked[...]
    fetches[2].wait()
    for cut in cuts(width, tile_width):
        back[:, cut] = lax.dot_general(values, w[cut, :], contract_last, preferred_element_type=f32)
    fetches[3].wait()
    fetches[4].wait()
    fetches[5].wait()
    for at in range(0, rows, 32):
        part = slice(at, at + 32)
        squares = jnp.zeros((32, lanes), f32)
        products = jnp.zeros((32, lanes), f32)
        for cut in cuts(width, lanes):
            wide = x[part, cut].astype(f32)
            squares += wide * wide
            products += wide * back[part, cut] * gain[:, cut]
        scale = lax.rsqrt(jnp.sum(squares, axis=1, keepdims=True) / width + eps_norm)
        pull = scale * jnp.sum(products, axis=1, keepdims=True) / width
        waits = jnp.concatenate(
            [
                lax.broadcasted_iota(jnp.int32, (slots, 1), 0) < jnp.where(receives, counts[m], 0)
                for m in range(at // slots, (at + 32) // slots)
            ],
            axis=0,
        )
        for cut in cuts(width, 2 * lanes):
            unit = x[part, cut].astype(f32) * scale
            here = back[part, cut]
            scaled = gain[:, cut]
            product = (unit * here).reshape(32 // sublanes, sublanes, 2 * lanes).sum(axis=0)
            if at:
                product += gain_part[:, cut]
            gain_part[:, cut] = product
            normed[part, cut] = (unit * scaled).astype(bf16)
            own = scale * (scaled * here - unit * pull)
            whole = (top[part, cut].astype(f32) + own).astype(bf16)
            sent[part, cut] = whole
            addend[part, cut] = jnp.where(waits, own, whole.astype(f32))
    for cut in cuts(width, tile_width):
        packed[:, cut] = lax.dot_general(
            gather, sent[:, cut], contract_rows, preferred_element_type=f32
        ).astype(bf16)
    for cut in cuts(width, tile_width):
        gain_out[:, cut] = jnp.sum(gain_part[:, cut], axis=0, keepdims=True)


def branch_rows(low, room, counts, x, top, v, w, gain):
    rows, width = top.shape
    depth = v.shape[2]
    return pl.pallas_call(
        functools.partial(branch_kernel, low),
        in_specs=[pl.BlockSpec(memory_space=pltpu.HBM)] * 6,
        out_specs=[near] * 3 + [scalar] + [near] * 3,
        out_shape=[
            jax.ShapeDtypeStruct((room, width), bf16),
            jax.ShapeDtypeStruct((rows, width), f32),
            jax.ShapeDtypeStruct((rows, room), bf16),
            pltpu.SMEM((1,), jnp.int32),
            jax.ShapeDtypeStruct((rows, width), bf16),
            jax.ShapeDtypeStruct((rows, depth), bf16),
            jax.ShapeDtypeStruct((1, width), f32),
        ],
        scratch_shapes=[
            pltpu.SMEM(counts.shape, jnp.int32),
            pltpu.VMEM((rows, width), bf16),
            pltpu.VMEM((rows, width), bf16),
            pltpu.VMEM((rows, depth), bf16),
            pltpu.VMEM((width, depth), bf16),
            pltpu.VMEM((1, width), f32),
            pltpu.VMEM((rows, width), f32),
            pltpu.VMEM((sublanes, width), f32),
            pltpu.VMEM((rows, width), bf16),
            pltpu.SemaphoreType.DMA((6,)),
        ],
        compiler_params=roomy,
        cost_estimate=small_cost,
    )(*[far(a) for a in (counts, x, top, v, w, gain)])


def pack_kernel(gather, sent, packed):
    for cut in cuts(sent.shape[1], tile_width):
        packed[:, cut] = lax.dot_general(
            gather[...], sent[:, cut], contract_rows, preferred_element_type=f32
        ).astype(bf16)


def pack(gather, sent):
    return pl.pallas_call(
        pack_kernel,
        in_specs=[near, near],
        out_specs=near,
        out_shape=jax.ShapeDtypeStruct((gather.shape[1], sent.shape[1]), bf16),
        compiler_params=roomy,
        cost_estimate=small_cost,
    )(gather, sent)


def receive_kernel(target, first, scatter, received, addend, more, *rest):
    out_far, more_out, out, done = rest[-4:]
    more_out[0] = more[0]
    rows, width = addend.shape
    place = scatter[...]
    if not first:
        here = (lax.axis_index("section") == target).astype(f32)
        covered = jnp.sum(place.astype(f32), axis=1, keepdims=True) * here > 0.5
    writes = []
    for k, cut in enumerate(cuts(width, tile_width)):
        total = jnp.dot(place, received[:, cut], preferred_element_type=f32) + addend[:, cut]
        if not first:
            total = jnp.where(covered, total, rest[0][:, cut].astype(f32))
        out[:, cut] = total.astype(bf16)
        write = pltpu.make_async_copy(out.at[:, cut], out_far.at[0, :, cut], done.at[k])
        write.start()
        writes.append(write)
    for write in writes:
        write.wait()


def receive(target, scatter, received, addend, more, after, previous=None):
    rows, width = addend.shape
    away = pl.BlockSpec(memory_space=pltpu.HBM)
    others = [far(a) for a in after] if previous is None else [previous]
    return pl.pallas_call(
        functools.partial(receive_kernel, target, previous is None),
        in_specs=[near, near, near, scalar] + [away if previous is None else near] * len(others),
        out_specs=[away, scalar],
        out_shape=[pltpu.HBM((1, rows, width), bf16), pltpu.SMEM(more.shape, more.dtype)],
        scratch_shapes=[pltpu.VMEM((rows, width), bf16), pltpu.SemaphoreType.DMA((width // tile_width,))],
        compiler_params=roomy,
        cost_estimate=small_cost,
    )(scatter, received, addend, more, *others)


def terms_kernel(owned_rows, normed, masked, gain, keep, give, total):
    width = normed.shape[1]
    values = masked[...]
    gain_rows = width // lanes
    for k in range(gain_rows):
        total[k : k + 1, :] = gain[:, k * lanes : (k + 1) * lanes]
    for at in range(0, width, tile_width):
        total[gain_rows + at : gain_rows + at + tile_width, :] = lax.dot_general(
            normed[:, at : at + tile_width], values, contract_rows, preferred_element_type=f32
        )
    even_core = lax.axis_index("dp") % pair == 0
    padded = keep.shape[1]
    for j in range(keep.shape[0]):
        even = total[2 * j * owned_rows : (2 * j + 1) * owned_rows, :]
        odd = total[(2 * j + 1) * owned_rows : (2 * j + 2) * owned_rows, :]
        keep[j, :owned_rows, :] = jnp.where(even_core, even, odd)
        give[j, :owned_rows, :] = jnp.where(even_core, odd, even)
        if padded > owned_rows:
            blank = jnp.zeros((padded - owned_rows, lanes), f32)
            keep[j, owned_rows:, :] = blank
            give[j, owned_rows:, :] = blank


def pair_terms(normed, masked, gain, owned_rows, owners):
    padded = -(-owned_rows // pack_rows) * pack_rows
    half = jax.ShapeDtypeStruct((owners // pair, padded, lanes), f32)
    return pl.pallas_call(
        functools.partial(terms_kernel, owned_rows),
        in_specs=[near, near, near],
        out_specs=[near, near],
        out_shape=[half, half],
        scratch_shapes=[pltpu.VMEM((owners * owned_rows, lanes), f32)],
        compiler_params=roomy,
        cost_estimate=small_cost,
    )(normed, masked, gain)


def merge_kernel(keep, taken, hold, give, hold_low, *give_low):
    cut = hold.shape[1]
    chip = lax.axis_index("dp") // pair
    mine, place = chip % 2, chip // 2
    count = hold.shape[0]
    for k in range(count):
        here = 2 * k + mine
        there = 2 * k + 1 - mine
        hold[k] = keep[here, :cut, :] + taken[here, :cut, :]
        give[k] = (keep[there, :cut, :] + taken[there, :cut, :]).astype(bf16)
    for side in range(2):
        at = 2 * place + side
        hold_low[side] = keep[at, cut:, :] + taken[at, cut:, :]
        for k in range(1, count):
            at = 2 * lax.rem(place + k, count) + side
            give_low[k - 1][side] = (keep[at, cut:, :] + taken[at, cut:, :]).astype(bf16)


def merge_terms(cut, keep, taken):
    blocks, padded, _ = keep.shape
    count = blocks // 2
    high = (count, cut, lanes)
    low = (2, padded - cut, lanes)
    return pl.pallas_call(
        merge_kernel,
        in_specs=[near, near],
        out_specs=[near] * (2 + count),
        out_shape=[
            jax.ShapeDtypeStruct(high, f32),
            jax.ShapeDtypeStruct(high, bf16),
            jax.ShapeDtypeStruct(low, f32),
        ]
        + [jax.ShapeDtypeStruct(low, bf16)] * (count - 1),
        compiler_params=roomy,
        cost_estimate=small_cost,
    )(keep, taken)


def split_kernel(hold, taken, own, *parts):
    count = hold.shape[0]
    place = lax.axis_index("dp") // (2 * pair)
    own[...] = hold[place] + taken[place].astype(f32)
    for k in range(1, count):
        at = lax.rem(place + k, count)
        parts[k - 1][...] = (hold[at] + taken[at].astype(f32)).astype(bf16)


def split_terms(hold, taken):
    count = hold.shape[0]
    return pl.pallas_call(
        split_kernel,
        in_specs=[near, near],
        out_specs=[near] * count,
        out_shape=[jax.ShapeDtypeStruct(hold.shape[1:], f32)]
        + [jax.ShapeDtypeStruct(hold.shape[1:], bf16)] * (count - 1),
        compiler_params=roomy,
        cost_estimate=small_cost,
    )(hold, taken)


def cross_kernel(hold, *refs):
    *landed, own, give = refs
    mine = lax.axis_index("dp") // pair % 2
    total = hold[mine]
    passed = hold[1 - mine]
    for part in landed:
        total += part[mine].astype(f32)
        passed += part[1 - mine].astype(f32)
    own[...] = total
    give[...] = passed.astype(bf16)


def cross_terms(hold, landed):
    return pl.pallas_call(
        cross_kernel,
        in_specs=[near] * (1 + len(landed)),
        out_specs=[near, near],
        out_shape=[jax.ShapeDtypeStruct(hold.shape[1:], f32), jax.ShapeDtypeStruct(hold.shape[1:], bf16)],
        compiler_params=roomy,
        cost_estimate=small_cost,
    )(hold, *landed)


def total_kernel(owned_rows, factor, own_low, landed_low, own, *rest):
    out = rest[-1]
    total = own[...]
    for part in rest[:-1]:
        total += part[...].astype(f32)
    low = (own_low[...] + landed_low[...].astype(f32)) * factor
    total = total * factor
    cut = total.shape[0]
    for k in range(owned_rows):
        row = total[k : k + 1, :] if k < cut else low[k - cut : k - cut + 1, :]
        out[:, k * lanes : (k + 1) * lanes] = row


def total_terms(owned_rows, factor, own_low, landed_low, own, landed):
    return pl.pallas_call(
        functools.partial(total_kernel, owned_rows, factor),
        in_specs=[near] * (3 + len(landed)),
        out_specs=near,
        out_shape=jax.ShapeDtypeStruct((1, owned_rows * lanes), f32),
        compiler_params=roomy,
        cost_estimate=small_cost,
    )(own_low, landed_low, own, *landed)


def plane_sum(owners, owned_rows, factor, keep, taken):
    quad = 2 * pair
    shifts = range(quad, owners, quad)
    near_by = [(i, i ^ pair) for i in range(owners)]
    farther = [[(i, (i + shift) % owners) for i in range(owners)] for shift in shifts]
    cut = -(-keep.shape[1] * 2 // 3 // pack_rows) * pack_rows
    hold, give, hold_low, *give_low = merge_terms(cut, keep, taken)
    across = lax.ppermute(give, "dp", near_by)
    landed_low = [lax.ppermute(part, "dp", hops) for part, hops in zip(give_low, farther)]
    own, *parts = split_terms(hold, across)
    landed = [lax.ppermute(part, "dp", hops) for part, hops in zip(parts, farther)]
    own_low, cross_low = cross_terms(hold_low, landed_low)
    return total_terms(owned_rows, factor, own_low, lax.ppermute(cross_low, "dp", near_by), own, landed)


def weight_owned(normed, masked, gain, factor):
    owners = lax.axis_size("dp")
    width = normed.shape[1]
    depth = masked.shape[1]
    owned = (width + width * depth) // owners
    if depth != lanes or owned % lanes or owners % (2 * pair):
        weight_term = lax.dot_general(normed, masked, contract_rows, preferred_element_type=f32)
        flat = jnp.concatenate([gain.reshape(-1), weight_term.reshape(-1)]) * factor
        return lax.psum_scatter(flat, "dp", scatter_dimension=0, tiled=True)[None, :]
    keep, give = pair_terms(normed, masked, gain, owned // lanes, owners)
    taken = lax.ppermute(give, "dp", [(i, i ^ 1) for i in range(owners)])
    return plane_sum(owners, owned // lanes, factor, keep, taken)


def shards(layer_inputs, top_grad, value_grads, weights, norm_gains, counts):
    rows = layer_inputs.shape[1]
    factor = 1.0 / math.sqrt(rows * lax.axis_size("dp"))
    sections = lax.axis_size("section")
    room = -(-rows * 3 // 4 // pack_rows) * pack_rows
    spare = rows - room
    inputs = (counts, layer_inputs, top_grad, value_grads, weights, norm_gains)
    packed, addend, scatter, more, normed, masked, gain = branch_rows(0, room, *inputs)
    owned = weight_owned(normed, masked, gain, factor)
    result = None
    for hop in range(sections - 1):
        target = sections - 2 - hop
        hops = [(target + 1, target)]
        before = result
        if hop:
            packed = pack(scatter, before)
        landed = lax.ppermute(packed, "section", hops)
        updated, more = receive(target, scatter, landed, addend, more, (owned,), before)

        def rest(updated):
            packed, addend, scatter, more, *_ = branch_rows(room, spare, *inputs)
            if hop:
                packed = pack(scatter, before)
            landed = lax.ppermute(packed, "section", hops)
            return receive(target, scatter, landed, addend, more, (), updated[0])[0]

        updated = lax.cond(more.reshape(()) > 0, rest, lambda updated: updated, updated)
        result = updated[0]
    return (result[None], owned)


def solution(mesh):
    placed = (
        P("section", "dp", None),
        P("dp", None),
        P("section", "dp", None),
        P("section", None, None),
        P("section", None),
        P("dp"),
    )
    return jax.shard_map(
        shards,
        mesh=mesh,
        in_specs=placed,
        out_specs=(P("section", "dp", None), P("section", "dp")),
        check_vma=False,
    )
```

```python
import functools
import math

import jax
import jax.numpy as jnp
from jax import lax
from jax.experimental import pallas as pl
from jax.experimental.pallas import tpu as pltpu
from jax.sharding import PartitionSpec as P

eps_norm = 1e-05
lanes = 128
sublanes = 8
pack_rows = 16
tile_width = 512
pair = 2
f32 = jnp.float32
bf16 = jnp.bfloat16
contract_last = (((1,), (1,)), ((), ()))
contract_rows = (((0,), (0,)), ((), ()))
small_cost = pl.CostEstimate(flops=1 << 20, bytes_accessed=1 << 16, transcendentals=0)
roomy = pltpu.CompilerParams(vmem_limit_bytes=32 << 20)
near = pl.BlockSpec(memory_space=pltpu.VMEM)
scalar = pl.BlockSpec(memory_space=pltpu.SMEM)


def far(array):
    return pltpu.with_memory_space_constraint(array, pltpu.HBM)


def cuts(width, step):
    return [pl.ds(at, step) for at in range(0, width, step)]


def one_hot(counts, micro_count, slots, low, size):
    slot = lax.broadcasted_iota(jnp.int32, (slots, size), 0)
    column = lax.broadcasted_iota(jnp.int32, (slots, size), 1) + low
    start = jnp.int32(0)
    pieces = []
    for m in range(micro_count):
        hit = (slot < counts[m]) & (slot + start == column)
        pieces.append(jnp.where(hit, 1.0, 0.0))
        start = start + counts[m]
    return jnp.concatenate(pieces, axis=0).astype(bf16)


def branch_kernel(low, sending, counts_far, x_far, top_far, v_far, w_far, gain_far, *refs):
    work = functools.partial(branch_work, low, sending, counts_far, x_far, top_far, v_far, w_far, gain_far)
    if sending is None:
        work(*refs)
        return
    later = lax.axis_index("section") == 0
    pl.when(jnp.logical_not(later) if sending else later)(lambda: work(*refs[0 if sending else 6 :]))


def branch_work(
    low, sending, counts_far, x_far, top_far, v_far, w_far, gain_far,
    addend, scatter, more, normed, masked, gain_out, *refs
):
    if sending is False:
        packed = None
    else:
        packed, *refs = refs
    counts, x, top, v, w, gain, back, gain_part, sent, ready = refs
    room = scatter.shape[1]
    rows, width = addend.shape
    micro_count = counts.shape[0]
    slots = rows // micro_count
    fetches = [
        pltpu.make_async_copy(v_far.at[0], v, ready.at[0]),
        pltpu.make_async_copy(counts_far, counts, ready.at[1]),
        pltpu.make_async_copy(w_far.at[0], w, ready.at[2]),
        pltpu.make_async_copy(x_far.at[0], x, ready.at[3]),
        pltpu.make_async_copy(gain_far, gain, ready.at[4]),
        pltpu.make_async_copy(top_far, top, ready.at[5]),
    ]
    for fetch in fetches:
        fetch.start()
    fetches[0].wait()
    fetches[1].wait()
    slot = lax.broadcasted_iota(jnp.int32, (slots, v.shape[1]), 0)
    for m in range(micro_count):
        piece = v[m * slots : (m + 1) * slots, :]
        masked[m * slots : (m + 1) * slots, :] = jnp.where(slot < counts[m], piece, jnp.zeros_like(piece))
    live = jnp.int32(0)
    for m in range(micro_count):
        live += counts[m]
    more[0] = (live > low + room).astype(jnp.int32)
    gather = one_hot(counts, micro_count, slots, low, room)
    receives = lax.axis_index("section") < lax.axis_size("section") - 1
    scatter[...] = jnp.where(receives, gather.astype(f32), 0.0).astype(bf16)
    values = masked[...]
    fetches[2].wait()
    for cut in cuts(width, tile_width):
        back[:, cut] = lax.dot_general(values, w[cut, :], contract_last, preferred_element_type=f32)
    fetches[3].wait()
    fetches[4].wait()
    fetches[5].wait()
    for at in range(0, rows, 32):
        part = slice(at, at + 32)
        squares = jnp.zeros((32, lanes), f32)
        products = jnp.zeros((32, lanes), f32)
        for cut in cuts(width, lanes):
            wide = x[part, cut].astype(f32)
            squares += wide * wide
            products += wide * back[part, cut] * gain[:, cut]
        scale = lax.rsqrt(jnp.sum(squares, axis=1, keepdims=True) / width + eps_norm)
        pull = scale * jnp.sum(products, axis=1, keepdims=True) / width
        waits = jnp.concatenate(
            [
                lax.broadcasted_iota(jnp.int32, (slots, 1), 0) < jnp.where(receives, counts[m], 0)
                for m in range(at // slots, (at + 32) // slots)
            ],
            axis=0,
        )
        for cut in cuts(width, 2 * lanes):
            unit = x[part, cut].astype(f32) * scale
            here = back[part, cut]
            scaled = gain[:, cut]
            product = (unit * here).reshape(32 // sublanes, sublanes, 2 * lanes).sum(axis=0)
            if at:
                product += gain_part[:, cut]
            gain_part[:, cut] = product
            normed[part, cut] = (unit * scaled).astype(bf16)
            own = scale * (scaled * here - unit * pull)
            whole = (top[part, cut].astype(f32) + own).astype(bf16)
            sent[part, cut] = whole
            addend[part, cut] = jnp.where(waits, own, whole.astype(f32))
    if packed is not None:
        for cut in cuts(width, tile_width):
            packed[:, cut] = lax.dot_general(
                gather, sent[:, cut], contract_rows, preferred_element_type=f32
            ).astype(bf16)
    for cut in cuts(width, tile_width):
        gain_out[:, cut] = jnp.sum(gain_part[:, cut], axis=0, keepdims=True)


def branch_rows(low, room, sending, inputs, made=()):
    counts, x, top, v, w, gain = inputs
    rows, width = top.shape
    depth = v.shape[2]
    outs = [
        jax.ShapeDtypeStruct((rows, width), f32),
        jax.ShapeDtypeStruct((rows, room), bf16),
        pltpu.SMEM((1,), jnp.int32),
        jax.ShapeDtypeStruct((rows, width), bf16),
        jax.ShapeDtypeStruct((rows, depth), bf16),
        jax.ShapeDtypeStruct((1, width), f32),
    ]
    specs = [near, near, scalar, near, near, near]
    aliases = {}
    if made:
        aliases = {6 + k: k for k in range(len(made))}
    extra = [] if made else [jax.ShapeDtypeStruct((room, width), bf16)]
    return pl.pallas_call(
        functools.partial(branch_kernel, low, sending),
        in_specs=[pl.BlockSpec(memory_space=pltpu.HBM)] * 6 + (specs if made else []),
        out_specs=specs + [near] * len(extra),
        out_shape=outs + extra,
        input_output_aliases=aliases,
        scratch_shapes=[
            pltpu.SMEM(counts.shape, jnp.int32),
            pltpu.VMEM((rows, width), bf16),
            pltpu.VMEM((rows, width), bf16),
            pltpu.VMEM((rows, depth), bf16),
            pltpu.VMEM((width, depth), bf16),
            pltpu.VMEM((1, width), f32),
            pltpu.VMEM((rows, width), f32),
            pltpu.VMEM((sublanes, width), f32),
            pltpu.VMEM((rows, width), bf16),
            pltpu.SemaphoreType.DMA((6,)),
        ],
        compiler_params=roomy,
        cost_estimate=small_cost,
    )(*[far(a) for a in inputs], *made)


def pack_kernel(gather, sent, packed):
    for cut in cuts(sent.shape[1], tile_width):
        packed[:, cut] = lax.dot_general(
            gather[...], sent[:, cut], contract_rows, preferred_element_type=f32
        ).astype(bf16)


def pack(gather, sent):
    return pl.pallas_call(
        pack_kernel,
        in_specs=[near, near],
        out_specs=near,
        out_shape=jax.ShapeDtypeStruct((gather.shape[1], sent.shape[1]), bf16),
        compiler_params=roomy,
        cost_estimate=small_cost,
    )(gather, sent)


def receive_kernel(target, first, scatter, received, addend, more, *rest):
    out_far, more_out, out, done = rest[-4:]
    more_out[0] = more[0]
    rows, width = addend.shape
    place = scatter[...]
    if not first:
        here = (lax.axis_index("section") == target).astype(f32)
        covered = jnp.sum(place.astype(f32), axis=1, keepdims=True) * here > 0.5
    writes = []
    for k, cut in enumerate(cuts(width, tile_width)):
        total = jnp.dot(place, received[:, cut], preferred_element_type=f32) + addend[:, cut]
        if not first:
            total = jnp.where(covered, total, rest[0][:, cut].astype(f32))
        out[:, cut] = total.astype(bf16)
        write = pltpu.make_async_copy(out.at[:, cut], out_far.at[0, :, cut], done.at[k])
        write.start()
        writes.append(write)
    for write in writes:
        write.wait()


def receive(target, scatter, received, addend, more, after, previous=None):
    rows, width = addend.shape
    away = pl.BlockSpec(memory_space=pltpu.HBM)
    others = [far(a) for a in after] if previous is None else [previous]
    return pl.pallas_call(
        functools.partial(receive_kernel, target, previous is None),
        in_specs=[near, near, near, scalar] + [away if previous is None else near] * len(others),
        out_specs=[away, scalar],
        out_shape=[pltpu.HBM((1, rows, width), bf16), pltpu.SMEM(more.shape, more.dtype)],
        scratch_shapes=[pltpu.VMEM((rows, width), bf16), pltpu.SemaphoreType.DMA((width // tile_width,))],
        compiler_params=roomy,
        cost_estimate=small_cost,
    )(scatter, received, addend, more, *others)


def terms_kernel(owned_rows, normed, masked, gain, keep, give, keep_low, give_low, total):
    width = normed.shape[1]
    values = masked[...]
    gain_rows = width // lanes
    for k in range(gain_rows):
        total[k : k + 1, :] = gain[:, k * lanes : (k + 1) * lanes]
    for at in range(0, width, tile_width):
        total[gain_rows + at : gain_rows + at + tile_width, :] = lax.dot_general(
            normed[:, at : at + tile_width], values, contract_rows, preferred_element_type=f32
        )
    even_core = lax.axis_index("dp") % pair == 0
    blocks, cut, _ = keep.shape
    blank = jnp.zeros((cut + keep_low.shape[1] - owned_rows, lanes), f32)
    for j in range(blocks):
        for low, high, mine, other in ((0, cut, keep, give), (cut, owned_rows, keep_low, give_low)):
            even = total[2 * j * owned_rows + low : 2 * j * owned_rows + high, :]
            odd = total[(2 * j + 1) * owned_rows + low : (2 * j + 1) * owned_rows + high, :]
            if low and blank.shape[0]:
                even = jnp.concatenate([even, blank], axis=0)
                odd = jnp.concatenate([odd, blank], axis=0)
            mine[j] = jnp.where(even_core, even, odd)
            other[j] = jnp.where(even_core, odd, even).astype(bf16)


def pair_terms(normed, masked, gain, cut, owned_rows, owners):
    padded = -(-owned_rows // pack_rows) * pack_rows
    high = (owners // pair, cut, lanes)
    low = (owners // pair, padded - cut, lanes)
    return pl.pallas_call(
        functools.partial(terms_kernel, owned_rows),
        in_specs=[near, near, near],
        out_specs=[near] * 4,
        out_shape=[
            jax.ShapeDtypeStruct(high, f32),
            jax.ShapeDtypeStruct(high, bf16),
            jax.ShapeDtypeStruct(low, f32),
            jax.ShapeDtypeStruct(low, bf16),
        ],
        scratch_shapes=[pltpu.VMEM((owners * owned_rows, lanes), f32)],
        compiler_params=roomy,
        cost_estimate=small_cost,
    )(normed, masked, gain)


def merge_kernel(keep, taken, hold, give):
    mine = lax.axis_index("dp") // pair % 2
    for k in range(hold.shape[0]):
        here = 2 * k + mine
        there = 2 * k + 1 - mine
        hold[k] = keep[here] + taken[here].astype(f32)
        give[k] = (keep[there] + taken[there].astype(f32)).astype(bf16)


def merge_terms(keep, taken):
    half = (keep.shape[0] // 2,) + keep.shape[1:]
    return pl.pallas_call(
        merge_kernel,
        in_specs=[near, near],
        out_specs=[near, near],
        out_shape=[jax.ShapeDtypeStruct(half, f32), jax.ShapeDtypeStruct(half, bf16)],
        compiler_params=roomy,
        cost_estimate=small_cost,
    )(keep, taken)


def spread_kernel(keep, taken, hold, *give):
    place = lax.axis_index("dp") // (2 * pair)
    count = keep.shape[0] // 2
    for side in range(2):
        at = 2 * place + side
        hold[side] = keep[at] + taken[at].astype(f32)
        for k in range(1, count):
            at = 2 * lax.rem(place + k, count) + side
            give[k - 1][side] = (keep[at] + taken[at].astype(f32)).astype(bf16)


def spread_terms(keep, taken):
    count = keep.shape[0] // 2
    two = (2,) + keep.shape[1:]
    return pl.pallas_call(
        spread_kernel,
        in_specs=[near, near],
        out_specs=[near] * count,
        out_shape=[jax.ShapeDtypeStruct(two, f32)] + [jax.ShapeDtypeStruct(two, bf16)] * (count - 1),
        compiler_params=roomy,
        cost_estimate=small_cost,
    )(keep, taken)


def split_kernel(hold, taken, own, *parts):
    count = hold.shape[0]
    place = lax.axis_index("dp") // (2 * pair)
    own[...] = hold[place] + taken[place].astype(f32)
    for k in range(1, count):
        at = lax.rem(place + k, count)
        parts[k - 1][...] = (hold[at] + taken[at].astype(f32)).astype(bf16)


def split_terms(hold, taken):
    count = hold.shape[0]
    return pl.pallas_call(
        split_kernel,
        in_specs=[near, near],
        out_specs=[near] * count,
        out_shape=[jax.ShapeDtypeStruct(hold.shape[1:], f32)]
        + [jax.ShapeDtypeStruct(hold.shape[1:], bf16)] * (count - 1),
        compiler_params=roomy,
        cost_estimate=small_cost,
    )(hold, taken)


def cross_kernel(hold, *refs):
    *landed, own, give = refs
    mine = lax.axis_index("dp") // pair % 2
    total = hold[mine]
    passed = hold[1 - mine]
    for part in landed:
        total += part[mine].astype(f32)
        passed += part[1 - mine].astype(f32)
    own[...] = total
    give[...] = passed.astype(bf16)


def cross_terms(hold, landed):
    return pl.pallas_call(
        cross_kernel,
        in_specs=[near] * (1 + len(landed)),
        out_specs=[near, near],
        out_shape=[jax.ShapeDtypeStruct(hold.shape[1:], f32), jax.ShapeDtypeStruct(hold.shape[1:], bf16)],
        compiler_params=roomy,
        cost_estimate=small_cost,
    )(hold, *landed)


def total_kernel(owned_rows, factor, own_low, landed_low, own, *rest):
    out = rest[-1]
    total = own[...]
    for part in rest[:-1]:
        total += part[...].astype(f32)
    low = (own_low[...] + landed_low[...].astype(f32)) * factor
    total = total * factor
    cut = total.shape[0]
    for k in range(owned_rows):
        row = total[k : k + 1, :] if k < cut else low[k - cut : k - cut + 1, :]
        out[:, k * lanes : (k + 1) * lanes] = row


def total_terms(owned_rows, factor, own_low, landed_low, own, landed):
    return pl.pallas_call(
        functools.partial(total_kernel, owned_rows, factor),
        in_specs=[near] * (3 + len(landed)),
        out_specs=near,
        out_shape=jax.ShapeDtypeStruct((1, owned_rows * lanes), f32),
        compiler_params=roomy,
        cost_estimate=small_cost,
    )(own_low, landed_low, own, *landed)


def weight_owned(normed, masked, gain, factor):
    owners = lax.axis_size("dp")
    width = normed.shape[1]
    depth = masked.shape[1]
    owned = (width + width * depth) // owners
    quad = 2 * pair
    if depth != lanes or owned % lanes or owners % quad:
        weight_term = lax.dot_general(normed, masked, contract_rows, preferred_element_type=f32)
        flat = jnp.concatenate([gain.reshape(-1), weight_term.reshape(-1)]) * factor
        return lax.psum_scatter(flat, "dp", scatter_dimension=0, tiled=True)[None, :]
    owned_rows = owned // lanes
    cut = -(-owned_rows * 2 // 3 // pack_rows) * pack_rows
    swap = [(i, i ^ 1) for i in range(owners)]
    near_by = [(i, i ^ pair) for i in range(owners)]
    farther = [[(i, (i + shift) % owners) for i in range(owners)] for shift in range(quad, owners, quad)]
    keep, give, keep_low, give_low = pair_terms(normed, masked, gain, cut, owned_rows, owners)
    taken = lax.ppermute(give, "dp", swap)
    taken_low = lax.ppermute(give_low, "dp", swap)
    hold, give = merge_terms(keep, taken)
    across = lax.ppermute(give, "dp", near_by)
    hold_low, *parts_low = spread_terms(keep_low, taken_low)
    landed_low = [lax.ppermute(part, "dp", hops) for part, hops in zip(parts_low, farther)]
    own, *parts = split_terms(hold, across)
    landed = [lax.ppermute(part, "dp", hops) for part, hops in zip(parts, farther)]
    own_low, cross_low = cross_terms(hold_low, landed_low)
    return total_terms(owned_rows, factor, own_low, lax.ppermute(cross_low, "dp", near_by), own, landed)


def shards(layer_inputs, top_grad, value_grads, weights, norm_gains, counts):
    rows = layer_inputs.shape[1]
    factor = 1.0 / math.sqrt(rows * lax.axis_size("dp"))
    sections = lax.axis_size("section")
    room = -(-rows * 3 // 4 // pack_rows) * pack_rows
    spare = rows - room
    inputs = (counts, layer_inputs, top_grad, value_grads, weights, norm_gains)
    *made, packed = branch_rows(0, room, True, inputs)
    addend, scatter, more, normed, masked, gain = branch_rows(0, room, False, inputs, made)
    owned = weight_owned(normed, masked, gain, factor)
    result = None
    for hop in range(sections - 1):
        target = sections - 2 - hop
        hops = [(target + 1, target)]
        before = result
        if hop:
            packed = pack(scatter, before)
        landed = lax.ppermute(packed, "section", hops)
        updated, more = receive(target, scatter, landed, addend, more, (owned,), before)

        def rest(updated):
            addend, scatter, more, *_, packed = branch_rows(room, spare, None, inputs)
            if hop:
                packed = pack(scatter, before)
            landed = lax.ppermute(packed, "section", hops)
            return receive(target, scatter, landed, addend, more, (), updated[0])[0]

        updated = lax.cond(more.reshape(()) > 0, rest, lambda updated: updated, updated)
        result = updated[0]
    return (result[None], owned)


def solution(mesh):
    placed = (
        P("section", "dp", None),
        P("dp", None),
        P("section", "dp", None),
        P("section", None, None),
        P("section", None),
        P("dp"),
    )
    return jax.shard_map(
        shards,
        mesh=mesh,
        in_specs=placed,
        out_specs=(P("section", "dp", None), P("section", "dp")),
        check_vma=False,
    )
```

```python
import functools
import math

import jax
import jax.numpy as jnp
from jax import lax
from jax.experimental import pallas as pl
from jax.experimental.pallas import tpu as pltpu
from jax.sharding import PartitionSpec as P

eps_norm = 1e-05
lanes = 128
sublanes = 8
pack_rows = 16
tile_width = 512
pair = 2
f32 = jnp.float32
bf16 = jnp.bfloat16
contract_last = (((1,), (1,)), ((), ()))
contract_rows = (((0,), (0,)), ((), ()))
small_cost = pl.CostEstimate(flops=1 << 20, bytes_accessed=1 << 16, transcendentals=0)
roomy = pltpu.CompilerParams(vmem_limit_bytes=32 << 20)
near = pl.BlockSpec(memory_space=pltpu.VMEM)
scalar = pl.BlockSpec(memory_space=pltpu.SMEM)


def far(array):
    return pltpu.with_memory_space_constraint(array, pltpu.HBM)


def cuts(width, step):
    return [pl.ds(at, step) for at in range(0, width, step)]


def one_hot(counts, micro_count, slots, low, size):
    slot = lax.broadcasted_iota(jnp.int32, (slots, size), 0)
    column = lax.broadcasted_iota(jnp.int32, (slots, size), 1) + low
    start = jnp.int32(0)
    pieces = []
    for m in range(micro_count):
        hit = (slot < counts[m]) & (slot + start == column)
        pieces.append(jnp.where(hit, 1.0, 0.0))
        start = start + counts[m]
    return jnp.concatenate(pieces, axis=0).astype(bf16)


def branch_kernel(low, sending, counts_far, x_far, top_far, v_far, w_far, gain_far, *refs):
    work = functools.partial(branch_work, low, sending, counts_far, x_far, top_far, v_far, w_far, gain_far)
    if sending is None:
        work(*refs)
        return
    later = lax.axis_index("section") == 0
    pl.when(jnp.logical_not(later) if sending else later)(lambda: work(*refs[0 if sending else 6 :]))


def branch_work(
    low, sending, counts_far, x_far, top_far, v_far, w_far, gain_far,
    addend, scatter, more, normed, masked, gain_out, *refs
):
    if sending is False:
        packed = None
    else:
        packed, *refs = refs
    counts, x, top, v, w, gain, back, gain_part, sent, ready = refs
    room = scatter.shape[1]
    rows, width = addend.shape
    micro_count = counts.shape[0]
    slots = rows // micro_count
    fetches = [
        pltpu.make_async_copy(v_far.at[0], v, ready.at[0]),
        pltpu.make_async_copy(counts_far, counts, ready.at[1]),
        pltpu.make_async_copy(w_far.at[0], w, ready.at[2]),
        pltpu.make_async_copy(x_far.at[0], x, ready.at[3]),
        pltpu.make_async_copy(gain_far, gain, ready.at[4]),
        pltpu.make_async_copy(top_far, top, ready.at[5]),
    ]
    for fetch in fetches:
        fetch.start()
    fetches[0].wait()
    fetches[1].wait()
    slot = lax.broadcasted_iota(jnp.int32, (slots, v.shape[1]), 0)
    for m in range(micro_count):
        piece = v[m * slots : (m + 1) * slots, :]
        masked[m * slots : (m + 1) * slots, :] = jnp.where(slot < counts[m], piece, jnp.zeros_like(piece))
    live = jnp.int32(0)
    for m in range(micro_count):
        live += counts[m]
    more[0] = (live > low + room).astype(jnp.int32)
    gather = one_hot(counts, micro_count, slots, low, room)
    receives = lax.axis_index("section") < lax.axis_size("section") - 1
    scatter[...] = jnp.where(receives, gather.astype(f32), 0.0).astype(bf16)
    values = masked[...]
    fetches[2].wait()
    for cut in cuts(width, tile_width):
        back[:, cut] = lax.dot_general(values, w[cut, :], contract_last, preferred_element_type=f32)
    fetches[3].wait()
    fetches[4].wait()
    fetches[5].wait()
    for at in range(0, rows, 32):
        part = slice(at, at + 32)
        squares = jnp.zeros((32, lanes), f32)
        products = jnp.zeros((32, lanes), f32)
        for cut in cuts(width, lanes):
            wide = x[part, cut].astype(f32)
            squares += wide * wide
            products += wide * back[part, cut] * gain[:, cut]
        scale = lax.rsqrt(jnp.sum(squares, axis=1, keepdims=True) / width + eps_norm)
        pull = scale * jnp.sum(products, axis=1, keepdims=True) / width
        waits = jnp.concatenate(
            [
                lax.broadcasted_iota(jnp.int32, (slots, 1), 0) < jnp.where(receives, counts[m], 0)
                for m in range(at // slots, (at + 32) // slots)
            ],
            axis=0,
        )
        for cut in cuts(width, 2 * lanes):
            unit = x[part, cut].astype(f32) * scale
            here = back[part, cut]
            scaled = gain[:, cut]
            product = (unit * here).reshape(32 // sublanes, sublanes, 2 * lanes).sum(axis=0)
            if at:
                product += gain_part[:, cut]
            gain_part[:, cut] = product
            normed[part, cut] = (unit * scaled).astype(bf16)
            own = scale * (scaled * here - unit * pull)
            whole = (top[part, cut].astype(f32) + own).astype(bf16)
            sent[part, cut] = whole
            addend[part, cut] = jnp.where(waits, own, whole.astype(f32))
    if packed is not None:
        for cut in cuts(width, tile_width):
            packed[:, cut] = lax.dot_general(
                gather, sent[:, cut], contract_rows, preferred_element_type=f32
            ).astype(bf16)
    for cut in cuts(width, tile_width):
        gain_out[:, cut] = jnp.sum(gain_part[:, cut], axis=0, keepdims=True)


def branch_rows(low, room, sending, inputs, made=()):
    counts, x, top, v, w, gain = inputs
    rows, width = top.shape
    depth = v.shape[2]
    outs = [
        jax.ShapeDtypeStruct((rows, width), f32),
        jax.ShapeDtypeStruct((rows, room), bf16),
        pltpu.SMEM((1,), jnp.int32),
        jax.ShapeDtypeStruct((rows, width), bf16),
        jax.ShapeDtypeStruct((rows, depth), bf16),
        jax.ShapeDtypeStruct((1, width), f32),
    ]
    specs = [near, near, scalar, near, near, near]
    aliases = {}
    if made:
        aliases = {6 + k: k for k in range(len(made))}
    extra = [] if made else [jax.ShapeDtypeStruct((room, width), bf16)]
    return pl.pallas_call(
        functools.partial(branch_kernel, low, sending),
        in_specs=[pl.BlockSpec(memory_space=pltpu.HBM)] * 6 + (specs if made else []),
        out_specs=specs + [near] * len(extra),
        out_shape=outs + extra,
        input_output_aliases=aliases,
        scratch_shapes=[
            pltpu.SMEM(counts.shape, jnp.int32),
            pltpu.VMEM((rows, width), bf16),
            pltpu.VMEM((rows, width), bf16),
            pltpu.VMEM((rows, depth), bf16),
            pltpu.VMEM((width, depth), bf16),
            pltpu.VMEM((1, width), f32),
            pltpu.VMEM((rows, width), f32),
            pltpu.VMEM((sublanes, width), f32),
            pltpu.VMEM((rows, width), bf16),
            pltpu.SemaphoreType.DMA((6,)),
        ],
        compiler_params=roomy,
        cost_estimate=small_cost,
    )(*[far(a) for a in inputs], *made)


def pack_kernel(gather, sent, packed):
    for cut in cuts(sent.shape[1], tile_width):
        packed[:, cut] = lax.dot_general(
            gather[...], sent[:, cut], contract_rows, preferred_element_type=f32
        ).astype(bf16)


def pack(gather, sent):
    return pl.pallas_call(
        pack_kernel,
        in_specs=[near, near],
        out_specs=near,
        out_shape=jax.ShapeDtypeStruct((gather.shape[1], sent.shape[1]), bf16),
        compiler_params=roomy,
        cost_estimate=small_cost,
    )(gather, sent)


def receive_kernel(target, first, scatter, received, addend, more, *rest):
    out_far, more_out, out, done = rest[-4:]
    more_out[0] = more[0]
    rows, width = addend.shape
    place = scatter[...]
    if not first:
        here = (lax.axis_index("section") == target).astype(f32)
        covered = jnp.sum(place.astype(f32), axis=1, keepdims=True) * here > 0.5
    writes = []
    for k, cut in enumerate(cuts(width, tile_width)):
        total = jnp.dot(place, received[:, cut], preferred_element_type=f32) + addend[:, cut]
        if not first:
            total = jnp.where(covered, total, rest[0][:, cut].astype(f32))
        out[:, cut] = total.astype(bf16)
        write = pltpu.make_async_copy(out.at[:, cut], out_far.at[0, :, cut], done.at[k])
        write.start()
        writes.append(write)
    for write in writes:
        write.wait()


def receive(target, scatter, received, addend, more, after, previous=None):
    rows, width = addend.shape
    away = pl.BlockSpec(memory_space=pltpu.HBM)
    others = [far(a) for a in after] if previous is None else [previous]
    return pl.pallas_call(
        functools.partial(receive_kernel, target, previous is None),
        in_specs=[near, near, near, scalar] + [away if previous is None else near] * len(others),
        out_specs=[away, scalar],
        out_shape=[pltpu.HBM((1, rows, width), bf16), pltpu.SMEM(more.shape, more.dtype)],
        scratch_shapes=[pltpu.VMEM((rows, width), bf16), pltpu.SemaphoreType.DMA((width // tile_width,))],
        compiler_params=roomy,
        cost_estimate=small_cost,
    )(scatter, received, addend, more, *others)


def terms_kernel(owned_rows, normed, masked, gain, keep, give, keep_low, give_low, total):
    width = normed.shape[1]
    values = masked[...]
    gain_rows = width // lanes
    for k in range(gain_rows):
        total[k : k + 1, :] = gain[:, k * lanes : (k + 1) * lanes]
    for at in range(0, width, tile_width):
        total[gain_rows + at : gain_rows + at + tile_width, :] = lax.dot_general(
            normed[:, at : at + tile_width], values, contract_rows, preferred_element_type=f32
        )
    even_core = lax.axis_index("dp") % pair == 0
    blocks, cut, _ = keep.shape
    blank = jnp.zeros((cut + keep_low.shape[1] - owned_rows, lanes), f32)
    for j in range(blocks):
        for low, high, mine, other in ((0, cut, keep, give), (cut, owned_rows, keep_low, give_low)):
            even = total[2 * j * owned_rows + low : 2 * j * owned_rows + high, :]
            odd = total[(2 * j + 1) * owned_rows + low : (2 * j + 1) * owned_rows + high, :]
            if low and blank.shape[0]:
                even = jnp.concatenate([even, blank], axis=0)
                odd = jnp.concatenate([odd, blank], axis=0)
            mine[j] = jnp.where(even_core, even, odd)
            other[j] = jnp.where(even_core, odd, even).astype(bf16)


def pair_terms(normed, masked, gain, cut, owned_rows, owners):
    padded = -(-owned_rows // pack_rows) * pack_rows
    high = (owners // pair, cut, lanes)
    low = (owners // pair, padded - cut, lanes)
    return pl.pallas_call(
        functools.partial(terms_kernel, owned_rows),
        in_specs=[near, near, near],
        out_specs=[near] * 4,
        out_shape=[
            jax.ShapeDtypeStruct(high, f32),
            jax.ShapeDtypeStruct(high, bf16),
            jax.ShapeDtypeStruct(low, f32),
            jax.ShapeDtypeStruct(low, bf16),
        ],
        scratch_shapes=[pltpu.VMEM((owners * owned_rows, lanes), f32)],
        compiler_params=roomy,
        cost_estimate=small_cost,
    )(normed, masked, gain)


def merge_kernel(keep, taken, hold, give):
    mine = lax.axis_index("dp") // pair % 2
    for k in range(hold.shape[0]):
        here = 2 * k + mine
        there = 2 * k + 1 - mine
        hold[k] = keep[here] + taken[here].astype(f32)
        give[k] = (keep[there] + taken[there].astype(f32)).astype(bf16)


def merge_terms(keep, taken):
    half = (keep.shape[0] // 2,) + keep.shape[1:]
    return pl.pallas_call(
        merge_kernel,
        in_specs=[near, near],
        out_specs=[near, near],
        out_shape=[jax.ShapeDtypeStruct(half, f32), jax.ShapeDtypeStruct(half, bf16)],
        compiler_params=roomy,
        cost_estimate=small_cost,
    )(keep, taken)


def add_kernel(keep, taken, out):
    for k in range(keep.shape[0]):
        out[k] = (keep[k] + taken[k].astype(f32)).astype(bf16)


def add_terms(keep, taken):
    return pl.pallas_call(
        add_kernel,
        in_specs=[near, near],
        out_specs=near,
        out_shape=jax.ShapeDtypeStruct(keep.shape, bf16),
        compiler_params=roomy,
        cost_estimate=small_cost,
    )(keep, taken)


def cross_kernel(landed, own, give):
    mine = lax.axis_index("dp") // pair % 2
    total = landed[mine].astype(f32)
    passed = landed[1 - mine].astype(f32)
    for k in range(2, landed.shape[0], 2):
        total += landed[k + mine].astype(f32)
        passed += landed[k + 1 - mine].astype(f32)
    own[...] = total
    give[...] = passed.astype(bf16)


def cross_terms(landed):
    return pl.pallas_call(
        cross_kernel,
        in_specs=[near],
        out_specs=[near, near],
        out_shape=[jax.ShapeDtypeStruct(landed.shape[1:], f32), jax.ShapeDtypeStruct(landed.shape[1:], bf16)],
        compiler_params=roomy,
        cost_estimate=small_cost,
    )(landed)


def total_kernel(owned_rows, factor, own_low, landed_low, landed, out):
    total = landed[0].astype(f32)
    for k in range(1, landed.shape[0]):
        total += landed[k].astype(f32)
    low = (own_low[...] + landed_low[...].astype(f32)) * factor
    total = total * factor
    cut = total.shape[0]
    for k in range(owned_rows):
        row = total[k : k + 1, :] if k < cut else low[k - cut : k - cut + 1, :]
        out[:, k * lanes : (k + 1) * lanes] = row


def total_terms(owned_rows, factor, own_low, landed_low, landed):
    return pl.pallas_call(
        functools.partial(total_kernel, owned_rows, factor),
        in_specs=[near] * 3,
        out_specs=near,
        out_shape=jax.ShapeDtypeStruct((1, owned_rows * lanes), f32),
        compiler_params=roomy,
        cost_estimate=small_cost,
    )(own_low, landed_low, landed)


def weight_owned(normed, masked, gain, factor):
    owners = lax.axis_size("dp")
    width = normed.shape[1]
    depth = masked.shape[1]
    owned = (width + width * depth) // owners
    quad = 2 * pair
    if depth != lanes or owned % lanes or owners % quad:
        weight_term = lax.dot_general(normed, masked, contract_rows, preferred_element_type=f32)
        flat = jnp.concatenate([gain.reshape(-1), weight_term.reshape(-1)]) * factor
        return lax.psum_scatter(flat, "dp", scatter_dimension=0, tiled=True)[None, :]
    owned_rows = owned // lanes
    cut = -(-owned_rows * 2 // 3 // pack_rows) * pack_rows
    swap = [(i, i ^ 1) for i in range(owners)]
    near_by = [(i, i ^ pair) for i in range(owners)]
    lines = [list(range(first, owners, quad)) for first in range(quad)]
    exchange = functools.partial(lax.all_to_all, axis_name="dp", split_axis=0, concat_axis=0, axis_index_groups=lines, tiled=True)
    keep, give, keep_low, give_low = pair_terms(normed, masked, gain, cut, owned_rows, owners)
    taken = lax.ppermute(give, "dp", swap)
    taken_low = lax.ppermute(give_low, "dp", swap)
    hold, give = merge_terms(keep, taken)
    across = lax.ppermute(give, "dp", near_by)
    landed_low = exchange(add_terms(keep_low, taken_low))
    landed = exchange(add_terms(hold, across))
    own_low, cross_low = cross_terms(landed_low)
    return total_terms(owned_rows, factor, own_low, lax.ppermute(cross_low, "dp", near_by), landed)


def shards(layer_inputs, top_grad, value_grads, weights, norm_gains, counts):
    rows = layer_inputs.shape[1]
    factor = 1.0 / math.sqrt(rows * lax.axis_size("dp"))
    sections = lax.axis_size("section")
    room = -(-rows * 3 // 4 // pack_rows) * pack_rows
    spare = rows - room
    inputs = (counts, layer_inputs, top_grad, value_grads, weights, norm_gains)
    *made, packed = branch_rows(0, room, True, inputs)
    addend, scatter, more, normed, masked, gain = branch_rows(0, room, False, inputs, made)
    owned = weight_owned(normed, masked, gain, factor)
    result = None
    for hop in range(sections - 1):
        target = sections - 2 - hop
        hops = [(target + 1, target)]
        before = result
        if hop:
            packed = pack(scatter, before)
        landed = lax.ppermute(packed, "section", hops)
        updated, more = receive(target, scatter, landed, addend, more, (owned,), before)

        def rest(updated):
            addend, scatter, more, *_, packed = branch_rows(room, spare, None, inputs)
            if hop:
                packed = pack(scatter, before)
            landed = lax.ppermute(packed, "section", hops)
            return receive(target, scatter, landed, addend, more, (), updated[0])[0]

        updated = lax.cond(more.reshape(()) > 0, rest, lambda updated: updated, updated)
        result = updated[0]
    return (result[None], owned)


def solution(mesh):
    placed = (
        P("section", "dp", None),
        P("dp", None),
        P("section", "dp", None),
        P("section", None, None),
        P("section", None),
        P("dp"),
    )
    return jax.shard_map(
        shards,
        mesh=mesh,
        in_specs=placed,
        out_specs=(P("section", "dp", None), P("section", "dp")),
        check_vma=False,
    )
```

```python
import functools
import math

import jax
import jax.numpy as jnp
from jax import lax
from jax.experimental import pallas as pl
from jax.experimental.pallas import tpu as pltpu
from jax.sharding import PartitionSpec as P

eps_norm = 1e-05
lanes = 128
sublanes = 8
pack_rows = 16
tile_width = 512
pair = 2
f32 = jnp.float32
bf16 = jnp.bfloat16
contract_last = (((1,), (1,)), ((), ()))
contract_rows = (((0,), (0,)), ((), ()))
small_cost = pl.CostEstimate(flops=1 << 20, bytes_accessed=1 << 16, transcendentals=0)
roomy = pltpu.CompilerParams(vmem_limit_bytes=32 << 20)
near = pl.BlockSpec(memory_space=pltpu.VMEM)
scalar = pl.BlockSpec(memory_space=pltpu.SMEM)


def far(array):
    return pltpu.with_memory_space_constraint(array, pltpu.HBM)


def cuts(width, step):
    return [pl.ds(at, step) for at in range(0, width, step)]


def one_hot(counts, micro_count, slots, low, size):
    slot = lax.broadcasted_iota(jnp.int32, (slots, size), 0)
    column = lax.broadcasted_iota(jnp.int32, (slots, size), 1) + low
    start = jnp.int32(0)
    pieces = []
    for m in range(micro_count):
        hit = (slot < counts[m]) & (slot + start == column)
        pieces.append(jnp.where(hit, 1.0, 0.0))
        start = start + counts[m]
    return jnp.concatenate(pieces, axis=0).astype(bf16)


def branch_kernel(
    low, counts_far, x_far, top_far, v_far, w_far, gain_far,
    packed, addend, scatter, more, normed, masked, gain_out,
    counts, x, top, v, w, gain, back, gain_part, sent, ready,
):
    rows, width = addend.shape
    micro_count = counts.shape[0]
    slots = rows // micro_count
    fetches = [
        pltpu.make_async_copy(v_far.at[0], v, ready.at[0]),
        pltpu.make_async_copy(counts_far, counts, ready.at[1]),
        pltpu.make_async_copy(w_far.at[0], w, ready.at[2]),
        pltpu.make_async_copy(x_far.at[0], x, ready.at[3]),
        pltpu.make_async_copy(gain_far, gain, ready.at[4]),
        pltpu.make_async_copy(top_far, top, ready.at[5]),
    ]
    for fetch in fetches:
        fetch.start()
    fetches[0].wait()
    fetches[1].wait()
    slot = lax.broadcasted_iota(jnp.int32, (slots, v.shape[1]), 0)
    for m in range(micro_count):
        piece = v[m * slots : (m + 1) * slots, :]
        masked[m * slots : (m + 1) * slots, :] = jnp.where(slot < counts[m], piece, jnp.zeros_like(piece))
    live = jnp.int32(0)
    for m in range(micro_count):
        live += counts[m]
    more[0] = (live > low + packed.shape[0]).astype(jnp.int32)
    gather = one_hot(counts, micro_count, slots, low, packed.shape[0])
    receives = lax.axis_index("section") < lax.axis_size("section") - 1
    scatter[...] = jnp.where(receives, gather.astype(f32), 0.0).astype(bf16)
    values = masked[...]
    fetches[2].wait()
    for cut in cuts(width, tile_width):
        back[:, cut] = lax.dot_general(values, w[cut, :], contract_last, preferred_element_type=f32)
    fetches[3].wait()
    fetches[4].wait()
    fetches[5].wait()
    for at in range(0, rows, 32):
        part = slice(at, at + 32)
        squares = jnp.zeros((32, lanes), f32)
        products = jnp.zeros((32, lanes), f32)
        for cut in cuts(width, lanes):
            wide = x[part, cut].astype(f32)
            squares += wide * wide
            products += wide * back[part, cut] * gain[:, cut]
        scale = lax.rsqrt(jnp.sum(squares, axis=1, keepdims=True) / width + eps_norm)
        pull = scale * jnp.sum(products, axis=1, keepdims=True) / width
        waits = jnp.concatenate(
            [
                lax.broadcasted_iota(jnp.int32, (slots, 1), 0) < jnp.where(receives, counts[m], 0)
                for m in range(at // slots, (at + 32) // slots)
            ],
            axis=0,
        )
        for cut in cuts(width, 2 * lanes):
            unit = x[part, cut].astype(f32) * scale
            here = back[part, cut]
            scaled = gain[:, cut]
            product = (unit * here).reshape(32 // sublanes, sublanes, 2 * lanes).sum(axis=0)
            if at:
                product += gain_part[:, cut]
            gain_part[:, cut] = product
            normed[part, cut] = (unit * scaled).astype(bf16)
            own = scale * (scaled * here - unit * pull)
            whole = (top[part, cut].astype(f32) + own).astype(bf16)
            sent[part, cut] = whole
            addend[part, cut] = jnp.where(waits, own, whole.astype(f32))
    for cut in cuts(width, tile_width):
        packed[:, cut] = lax.dot_general(
            gather, sent[:, cut], contract_rows, preferred_element_type=f32
        ).astype(bf16)
    for cut in cuts(width, tile_width):
        gain_out[:, cut] = jnp.sum(gain_part[:, cut], axis=0, keepdims=True)


def branch_rows(low, room, counts, x, top, v, w, gain):
    rows, width = top.shape
    depth = v.shape[2]
    return pl.pallas_call(
        functools.partial(branch_kernel, low),
        in_specs=[pl.BlockSpec(memory_space=pltpu.HBM)] * 6,
        out_specs=[near] * 3 + [scalar] + [near] * 3,
        out_shape=[
            jax.ShapeDtypeStruct((room, width), bf16),
            jax.ShapeDtypeStruct((rows, width), f32),
            jax.ShapeDtypeStruct((rows, room), bf16),
            pltpu.SMEM((1,), jnp.int32),
            jax.ShapeDtypeStruct((rows, width), bf16),
            jax.ShapeDtypeStruct((rows, depth), bf16),
            jax.ShapeDtypeStruct((1, width), f32),
        ],
        scratch_shapes=[
            pltpu.SMEM(counts.shape, jnp.int32),
            pltpu.VMEM((rows, width), bf16),
            pltpu.VMEM((rows, width), bf16),
            pltpu.VMEM((rows, depth), bf16),
            pltpu.VMEM((width, depth), bf16),
            pltpu.VMEM((1, width), f32),
            pltpu.VMEM((rows, width), f32),
            pltpu.VMEM((sublanes, width), f32),
            pltpu.VMEM((rows, width), bf16),
            pltpu.SemaphoreType.DMA((6,)),
        ],
        compiler_params=roomy,
        cost_estimate=small_cost,
    )(*[far(a) for a in (counts, x, top, v, w, gain)])


def pack_kernel(gather, sent, packed):
    for cut in cuts(sent.shape[1], tile_width):
        packed[:, cut] = lax.dot_general(
            gather[...], sent[:, cut], contract_rows, preferred_element_type=f32
        ).astype(bf16)


def pack(gather, sent):
    return pl.pallas_call(
        pack_kernel,
        in_specs=[near, near],
        out_specs=near,
        out_shape=jax.ShapeDtypeStruct((gather.shape[1], sent.shape[1]), bf16),
        compiler_params=roomy,
        cost_estimate=small_cost,
    )(gather, sent)


def receive_kernel(target, first, factor, scatter, received, addend, more, *refs):
    rows, width = addend.shape
    if first:
        *parts, out_far, more_out, owned_far, out, owned, done = refs
    else:
        previous, out_far, more_out, out, done = refs
    more_out[0] = more[0]
    place = scatter[...]
    writes = []
    if first and parts:
        total_rows(factor, owned, *parts)
        writes.append(pltpu.make_async_copy(owned, owned_far, done.at[width // tile_width]))
        writes[0].start()
    if not first:
        here = (lax.axis_index("section") == target).astype(f32)
        covered = jnp.sum(place.astype(f32), axis=1, keepdims=True) * here > 0.5
    for k, cut in enumerate(cuts(width, tile_width)):
        total = jnp.dot(place, received[:, cut], preferred_element_type=f32) + addend[:, cut]
        if not first:
            total = jnp.where(covered, total, previous[:, cut].astype(f32))
        out[:, cut] = total.astype(bf16)
        write = pltpu.make_async_copy(out.at[:, cut], out_far.at[0, :, cut], done.at[k])
        write.start()
        writes.append(write)
    for write in writes:
        write.wait()


def receive(target, scatter, received, addend, more, previous=None, parts=(), owned=lanes, factor=1.0):
    rows, width = addend.shape
    away = pl.BlockSpec(memory_space=pltpu.HBM)
    first = previous is None
    others = parts if first else [previous]
    outs = [pltpu.HBM((1, rows, width), bf16), pltpu.SMEM(more.shape, more.dtype)]
    scratch = [pltpu.VMEM((rows, width), bf16)]
    if first:
        outs.append(pltpu.HBM((1, owned), f32))
        scratch.append(pltpu.VMEM((1, owned), f32))
    return pl.pallas_call(
        functools.partial(receive_kernel, target, first, factor),
        in_specs=[near, near, near, scalar] + [near] * len(others),
        out_specs=[away, scalar] + [away] * first,
        out_shape=outs,
        scratch_shapes=scratch + [pltpu.SemaphoreType.DMA((width // tile_width + 1,))],
        compiler_params=roomy,
        cost_estimate=small_cost,
    )(scatter, received, addend, more, *others)


def terms_kernel(owned_rows, normed, masked, gain, keep, give, total):
    width = normed.shape[1]
    values = masked[...]
    gain_rows = width // lanes
    for k in range(gain_rows):
        total[k : k + 1, :] = gain[:, k * lanes : (k + 1) * lanes]
    for at in range(0, width, tile_width):
        total[gain_rows + at : gain_rows + at + tile_width, :] = lax.dot_general(
            normed[:, at : at + tile_width], values, contract_rows, preferred_element_type=f32
        )
    even_core = lax.axis_index("dp") % pair == 0
    padded = keep.shape[1]
    for j in range(keep.shape[0]):
        even = total[2 * j * owned_rows : (2 * j + 1) * owned_rows, :]
        odd = total[(2 * j + 1) * owned_rows : (2 * j + 2) * owned_rows, :]
        if padded > owned_rows:
            blank = jnp.zeros((padded - owned_rows, lanes), f32)
            even = jnp.concatenate([even, blank], axis=0)
            odd = jnp.concatenate([odd, blank], axis=0)
        keep[j] = jnp.where(even_core, even, odd)
        give[j] = jnp.where(even_core, odd, even)


def pair_terms(normed, masked, gain, owned_rows, owners):
    padded = -(-owned_rows // pack_rows) * pack_rows
    half = jax.ShapeDtypeStruct((owners // pair, padded, lanes), f32)
    return pl.pallas_call(
        functools.partial(terms_kernel, owned_rows),
        in_specs=[near, near, near],
        out_specs=[near, near],
        out_shape=[half, half],
        scratch_shapes=[pltpu.VMEM((owners * owned_rows, lanes), f32)],
        compiler_params=roomy,
        cost_estimate=small_cost,
    )(normed, masked, gain)


def merge_kernel(keep, taken, hold, give, hold_low, *give_low):
    cut = hold.shape[1]
    chip = lax.axis_index("dp") // pair
    mine, place = chip % 2, chip // 2
    count = hold.shape[0]
    for k in range(count):
        here = 2 * k + mine
        there = 2 * k + 1 - mine
        hold[k] = keep[here, :cut, :] + taken[here, :cut, :].astype(f32)
        give[k] = (keep[there, :cut, :] + taken[there, :cut, :].astype(f32)).astype(bf16)
    for side in range(2):
        at = 2 * place + side
        hold_low[side] = keep[at, cut:, :] + taken[at, cut:, :].astype(f32)
        for k in range(1, count):
            at = 2 * lax.rem(place + k, count) + side
            give_low[k - 1][side] = (keep[at, cut:, :] + taken[at, cut:, :].astype(f32)).astype(bf16)


def merge_terms(cut, keep, taken):
    blocks, padded, _ = keep.shape
    count = blocks // 2
    high = (count, cut, lanes)
    low = (2, padded - cut, lanes)
    return pl.pallas_call(
        merge_kernel,
        in_specs=[near, near],
        out_specs=[near] * (2 + count),
        out_shape=[
            jax.ShapeDtypeStruct(high, f32),
            jax.ShapeDtypeStruct(high, bf16),
            jax.ShapeDtypeStruct(low, f32),
        ]
        + [jax.ShapeDtypeStruct(low, bf16)] * (count - 1),
        compiler_params=roomy,
        cost_estimate=small_cost,
    )(keep, taken)


def split_kernel(hold, taken, own, *parts):
    count = hold.shape[0]
    place = lax.axis_index("dp") // (2 * pair)
    own[...] = hold[place] + taken[place].astype(f32)
    for k in range(1, count):
        at = lax.rem(place + k, count)
        parts[k - 1][...] = (hold[at] + taken[at].astype(f32)).astype(bf16)


def split_terms(hold, taken):
    count = hold.shape[0]
    return pl.pallas_call(
        split_kernel,
        in_specs=[near, near],
        out_specs=[near] * count,
        out_shape=[jax.ShapeDtypeStruct(hold.shape[1:], f32)]
        + [jax.ShapeDtypeStruct(hold.shape[1:], bf16)] * (count - 1),
        compiler_params=roomy,
        cost_estimate=small_cost,
    )(hold, taken)


def cross_kernel(hold, *refs):
    *landed, own, give = refs
    mine = lax.axis_index("dp") // pair % 2
    total = hold[mine]
    passed = hold[1 - mine]
    for part in landed:
        total += part[mine].astype(f32)
        passed += part[1 - mine].astype(f32)
    own[...] = total
    give[...] = passed.astype(bf16)


def cross_terms(hold, landed):
    return pl.pallas_call(
        cross_kernel,
        in_specs=[near] * (1 + len(landed)),
        out_specs=[near, near],
        out_shape=[jax.ShapeDtypeStruct(hold.shape[1:], f32), jax.ShapeDtypeStruct(hold.shape[1:], bf16)],
        compiler_params=roomy,
        cost_estimate=small_cost,
    )(hold, *landed)


def total_rows(factor, out, own_low, landed_low, own, *landed):
    total = own[...]
    for part in landed:
        total += part[...].astype(f32)
    low = (own_low[...] + landed_low[...].astype(f32)) * factor
    total = total * factor
    cut = total.shape[0]
    for k in range(out.shape[1] // lanes):
        row = total[k : k + 1, :] if k < cut else low[k - cut : k - cut + 1, :]
        out[:, k * lanes : (k + 1) * lanes] = row


def plane_parts(owners, owned_rows, keep, taken):
    quad = 2 * pair
    shifts = range(quad, owners, quad)
    near_by = [(i, i ^ pair) for i in range(owners)]
    farther = [[(i, (i + shift) % owners) for i in range(owners)] for shift in shifts]
    cut = -(-owned_rows * 2 // 3 // pack_rows) * pack_rows
    hold, give, hold_low, *give_low = merge_terms(cut, keep, taken)
    across = lax.ppermute(give, "dp", near_by)
    landed_low = [lax.ppermute(part, "dp", hops) for part, hops in zip(give_low, farther)]
    own, *parts = split_terms(hold, across)
    landed = [lax.ppermute(part, "dp", hops) for part, hops in zip(parts, farther)]
    own_low, cross_low = cross_terms(hold_low, landed_low)
    return own_low, lax.ppermute(cross_low, "dp", near_by), own, *landed


def weight_owned(normed, masked, gain, factor):
    owners = lax.axis_size("dp")
    width = normed.shape[1]
    depth = masked.shape[1]
    owned = (width + width * depth) // owners
    if depth != lanes or owned % lanes or owners % (2 * pair):
        weight_term = lax.dot_general(normed, masked, contract_rows, preferred_element_type=f32)
        flat = jnp.concatenate([gain.reshape(-1), weight_term.reshape(-1)]) * factor
        return (), owned, lax.psum_scatter(flat, "dp", scatter_dimension=0, tiled=True)[None, :]
    keep, give = pair_terms(normed, masked, gain, owned // lanes, owners)
    taken = lax.ppermute(give, "dp", [(i, i ^ 1) for i in range(owners)])
    return plane_parts(owners, owned // lanes, keep, taken), owned, None


def shards(layer_inputs, top_grad, value_grads, weights, norm_gains, counts):
    rows = layer_inputs.shape[1]
    factor = 1.0 / math.sqrt(rows * lax.axis_size("dp"))
    sections = lax.axis_size("section")
    room = -(-rows * 3 // 4 // pack_rows) * pack_rows
    spare = rows - room
    inputs = (counts, layer_inputs, top_grad, value_grads, weights, norm_gains)
    packed, addend, scatter, more, normed, masked, gain = branch_rows(0, room, *inputs)
    parts, owned_size, owned = weight_owned(normed, masked, gain, factor)
    result = None
    for hop in range(sections - 1):
        target = sections - 2 - hop
        hops = [(target + 1, target), (target, target + 1)]
        before = result
        if hop:
            packed = pack(scatter, before)
        landed = lax.ppermute(packed, "section", hops)
        if hop:
            updated, more = receive(target, scatter, landed, addend, more, before)
        else:
            updated, more, summed = receive(target, scatter, landed, addend, more, None, parts, owned_size, factor)

        def rest(updated):
            packed, addend, scatter, more, *_ = branch_rows(room, spare, *inputs)
            if hop:
                packed = pack(scatter, before)
            landed = lax.ppermute(packed, "section", hops)
            return receive(target, scatter, landed, addend, more, updated[0])[0]

        updated = lax.cond(more.reshape(()) > 0, rest, lambda updated: updated, updated)
        result = updated[0]
    return (result[None], summed if owned is None else owned)


def solution(mesh):
    placed = (
        P("section", "dp", None),
        P("dp", None),
        P("section", "dp", None),
        P("section", None, None),
        P("section", None),
        P("dp"),
    )
    return jax.shard_map(
        shards,
        mesh=mesh,
        in_specs=placed,
        out_specs=(P("section", "dp", None), P("section", "dp")),
        check_vma=False,
    )
```

```python
import functools
import math

import jax
import jax.numpy as jnp
from jax import lax
from jax.experimental import pallas as pl
from jax.experimental.pallas import tpu as pltpu
from jax.sharding import PartitionSpec as P

eps_norm = 1e-05
lanes = 128
sublanes = 8
pack_rows = 16
tile_width = 512
pair = 2
f32 = jnp.float32
bf16 = jnp.bfloat16
contract_last = (((1,), (1,)), ((), ()))
contract_rows = (((0,), (0,)), ((), ()))
small_cost = pl.CostEstimate(flops=1 << 20, bytes_accessed=1 << 16, transcendentals=0)
roomy = pltpu.CompilerParams(vmem_limit_bytes=32 << 20)
near = pl.BlockSpec(memory_space=pltpu.VMEM)
scalar = pl.BlockSpec(memory_space=pltpu.SMEM)


def far(array):
    return pltpu.with_memory_space_constraint(array, pltpu.HBM)


def cuts(width, step):
    return [pl.ds(at, step) for at in range(0, width, step)]


def one_hot(counts, micro_count, slots, low, size):
    slot = lax.broadcasted_iota(jnp.int32, (slots, size), 0)
    column = lax.broadcasted_iota(jnp.int32, (slots, size), 1) + low
    start = jnp.int32(0)
    pieces = []
    for m in range(micro_count):
        hit = (slot < counts[m]) & (slot + start == column)
        pieces.append(jnp.where(hit, 1.0, 0.0))
        start = start + counts[m]
    return jnp.concatenate(pieces, axis=0).astype(bf16)


def branch_kernel(
    low, counts_far, x_far, top_far, v_far, w_far, gain_far,
    packed, addend, scatter, more, normed, masked, gain_out,
    counts, x, top, v, w, gain, back, gain_part, sent, ready,
):
    rows, width = addend.shape
    micro_count = counts.shape[0]
    slots = rows // micro_count
    fetches = [
        pltpu.make_async_copy(v_far.at[0], v, ready.at[0]),
        pltpu.make_async_copy(counts_far, counts, ready.at[1]),
        pltpu.make_async_copy(w_far.at[0], w, ready.at[2]),
        pltpu.make_async_copy(x_far.at[0], x, ready.at[3]),
        pltpu.make_async_copy(gain_far, gain, ready.at[4]),
        pltpu.make_async_copy(top_far, top, ready.at[5]),
    ]
    for fetch in fetches:
        fetch.start()
    fetches[0].wait()
    fetches[1].wait()
    slot = lax.broadcasted_iota(jnp.int32, (slots, v.shape[1]), 0)
    for m in range(micro_count):
        piece = v[m * slots : (m + 1) * slots, :]
        masked[m * slots : (m + 1) * slots, :] = jnp.where(slot < counts[m], piece, jnp.zeros_like(piece))
    live = jnp.int32(0)
    for m in range(micro_count):
        live += counts[m]
    more[0] = (live > low + packed.shape[0]).astype(jnp.int32)
    gather = one_hot(counts, micro_count, slots, low, packed.shape[0])
    receives = lax.axis_index("section") < lax.axis_size("section") - 1
    scatter[...] = jnp.where(receives, gather.astype(f32), 0.0).astype(bf16)
    values = masked[...]
    fetches[2].wait()
    for cut in cuts(width, tile_width):
        back[:, cut] = lax.dot_general(values, w[cut, :], contract_last, preferred_element_type=f32)
    fetches[3].wait()
    fetches[4].wait()
    fetches[5].wait()
    for at in range(0, rows, 32):
        part = slice(at, at + 32)
        squares = jnp.zeros((32, lanes), f32)
        products = jnp.zeros((32, lanes), f32)
        for cut in cuts(width, lanes):
            wide = x[part, cut].astype(f32)
            squares += wide * wide
            products += wide * back[part, cut] * gain[:, cut]
        scale = lax.rsqrt(jnp.sum(squares, axis=1, keepdims=True) / width + eps_norm)
        pull = scale * jnp.sum(products, axis=1, keepdims=True) / width
        waits = jnp.concatenate(
            [
                lax.broadcasted_iota(jnp.int32, (slots, 1), 0) < jnp.where(receives, counts[m], 0)
                for m in range(at // slots, (at + 32) // slots)
            ],
            axis=0,
        )
        for cut in cuts(width, 2 * lanes):
            unit = x[part, cut].astype(f32) * scale
            here = back[part, cut]
            scaled = gain[:, cut]
            product = (unit * here).reshape(32 // sublanes, sublanes, 2 * lanes).sum(axis=0)
            if at:
                product += gain_part[:, cut]
            gain_part[:, cut] = product
            normed[part, cut] = (unit * scaled).astype(bf16)
            own = scale * (scaled * here - unit * pull)
            whole = (top[part, cut].astype(f32) + own).astype(bf16)
            sent[part, cut] = whole
            addend[part, cut] = jnp.where(waits, own, whole.astype(f32))
    for cut in cuts(width, tile_width):
        packed[:, cut] = lax.dot_general(
            gather, sent[:, cut], contract_rows, preferred_element_type=f32
        ).astype(bf16)
    for cut in cuts(width, tile_width):
        gain_out[:, cut] = jnp.sum(gain_part[:, cut], axis=0, keepdims=True)


def branch_rows(low, room, counts, x, top, v, w, gain):
    rows, width = top.shape
    depth = v.shape[2]
    return pl.pallas_call(
        functools.partial(branch_kernel, low),
        in_specs=[pl.BlockSpec(memory_space=pltpu.HBM)] * 6,
        out_specs=[near] * 3 + [scalar] + [near] * 3,
        out_shape=[
            jax.ShapeDtypeStruct((room, width), bf16),
            jax.ShapeDtypeStruct((rows, width), f32),
            jax.ShapeDtypeStruct((rows, room), bf16),
            pltpu.SMEM((1,), jnp.int32),
            jax.ShapeDtypeStruct((rows, width), bf16),
            jax.ShapeDtypeStruct((rows, depth), bf16),
            jax.ShapeDtypeStruct((1, width), f32),
        ],
        scratch_shapes=[
            pltpu.SMEM(counts.shape, jnp.int32),
            pltpu.VMEM((rows, width), bf16),
            pltpu.VMEM((rows, width), bf16),
            pltpu.VMEM((rows, depth), bf16),
            pltpu.VMEM((width, depth), bf16),
            pltpu.VMEM((1, width), f32),
            pltpu.VMEM((rows, width), f32),
            pltpu.VMEM((sublanes, width), f32),
            pltpu.VMEM((rows, width), bf16),
            pltpu.SemaphoreType.DMA((6,)),
        ],
        compiler_params=roomy,
        cost_estimate=small_cost,
    )(*[far(a) for a in (counts, x, top, v, w, gain)])


def pack_kernel(gather, sent, packed):
    for cut in cuts(sent.shape[1], tile_width):
        packed[:, cut] = lax.dot_general(
            gather[...], sent[:, cut], contract_rows, preferred_element_type=f32
        ).astype(bf16)


def pack(gather, sent):
    return pl.pallas_call(
        pack_kernel,
        in_specs=[near, near],
        out_specs=near,
        out_shape=jax.ShapeDtypeStruct((gather.shape[1], sent.shape[1]), bf16),
        compiler_params=roomy,
        cost_estimate=small_cost,
    )(gather, sent)


def receive_kernel(target, first, factor, scatter, received, addend, more, *refs):
    rows, width = addend.shape
    if first:
        *parts, out_far, more_out, owned_far, out, owned, done = refs
    else:
        previous, out_far, more_out, out, done = refs
    more_out[0] = more[0]
    place = scatter[...]
    writes = []
    if first and parts:
        total_rows(factor, owned, *parts)
        writes.append(pltpu.make_async_copy(owned, owned_far, done.at[width // tile_width]))
        writes[0].start()
    if not first:
        here = (lax.axis_index("section") == target).astype(f32)
        covered = jnp.sum(place.astype(f32), axis=1, keepdims=True) * here > 0.5
    for k, cut in enumerate(cuts(width, tile_width)):
        total = jnp.dot(place, received[:, cut], preferred_element_type=f32) + addend[:, cut]
        if not first:
            total = jnp.where(covered, total, previous[:, cut].astype(f32))
        out[:, cut] = total.astype(bf16)
        write = pltpu.make_async_copy(out.at[:, cut], out_far.at[0, :, cut], done.at[k])
        write.start()
        writes.append(write)
    for write in writes:
        write.wait()


def receive(target, scatter, received, addend, more, previous=None, parts=(), owned=lanes, factor=1.0):
    rows, width = addend.shape
    away = pl.BlockSpec(memory_space=pltpu.HBM)
    first = previous is None
    others = parts if first else [previous]
    outs = [pltpu.HBM((1, rows, width), bf16), pltpu.SMEM(more.shape, more.dtype)]
    scratch = [pltpu.VMEM((rows, width), bf16)]
    if first:
        outs.append(pltpu.HBM((1, owned), f32))
        scratch.append(pltpu.VMEM((1, owned), f32))
    return pl.pallas_call(
        functools.partial(receive_kernel, target, first, factor),
        in_specs=[near, near, near, scalar] + [near] * len(others),
        out_specs=[away, scalar] + [away] * first,
        out_shape=outs,
        scratch_shapes=scratch + [pltpu.SemaphoreType.DMA((width // tile_width + 1,))],
        compiler_params=roomy,
        cost_estimate=small_cost,
    )(scatter, received, addend, more, *others)


def terms_kernel(owned_rows, normed, masked, gain, keep, give, total):
    width = normed.shape[1]
    values = masked[...]
    gain_rows = width // lanes
    for k in range(gain_rows):
        total[k : k + 1, :] = gain[:, k * lanes : (k + 1) * lanes]
    for at in range(0, width, tile_width):
        total[gain_rows + at : gain_rows + at + tile_width, :] = lax.dot_general(
            normed[:, at : at + tile_width], values, contract_rows, preferred_element_type=f32
        )
    even_core = lax.axis_index("dp") % pair == 0
    padded = keep.shape[1]
    for j in range(keep.shape[0]):
        even = total[2 * j * owned_rows : (2 * j + 1) * owned_rows, :]
        odd = total[(2 * j + 1) * owned_rows : (2 * j + 2) * owned_rows, :]
        if padded > owned_rows:
            blank = jnp.zeros((padded - owned_rows, lanes), f32)
            even = jnp.concatenate([even, blank], axis=0)
            odd = jnp.concatenate([odd, blank], axis=0)
        keep[j] = jnp.where(even_core, even, odd)
        give[j] = jnp.where(even_core, odd, even).astype(bf16)


def pair_terms(normed, masked, gain, owned_rows, owners):
    padded = -(-owned_rows // pack_rows) * pack_rows
    half = jax.ShapeDtypeStruct((owners // pair, padded, lanes), f32)
    return pl.pallas_call(
        functools.partial(terms_kernel, owned_rows),
        in_specs=[near, near, near],
        out_specs=[near, near],
        out_shape=[half, jax.ShapeDtypeStruct(half.shape, bf16)],
        scratch_shapes=[pltpu.VMEM((owners * owned_rows, lanes), f32)],
        compiler_params=roomy,
        cost_estimate=small_cost,
    )(normed, masked, gain)


def merge_kernel(keep, taken, hold, *give):
    spot = lax.axis_index("dp")
    even = spot % pair == 0
    chip = spot // pair
    mine, place = chip % 2, chip // 2
    count = hold.shape[0]

    def block(across, along):
        at = jnp.where(even, across, along)
        return keep[at] + taken[at].astype(f32)

    for k in range(count):
        hold[k] = block(2 * k + mine, 2 * place + k % 2)
    for k in range(1, count):
        for side in range(2):
            across = min(2 * (k - 1) + side, count - 1)
            at = 2 * lax.rem(place + k, count) + side
            give[k - 1][side] = block(2 * across + 1 - mine, at).astype(bf16)


def merge_terms(keep, taken):
    count = keep.shape[0] // 2
    return pl.pallas_call(
        merge_kernel,
        in_specs=[near, near],
        out_specs=[near] * count,
        out_shape=[jax.ShapeDtypeStruct((count,) + keep.shape[1:], f32)]
        + [jax.ShapeDtypeStruct((2,) + keep.shape[1:], bf16)] * (count - 1),
        compiler_params=roomy,
        cost_estimate=small_cost,
    )(keep, taken)


def split_kernel(hold, *refs):
    count = hold.shape[0]
    landed, own, parts = refs[: count - 1], refs[count - 1], refs[count:]
    spot = lax.axis_index("dp")
    chip = spot // pair
    mine, place = chip % 2, chip // 2

    @pl.when(spot % pair == 0)
    def _():
        sums = [hold[k] + landed[k // 2][k % 2].astype(f32) for k in range(count)]

        def pick(at):
            total = sums[0]
            for k in range(1, count):
                total = jnp.where(at == k, sums[k], total)
            return total

        own[...] = pick(place)
        for k in range(1, count):
            parts[k - 1][...] = pick(lax.rem(place + k, count)).astype(bf16)

    @pl.when(spot % pair != 0)
    def _():
        total = hold[mine]
        passed = hold[1 - mine]
        for part in landed:
            total += part[mine].astype(f32)
            passed += part[1 - mine].astype(f32)
        own[...] = total
        parts[0][...] = passed.astype(bf16)
        for part in parts[1:]:
            part[...] = jnp.zeros_like(part)


def split_terms(hold, landed):
    count = hold.shape[0]
    return pl.pallas_call(
        split_kernel,
        in_specs=[near] * count,
        out_specs=[near] * count,
        out_shape=[jax.ShapeDtypeStruct(hold.shape[1:], f32)]
        + [jax.ShapeDtypeStruct(hold.shape[1:], bf16)] * (count - 1),
        compiler_params=roomy,
        cost_estimate=small_cost,
    )(hold, *landed)


def total_rows(factor, out, own, *landed):
    total = own[...]
    for part in landed:
        total += part[...].astype(f32)
    total = total * factor
    for k in range(out.shape[1] // lanes):
        out[:, k * lanes : (k + 1) * lanes] = total[k : k + 1, :]


def plane_parts(owners, keep, taken):
    quad = 2 * pair
    shifts = range(quad, owners, quad)
    even, odd = range(0, owners, pair), range(1, owners, pair)
    across = [[(i, i ^ pair) for i in one] for one in (even, odd)]
    along = [[[(i, (i + shift) % owners) for i in one] for shift in shifts] for one in (even, odd)]
    hold, *give = merge_terms(keep, taken)
    landed = []
    for k, part in enumerate(give):
        hops = along[1][k] + (across[0] if 2 * k < owners // quad else [])
        landed.append(lax.ppermute(part, "dp", hops))
    own, *parts = split_terms(hold, landed)
    arrived = [lax.ppermute(part, "dp", along[0][k] + (across[1] if k == 0 else [])) for k, part in enumerate(parts)]
    return own, *arrived


def weight_owned(normed, masked, gain, factor):
    owners = lax.axis_size("dp")
    width = normed.shape[1]
    depth = masked.shape[1]
    owned = (width + width * depth) // owners
    if depth != lanes or owned % lanes or owners % (2 * pair):
        weight_term = lax.dot_general(normed, masked, contract_rows, preferred_element_type=f32)
        flat = jnp.concatenate([gain.reshape(-1), weight_term.reshape(-1)]) * factor
        return (), owned, lax.psum_scatter(flat, "dp", scatter_dimension=0, tiled=True)[None, :]
    keep, give = pair_terms(normed, masked, gain, owned // lanes, owners)
    taken = lax.ppermute(give, "dp", [(i, i ^ 1) for i in range(owners)])
    return plane_parts(owners, keep, taken), owned, None


def shards(layer_inputs, top_grad, value_grads, weights, norm_gains, counts):
    rows = layer_inputs.shape[1]
    factor = 1.0 / math.sqrt(rows * lax.axis_size("dp"))
    sections = lax.axis_size("section")
    room = -(-rows * 3 // 4 // pack_rows) * pack_rows
    spare = rows - room
    inputs = (counts, layer_inputs, top_grad, value_grads, weights, norm_gains)
    packed, addend, scatter, more, normed, masked, gain = branch_rows(0, room, *inputs)
    parts, owned_size, owned = weight_owned(normed, masked, gain, factor)
    result = None
    for hop in range(sections - 1):
        target = sections - 2 - hop
        hops = [(target + 1, target), (target, target + 1)]
        before = result
        if hop:
            packed = pack(scatter, before)
        landed = lax.ppermute(packed, "section", hops)
        if hop:
            updated, more = receive(target, scatter, landed, addend, more, before)
        else:
            updated, more, summed = receive(target, scatter, landed, addend, more, None, parts, owned_size, factor)

        def rest(updated):
            packed, addend, scatter, more, *_ = branch_rows(room, spare, *inputs)
            if hop:
                packed = pack(scatter, before)
            landed = lax.ppermute(packed, "section", hops)
            return receive(target, scatter, landed, addend, more, updated[0])[0]

        updated = lax.cond(more.reshape(()) > 0, rest, lambda updated: updated, updated)
        result = updated[0]
    return (result[None], summed if owned is None else owned)


def solution(mesh):
    placed = (
        P("section", "dp", None),
        P("dp", None),
        P("section", "dp", None),
        P("section", None, None),
        P("section", None),
        P("dp"),
    )
    return jax.shard_map(
        shards,
        mesh=mesh,
        in_specs=placed,
        out_specs=(P("section", "dp", None), P("section", "dp")),
        check_vma=False,
    )
```

```python
import functools
import math

import jax
import jax.numpy as jnp
from jax import lax
from jax.experimental import pallas as pl
from jax.experimental.pallas import tpu as pltpu
from jax.sharding import PartitionSpec as P

eps_norm = 1e-05
lanes = 128
sublanes = 8
pack_rows = 16
tile_width = 512
pair = 2
f32 = jnp.float32
bf16 = jnp.bfloat16
contract_last = (((1,), (1,)), ((), ()))
contract_rows = (((0,), (0,)), ((), ()))
small_cost = pl.CostEstimate(flops=1 << 20, bytes_accessed=1 << 16, transcendentals=0)
roomy = pltpu.CompilerParams(vmem_limit_bytes=32 << 20)
near = pl.BlockSpec(memory_space=pltpu.VMEM)
scalar = pl.BlockSpec(memory_space=pltpu.SMEM)


def far(array):
    return pltpu.with_memory_space_constraint(array, pltpu.HBM)


def cuts(width, step):
    return [pl.ds(at, step) for at in range(0, width, step)]


def one_hot(counts, micro_count, slots, low, size):
    slot = lax.broadcasted_iota(jnp.int32, (slots, size), 0)
    column = lax.broadcasted_iota(jnp.int32, (slots, size), 1) + low
    start = jnp.int32(0)
    pieces = []
    for m in range(micro_count):
        hit = (slot < counts[m]) & (slot + start == column)
        pieces.append(jnp.where(hit, 1.0, 0.0))
        start = start + counts[m]
    return jnp.concatenate(pieces, axis=0).astype(bf16)


def branch_kernel(
    low, counts_far, x_far, top_far, v_far, w_far, gain_far,
    packed, addend, scatter, more, normed, masked, gain_out,
    counts, x, top, v, w, gain, back, gain_part, sent, ready,
):
    rows, width = addend.shape
    micro_count = counts.shape[0]
    slots = rows // micro_count
    fetches = [
        pltpu.make_async_copy(v_far.at[0], v, ready.at[0]),
        pltpu.make_async_copy(counts_far, counts, ready.at[1]),
        pltpu.make_async_copy(w_far.at[0], w, ready.at[2]),
        pltpu.make_async_copy(x_far.at[0], x, ready.at[3]),
        pltpu.make_async_copy(gain_far, gain, ready.at[4]),
        pltpu.make_async_copy(top_far, top, ready.at[5]),
    ]
    for fetch in fetches:
        fetch.start()
    fetches[0].wait()
    fetches[1].wait()
    slot = lax.broadcasted_iota(jnp.int32, (slots, v.shape[1]), 0)
    for m in range(micro_count):
        piece = v[m * slots : (m + 1) * slots, :]
        masked[m * slots : (m + 1) * slots, :] = jnp.where(slot < counts[m], piece, jnp.zeros_like(piece))
    live = jnp.int32(0)
    for m in range(micro_count):
        live += counts[m]
    more[0] = (live > low + packed.shape[0]).astype(jnp.int32)
    gather = one_hot(counts, micro_count, slots, low, packed.shape[0])
    receives = lax.axis_index("section") < lax.axis_size("section") - 1
    scatter[...] = jnp.where(receives, gather.astype(f32), 0.0).astype(bf16)
    values = masked[...]
    fetches[2].wait()
    for cut in cuts(width, tile_width):
        back[:, cut] = lax.dot_general(values, w[cut, :], contract_last, preferred_element_type=f32)
    fetches[3].wait()
    fetches[4].wait()
    fetches[5].wait()
    for at in range(0, rows, 32):
        part = slice(at, at + 32)
        squares = jnp.zeros((32, lanes), f32)
        products = jnp.zeros((32, lanes), f32)
        for cut in cuts(width, lanes):
            wide = x[part, cut].astype(f32)
            squares += wide * wide
            products += wide * back[part, cut] * gain[:, cut]
        scale = lax.rsqrt(jnp.sum(squares, axis=1, keepdims=True) / width + eps_norm)
        pull = scale * jnp.sum(products, axis=1, keepdims=True) / width
        waits = jnp.concatenate(
            [
                lax.broadcasted_iota(jnp.int32, (slots, 1), 0) < jnp.where(receives, counts[m], 0)
                for m in range(at // slots, (at + 32) // slots)
            ],
            axis=0,
        )
        for cut in cuts(width, 2 * lanes):
            unit = x[part, cut].astype(f32) * scale
            here = back[part, cut]
            scaled = gain[:, cut]
            product = (unit * here).reshape(32 // sublanes, sublanes, 2 * lanes).sum(axis=0)
            if at:
                product += gain_part[:, cut]
            gain_part[:, cut] = product
            normed[part, cut] = (unit * scaled).astype(bf16)
            own = scale * (scaled * here - unit * pull)
            whole = (top[part, cut].astype(f32) + own).astype(bf16)
            sent[part, cut] = whole
            addend[part, cut] = jnp.where(waits, own, whole.astype(f32))
    for cut in cuts(width, tile_width):
        packed[:, cut] = lax.dot_general(
            gather, sent[:, cut], contract_rows, preferred_element_type=f32
        ).astype(bf16)
    for cut in cuts(width, tile_width):
        gain_out[:, cut] = jnp.sum(gain_part[:, cut], axis=0, keepdims=True)


def branch_rows(low, room, counts, x, top, v, w, gain):
    rows, width = top.shape
    depth = v.shape[2]
    return pl.pallas_call(
        functools.partial(branch_kernel, low),
        in_specs=[pl.BlockSpec(memory_space=pltpu.HBM)] * 6,
        out_specs=[near] * 3 + [scalar] + [near] * 3,
        out_shape=[
            jax.ShapeDtypeStruct((room, width), bf16),
            jax.ShapeDtypeStruct((rows, width), f32),
            jax.ShapeDtypeStruct((rows, room), bf16),
            pltpu.SMEM((1,), jnp.int32),
            jax.ShapeDtypeStruct((rows, width), bf16),
            jax.ShapeDtypeStruct((rows, depth), bf16),
            jax.ShapeDtypeStruct((1, width), f32),
        ],
        scratch_shapes=[
            pltpu.SMEM(counts.shape, jnp.int32),
            pltpu.VMEM((rows, width), bf16),
            pltpu.VMEM((rows, width), bf16),
            pltpu.VMEM((rows, depth), bf16),
            pltpu.VMEM((width, depth), bf16),
            pltpu.VMEM((1, width), f32),
            pltpu.VMEM((rows, width), f32),
            pltpu.VMEM((sublanes, width), f32),
            pltpu.VMEM((rows, width), bf16),
            pltpu.SemaphoreType.DMA((6,)),
        ],
        compiler_params=roomy,
        cost_estimate=small_cost,
    )(*[far(a) for a in (counts, x, top, v, w, gain)])


def pack_kernel(gather, sent, packed):
    for cut in cuts(sent.shape[1], tile_width):
        packed[:, cut] = lax.dot_general(
            gather[...], sent[:, cut], contract_rows, preferred_element_type=f32
        ).astype(bf16)


def pack(gather, sent):
    return pl.pallas_call(
        pack_kernel,
        in_specs=[near, near],
        out_specs=near,
        out_shape=jax.ShapeDtypeStruct((gather.shape[1], sent.shape[1]), bf16),
        compiler_params=roomy,
        cost_estimate=small_cost,
    )(gather, sent)


def receive_kernel(target, first, factor, scatter, received, addend, more, *refs):
    rows, width = addend.shape
    if first:
        *parts, out_far, more_out, owned_far, out, owned, done = refs
    else:
        previous, out_far, more_out, out, done = refs
    more_out[0] = more[0]
    place = scatter[...]
    writes = []
    if first and parts:
        total_rows(factor, owned, *parts)
        writes.append(pltpu.make_async_copy(owned, owned_far, done.at[width // tile_width]))
        writes[0].start()
    if not first:
        here = (lax.axis_index("section") == target).astype(f32)
        covered = jnp.sum(place.astype(f32), axis=1, keepdims=True) * here > 0.5
    for k, cut in enumerate(cuts(width, tile_width)):
        total = jnp.dot(place, received[:, cut], preferred_element_type=f32) + addend[:, cut]
        if not first:
            total = jnp.where(covered, total, previous[:, cut].astype(f32))
        out[:, cut] = total.astype(bf16)
        write = pltpu.make_async_copy(out.at[:, cut], out_far.at[0, :, cut], done.at[k])
        write.start()
        writes.append(write)
    for write in writes:
        write.wait()


def receive(target, scatter, received, addend, more, previous=None, parts=(), owned=lanes, factor=1.0):
    rows, width = addend.shape
    away = pl.BlockSpec(memory_space=pltpu.HBM)
    first = previous is None
    others = parts if first else [previous]
    outs = [pltpu.HBM((1, rows, width), bf16), pltpu.SMEM(more.shape, more.dtype)]
    scratch = [pltpu.VMEM((rows, width), bf16)]
    if first:
        outs.append(pltpu.HBM((1, owned), f32))
        scratch.append(pltpu.VMEM((1, owned), f32))
    return pl.pallas_call(
        functools.partial(receive_kernel, target, first, factor),
        in_specs=[near, near, near, scalar] + [near] * len(others),
        out_specs=[away, scalar] + [away] * first,
        out_shape=outs,
        scratch_shapes=scratch + [pltpu.SemaphoreType.DMA((width // tile_width + 1,))],
        compiler_params=roomy,
        cost_estimate=small_cost,
    )(scatter, received, addend, more, *others)


def terms_kernel(owned_rows, normed, masked, gain, keep, give, total):
    width = normed.shape[1]
    values = masked[...]
    gain_rows = width // lanes
    for k in range(gain_rows):
        total[k : k + 1, :] = gain[:, k * lanes : (k + 1) * lanes]
    for at in range(0, width, tile_width):
        total[gain_rows + at : gain_rows + at + tile_width, :] = lax.dot_general(
            normed[:, at : at + tile_width], values, contract_rows, preferred_element_type=f32
        )
    even_core = lax.axis_index("dp") % pair == 0
    padded = keep.shape[1]
    for j in range(keep.shape[0]):
        even = total[2 * j * owned_rows : (2 * j + 1) * owned_rows, :]
        odd = total[(2 * j + 1) * owned_rows : (2 * j + 2) * owned_rows, :]
        if padded > owned_rows:
            blank = jnp.zeros((padded - owned_rows, lanes), f32)
            even = jnp.concatenate([even, blank], axis=0)
            odd = jnp.concatenate([odd, blank], axis=0)
        keep[j] = jnp.where(even_core, even, odd)
        give[j] = jnp.where(even_core, odd, even).astype(bf16)


def pair_terms(normed, masked, gain, owned_rows, owners):
    padded = -(-owned_rows // pack_rows) * pack_rows
    half = jax.ShapeDtypeStruct((owners // pair, padded, lanes), f32)
    return pl.pallas_call(
        functools.partial(terms_kernel, owned_rows),
        in_specs=[near, near, near],
        out_specs=[near, near],
        out_shape=[half, jax.ShapeDtypeStruct(half.shape, bf16)],
        scratch_shapes=[pltpu.VMEM((owners * owned_rows, lanes), f32)],
        compiler_params=roomy,
        cost_estimate=small_cost,
    )(normed, masked, gain)


def partner(chips, chip, step):
    return chip ^ step if chips & (chips - 1) == 0 else (chip + step) % chips


def merge_kernel(keep, taken, own, *parts):
    chip = lax.axis_index("dp") // pair
    chips = keep.shape[0]
    own[...] = keep[chip] + taken[chip].astype(f32)
    for k, part in enumerate(parts):
        at = partner(chips, chip, k + 1)
        part[...] = (keep[at] + taken[at].astype(f32)).astype(bf16)


def merge_terms(keep, taken):
    chips = keep.shape[0]
    return pl.pallas_call(
        merge_kernel,
        in_specs=[near, near],
        out_specs=[near] * chips,
        out_shape=[jax.ShapeDtypeStruct(keep.shape[1:], f32)]
        + [jax.ShapeDtypeStruct(keep.shape[1:], bf16)] * (chips - 1),
        compiler_params=roomy,
        cost_estimate=small_cost,
    )(keep, taken)


def total_rows(factor, out, own, *landed):
    total = own[...]
    for part in landed:
        total += part[...].astype(f32)
    total = total * factor
    for k in range(out.shape[1] // lanes):
        out[:, k * lanes : (k + 1) * lanes] = total[k : k + 1, :]


def plane_parts(owners, keep, taken):
    own, *parts = merge_terms(keep, taken)
    arrived = []
    for k, part in enumerate(parts):
        hops = [(i, partner(owners // pair, i // pair, k + 1) * pair + i % pair) for i in range(owners)]
        arrived.append(lax.ppermute(part, "dp", hops))
    return own, *arrived


def weight_owned(normed, masked, gain, factor):
    owners = lax.axis_size("dp")
    width = normed.shape[1]
    depth = masked.shape[1]
    owned = (width + width * depth) // owners
    if depth != lanes or owned % lanes or owners % (2 * pair):
        weight_term = lax.dot_general(normed, masked, contract_rows, preferred_element_type=f32)
        flat = jnp.concatenate([gain.reshape(-1), weight_term.reshape(-1)]) * factor
        return (), owned, lax.psum_scatter(flat, "dp", scatter_dimension=0, tiled=True)[None, :]
    keep, give = pair_terms(normed, masked, gain, owned // lanes, owners)
    taken = lax.ppermute(give, "dp", [(i, i ^ 1) for i in range(owners)])
    return plane_parts(owners, keep, taken), owned, None


def shards(layer_inputs, top_grad, value_grads, weights, norm_gains, counts):
    rows = layer_inputs.shape[1]
    factor = 1.0 / math.sqrt(rows * lax.axis_size("dp"))
    sections = lax.axis_size("section")
    room = -(-rows * 3 // 4 // pack_rows) * pack_rows
    spare = rows - room
    inputs = (counts, layer_inputs, top_grad, value_grads, weights, norm_gains)
    packed, addend, scatter, more, normed, masked, gain = branch_rows(0, room, *inputs)
    parts, owned_size, owned = weight_owned(normed, masked, gain, factor)
    result = None
    for hop in range(sections - 1):
        target = sections - 2 - hop
        hops = [(target + 1, target), (target, target + 1)]
        before = result
        if hop:
            packed = pack(scatter, before)
        landed = lax.ppermute(packed, "section", hops)
        if hop:
            updated, more = receive(target, scatter, landed, addend, more, before)
        else:
            updated, more, summed = receive(target, scatter, landed, addend, more, None, parts, owned_size, factor)

        def rest(updated):
            packed, addend, scatter, more, *_ = branch_rows(room, spare, *inputs)
            if hop:
                packed = pack(scatter, before)
            landed = lax.ppermute(packed, "section", hops)
            return receive(target, scatter, landed, addend, more, updated[0])[0]

        updated = lax.cond(more.reshape(()) > 0, rest, lambda updated: updated, updated)
        result = updated[0]
    return (result[None], summed if owned is None else owned)


def solution(mesh):
    placed = (
        P("section", "dp", None),
        P("dp", None),
        P("section", "dp", None),
        P("section", None, None),
        P("section", None),
        P("dp"),
    )
    return jax.shard_map(
        shards,
        mesh=mesh,
        in_specs=placed,
        out_specs=(P("section", "dp", None), P("section", "dp")),
        check_vma=False,
    )
```

```python
import functools
import math

import jax
import jax.numpy as jnp
from jax import lax
from jax.experimental import pallas as pl
from jax.experimental.pallas import tpu as pltpu
from jax.sharding import PartitionSpec as P

eps_norm = 1e-05
lanes = 128
sublanes = 8
pack_rows = 16
tile_width = 512
pair = 2
f32 = jnp.float32
bf16 = jnp.bfloat16
contract_last = (((1,), (1,)), ((), ()))
contract_rows = (((0,), (0,)), ((), ()))
small_cost = pl.CostEstimate(flops=1 << 20, bytes_accessed=1 << 16, transcendentals=0)
roomy = pltpu.CompilerParams(vmem_limit_bytes=32 << 20)
near = pl.BlockSpec(memory_space=pltpu.VMEM)
scalar = pl.BlockSpec(memory_space=pltpu.SMEM)


def far(array):
    return pltpu.with_memory_space_constraint(array, pltpu.HBM)


def cuts(width, step):
    return [pl.ds(at, step) for at in range(0, width, step)]


def one_hot(counts, micro_count, slots, low, size):
    slot = lax.broadcasted_iota(jnp.int32, (slots, size), 0)
    column = lax.broadcasted_iota(jnp.int32, (slots, size), 1) + low
    start = jnp.int32(0)
    pieces = []
    for m in range(micro_count):
        hit = (slot < counts[m]) & (slot + start == column)
        pieces.append(jnp.where(hit, 1.0, 0.0))
        start = start + counts[m]
    return jnp.concatenate(pieces, axis=0).astype(bf16)


def branch_kernel(
    low, counts_far, x_far, top_far, v_far, w_far, gain_far,
    packed, addend, scatter, more, normed, masked, gain_out,
    counts, x, top, v, w, gain, back, gain_part, sent, ready,
):
    rows, width = addend.shape
    micro_count = counts.shape[0]
    slots = rows // micro_count
    fetches = [
        pltpu.make_async_copy(v_far.at[0], v, ready.at[0]),
        pltpu.make_async_copy(counts_far, counts, ready.at[1]),
        pltpu.make_async_copy(w_far.at[0], w, ready.at[2]),
        pltpu.make_async_copy(x_far.at[0], x, ready.at[3]),
        pltpu.make_async_copy(gain_far, gain, ready.at[4]),
        pltpu.make_async_copy(top_far, top, ready.at[5]),
    ]
    for fetch in fetches:
        fetch.start()
    fetches[0].wait()
    fetches[1].wait()
    slot = lax.broadcasted_iota(jnp.int32, (slots, v.shape[1]), 0)
    for m in range(micro_count):
        piece = v[m * slots : (m + 1) * slots, :]
        masked[m * slots : (m + 1) * slots, :] = jnp.where(slot < counts[m], piece, jnp.zeros_like(piece))
    live = jnp.int32(0)
    for m in range(micro_count):
        live += counts[m]
    more[0] = (live > low + packed.shape[0]).astype(jnp.int32)
    gather = one_hot(counts, micro_count, slots, low, packed.shape[0])
    receives = lax.axis_index("section") < lax.axis_size("section") - 1
    scatter[...] = jnp.where(receives, gather.astype(f32), 0.0).astype(bf16)
    values = masked[...]
    fetches[2].wait()
    for cut in cuts(width, tile_width):
        back[:, cut] = lax.dot_general(values, w[cut, :], contract_last, preferred_element_type=f32)
    fetches[3].wait()
    fetches[4].wait()
    fetches[5].wait()
    for at in range(0, rows, 32):
        part = slice(at, at + 32)
        squares = jnp.zeros((32, lanes), f32)
        products = jnp.zeros((32, lanes), f32)
        for cut in cuts(width, lanes):
            wide = x[part, cut].astype(f32)
            squares += wide * wide
            products += wide * back[part, cut] * gain[:, cut]
        scale = lax.rsqrt(jnp.sum(squares, axis=1, keepdims=True) / width + eps_norm)
        pull = scale * jnp.sum(products, axis=1, keepdims=True) / width
        waits = jnp.concatenate(
            [
                lax.broadcasted_iota(jnp.int32, (slots, 1), 0) < jnp.where(receives, counts[m], 0)
                for m in range(at // slots, (at + 32) // slots)
            ],
            axis=0,
        )
        for cut in cuts(width, 2 * lanes):
            unit = x[part, cut].astype(f32) * scale
            here = back[part, cut]
            scaled = gain[:, cut]
            product = (unit * here).reshape(32 // sublanes, sublanes, 2 * lanes).sum(axis=0)
            if at:
                product += gain_part[:, cut]
            gain_part[:, cut] = product
            normed[part, cut] = (unit * scaled).astype(bf16)
            own = scale * (scaled * here - unit * pull)
            whole = (top[part, cut].astype(f32) + own).astype(bf16)
            sent[part, cut] = whole
            addend[part, cut] = jnp.where(waits, own, whole.astype(f32))
    for cut in cuts(width, tile_width):
        packed[:, cut] = lax.dot_general(
            gather, sent[:, cut], contract_rows, preferred_element_type=f32
        ).astype(bf16)
    for cut in cuts(width, tile_width):
        gain_out[:, cut] = jnp.sum(gain_part[:, cut], axis=0, keepdims=True)


def branch_rows(low, room, counts, x, top, v, w, gain):
    rows, width = top.shape
    depth = v.shape[2]
    return pl.pallas_call(
        functools.partial(branch_kernel, low),
        in_specs=[pl.BlockSpec(memory_space=pltpu.HBM)] * 6,
        out_specs=[near] * 3 + [scalar] + [near] * 3,
        out_shape=[
            jax.ShapeDtypeStruct((room, width), bf16),
            jax.ShapeDtypeStruct((rows, width), f32),
            jax.ShapeDtypeStruct((rows, room), bf16),
            pltpu.SMEM((1,), jnp.int32),
            jax.ShapeDtypeStruct((rows, width), bf16),
            jax.ShapeDtypeStruct((rows, depth), bf16),
            jax.ShapeDtypeStruct((1, width), f32),
        ],
        scratch_shapes=[
            pltpu.SMEM(counts.shape, jnp.int32),
            pltpu.VMEM((rows, width), bf16),
            pltpu.VMEM((rows, width), bf16),
            pltpu.VMEM((rows, depth), bf16),
            pltpu.VMEM((width, depth), bf16),
            pltpu.VMEM((1, width), f32),
            pltpu.VMEM((rows, width), f32),
            pltpu.VMEM((sublanes, width), f32),
            pltpu.VMEM((rows, width), bf16),
            pltpu.SemaphoreType.DMA((6,)),
        ],
        compiler_params=roomy,
        cost_estimate=small_cost,
    )(*[far(a) for a in (counts, x, top, v, w, gain)])


def pack_kernel(gather, sent, packed):
    for cut in cuts(sent.shape[1], tile_width):
        packed[:, cut] = lax.dot_general(
            gather[...], sent[:, cut], contract_rows, preferred_element_type=f32
        ).astype(bf16)


def pack(gather, sent):
    return pl.pallas_call(
        pack_kernel,
        in_specs=[near, near],
        out_specs=near,
        out_shape=jax.ShapeDtypeStruct((gather.shape[1], sent.shape[1]), bf16),
        compiler_params=roomy,
        cost_estimate=small_cost,
    )(gather, sent)


def receive_kernel(target, first, factor, scatter, received, addend, more, *refs):
    rows, width = addend.shape
    if first:
        *parts, out_far, more_out, owned_far, out, owned, done = refs
    else:
        previous, out_far, more_out, out, done = refs
    more_out[0] = more[0]
    place = scatter[...]
    writes = []
    if first and parts:
        total_rows(factor, owned, *parts)
        writes.append(pltpu.make_async_copy(owned, owned_far, done.at[width // tile_width]))
        writes[0].start()
    if not first:
        here = (lax.axis_index("section") == target).astype(f32)
        covered = jnp.sum(place.astype(f32), axis=1, keepdims=True) * here > 0.5
    for k, cut in enumerate(cuts(width, tile_width)):
        total = jnp.dot(place, received[:, cut], preferred_element_type=f32) + addend[:, cut]
        if not first:
            total = jnp.where(covered, total, previous[:, cut].astype(f32))
        out[:, cut] = total.astype(bf16)
        write = pltpu.make_async_copy(out.at[:, cut], out_far.at[0, :, cut], done.at[k])
        write.start()
        writes.append(write)
    for write in writes:
        write.wait()


def receive(target, scatter, received, addend, more, previous=None, parts=(), owned=lanes, factor=1.0):
    rows, width = addend.shape
    away = pl.BlockSpec(memory_space=pltpu.HBM)
    first = previous is None
    others = parts if first else [previous]
    outs = [pltpu.HBM((1, rows, width), bf16), pltpu.SMEM(more.shape, more.dtype)]
    scratch = [pltpu.VMEM((rows, width), bf16)]
    if first:
        outs.append(pltpu.HBM((1, owned), f32))
        scratch.append(pltpu.VMEM((1, owned), f32))
    return pl.pallas_call(
        functools.partial(receive_kernel, target, first, factor),
        in_specs=[near, near, near, scalar] + [near] * len(others),
        out_specs=[away, scalar] + [away] * first,
        out_shape=outs,
        scratch_shapes=scratch + [pltpu.SemaphoreType.DMA((width // tile_width + 1,))],
        compiler_params=roomy,
        cost_estimate=small_cost,
    )(scatter, received, addend, more, *others)


def terms_kernel(owned_rows, normed, masked, gain, keep, give, total):
    width = normed.shape[1]
    values = masked[...]
    gain_rows = width // lanes
    for k in range(gain_rows):
        total[k : k + 1, :] = gain[:, k * lanes : (k + 1) * lanes]
    for at in range(0, width, tile_width):
        total[gain_rows + at : gain_rows + at + tile_width, :] = lax.dot_general(
            normed[:, at : at + tile_width], values, contract_rows, preferred_element_type=f32
        )
    even_core = lax.axis_index("dp") % pair == 0
    padded = keep.shape[1]
    for j in range(keep.shape[0]):
        even = total[2 * j * owned_rows : (2 * j + 1) * owned_rows, :]
        odd = total[(2 * j + 1) * owned_rows : (2 * j + 2) * owned_rows, :]
        if padded > owned_rows:
            blank = jnp.zeros((padded - owned_rows, lanes), f32)
            even = jnp.concatenate([even, blank], axis=0)
            odd = jnp.concatenate([odd, blank], axis=0)
        keep[j] = jnp.where(even_core, even, odd)
        give[j] = jnp.where(even_core, odd, even).astype(bf16)


def pair_terms(normed, masked, gain, owned_rows, owners):
    padded = -(-owned_rows // pack_rows) * pack_rows
    half = jax.ShapeDtypeStruct((owners // pair, padded, lanes), f32)
    return pl.pallas_call(
        functools.partial(terms_kernel, owned_rows),
        in_specs=[near, near, near],
        out_specs=[near, near],
        out_shape=[half, jax.ShapeDtypeStruct(half.shape, bf16)],
        scratch_shapes=[pltpu.VMEM((owners * owned_rows, lanes), f32)],
        compiler_params=roomy,
        cost_estimate=small_cost,
    )(normed, masked, gain)


def merge_kernel(offsets, keep, taken, *halves):
    chip = lax.axis_index("dp") // pair
    mine, place = chip % 2, chip // 2
    count = keep.shape[0] // 2
    for part, (hold, give) in zip(offsets, (halves[:2], halves[2:])):
        for k, offset in enumerate(part):
            at = 2 * lax.rem(place + offset, count)
            hold[k] = keep[at + mine] + taken[at + mine].astype(f32)
            give[k] = (keep[at + 1 - mine] + taken[at + 1 - mine].astype(f32)).astype(bf16)


def merge_terms(offsets, keep, taken):
    outs = []
    for part in offsets:
        block = (len(part),) + keep.shape[1:]
        outs += [jax.ShapeDtypeStruct(block, f32), jax.ShapeDtypeStruct(block, bf16)]
    return pl.pallas_call(
        functools.partial(merge_kernel, offsets),
        in_specs=[near, near],
        out_specs=[near] * len(outs),
        out_shape=outs,
        compiler_params=roomy,
        cost_estimate=small_cost,
    )(keep, taken)


def split_kernel(hold, taken, *parts):
    for k, part in enumerate(parts):
        part[...] = (hold[k] + taken[k].astype(f32)).astype(part.dtype)


def split_terms(part, hold, taken):
    return pl.pallas_call(
        split_kernel,
        in_specs=[near, near],
        out_specs=[near] * len(part),
        out_shape=[jax.ShapeDtypeStruct(hold.shape[1:], bf16 if offset else f32) for offset in part],
        compiler_params=roomy,
        cost_estimate=small_cost,
    )(hold, taken)


def total_rows(factor, out, own, *landed):
    total = own[...]
    for part in landed:
        total += part[...].astype(f32)
    total = total * factor
    for k in range(out.shape[1] // lanes):
        out[:, k * lanes : (k + 1) * lanes] = total[k : k + 1, :]


def plane_parts(owners, keep, taken):
    quad = 2 * pair
    count = owners // quad
    order = [0, count // 2, *(k for k in range(1, count) if k != count // 2)]
    offsets = (order[:2], order[2:])
    hold, give, hold_next, give_next = merge_terms(offsets, keep, taken)
    near_by = [(i, i ^ pair) for i in range(owners)]
    across = [lax.ppermute(part, "dp", near_by) for part in (give, give_next)]
    own, *parts = split_terms(offsets[0], hold, across[0])
    parts += split_terms(offsets[1], hold_next, across[1])
    arrived = []
    for offset, part in zip(order[1:], parts):
        arrived.append(lax.ppermute(part, "dp", [(i, (i + quad * offset) % owners) for i in range(owners)]))
    return own, *arrived


def weight_owned(normed, masked, gain, factor):
    owners = lax.axis_size("dp")
    width = normed.shape[1]
    depth = masked.shape[1]
    owned = (width + width * depth) // owners
    if depth != lanes or owned % lanes or owners % (2 * pair):
        weight_term = lax.dot_general(normed, masked, contract_rows, preferred_element_type=f32)
        flat = jnp.concatenate([gain.reshape(-1), weight_term.reshape(-1)]) * factor
        return (), owned, lax.psum_scatter(flat, "dp", scatter_dimension=0, tiled=True)[None, :]
    keep, give = pair_terms(normed, masked, gain, owned // lanes, owners)
    taken = lax.ppermute(give, "dp", [(i, i ^ 1) for i in range(owners)])
    return plane_parts(owners, keep, taken), owned, None


def shards(layer_inputs, top_grad, value_grads, weights, norm_gains, counts):
    rows = layer_inputs.shape[1]
    factor = 1.0 / math.sqrt(rows * lax.axis_size("dp"))
    sections = lax.axis_size("section")
    room = -(-rows * 3 // 4 // pack_rows) * pack_rows
    spare = rows - room
    inputs = (counts, layer_inputs, top_grad, value_grads, weights, norm_gains)
    packed, addend, scatter, more, normed, masked, gain = branch_rows(0, room, *inputs)
    parts, owned_size, owned = weight_owned(normed, masked, gain, factor)
    result = None
    for hop in range(sections - 1):
        target = sections - 2 - hop
        hops = [(target + 1, target), (target, target + 1)]
        before = result
        if hop:
            packed = pack(scatter, before)
        landed = lax.ppermute(packed, "section", hops)
        if hop:
            updated, more = receive(target, scatter, landed, addend, more, before)
        else:
            updated, more, summed = receive(target, scatter, landed, addend, more, None, parts, owned_size, factor)

        def rest(updated):
            packed, addend, scatter, more, *_ = branch_rows(room, spare, *inputs)
            if hop:
                packed = pack(scatter, before)
            landed = lax.ppermute(packed, "section", hops)
            return receive(target, scatter, landed, addend, more, updated[0])[0]

        updated = lax.cond(more.reshape(()) > 0, rest, lambda updated: updated, updated)
        result = updated[0]
    return (result[None], summed if owned is None else owned)


def solution(mesh):
    placed = (
        P("section", "dp", None),
        P("dp", None),
        P("section", "dp", None),
        P("section", None, None),
        P("section", None),
        P("dp"),
    )
    return jax.shard_map(
        shards,
        mesh=mesh,
        in_specs=placed,
        out_specs=(P("section", "dp", None), P("section", "dp")),
        check_vma=False,
    )
```

```python
import functools
import math

import jax
import jax.numpy as jnp
from jax import lax
from jax.experimental import pallas as pl
from jax.experimental.pallas import tpu as pltpu
from jax.sharding import PartitionSpec as P

eps_norm = 1e-05
lanes = 128
sublanes = 8
pack_rows = 16
tile_width = 512
pair = 2
f32 = jnp.float32
bf16 = jnp.bfloat16
contract_last = (((1,), (1,)), ((), ()))
contract_rows = (((0,), (0,)), ((), ()))
small_cost = pl.CostEstimate(flops=1 << 20, bytes_accessed=1 << 16, transcendentals=0)
roomy = pltpu.CompilerParams(vmem_limit_bytes=32 << 20)
near = pl.BlockSpec(memory_space=pltpu.VMEM)
scalar = pl.BlockSpec(memory_space=pltpu.SMEM)


def far(array):
    return pltpu.with_memory_space_constraint(array, pltpu.HBM)


def cuts(width, step):
    return [pl.ds(at, step) for at in range(0, width, step)]


def one_hot(counts, micro_count, slots, low, size):
    slot = lax.broadcasted_iota(jnp.int32, (slots, size), 0)
    column = lax.broadcasted_iota(jnp.int32, (slots, size), 1) + low
    start = jnp.int32(0)
    pieces = []
    for m in range(micro_count):
        hit = (slot < counts[m]) & (slot + start == column)
        pieces.append(jnp.where(hit, 1.0, 0.0))
        start = start + counts[m]
    return jnp.concatenate(pieces, axis=0).astype(bf16)


def branch_kernel(
    low, counts_far, x_far, top_far, v_far, w_far, gain_far,
    packed, addend, scatter, more, normed, masked, gain_out,
    counts, x, top, v, w, gain, back, gain_part, sent, ready,
):
    rows, width = addend.shape
    micro_count = counts.shape[0]
    slots = rows // micro_count
    fetches = [
        pltpu.make_async_copy(v_far.at[0], v, ready.at[0]),
        pltpu.make_async_copy(counts_far, counts, ready.at[1]),
        pltpu.make_async_copy(w_far.at[0], w, ready.at[2]),
        pltpu.make_async_copy(x_far.at[0], x, ready.at[3]),
        pltpu.make_async_copy(gain_far, gain, ready.at[4]),
        pltpu.make_async_copy(top_far, top, ready.at[5]),
    ]
    for fetch in fetches:
        fetch.start()
    fetches[0].wait()
    fetches[1].wait()
    slot = lax.broadcasted_iota(jnp.int32, (slots, v.shape[1]), 0)
    for m in range(micro_count):
        piece = v[m * slots : (m + 1) * slots, :]
        masked[m * slots : (m + 1) * slots, :] = jnp.where(slot < counts[m], piece, jnp.zeros_like(piece))
    live = jnp.int32(0)
    for m in range(micro_count):
        live += counts[m]
    more[0] = (live > low + packed.shape[0]).astype(jnp.int32)
    gather = one_hot(counts, micro_count, slots, low, packed.shape[0])
    receives = lax.axis_index("section") < lax.axis_size("section") - 1
    scatter[...] = jnp.where(receives, gather.astype(f32), 0.0).astype(bf16)
    values = masked[...]
    fetches[2].wait()
    for cut in cuts(width, tile_width):
        back[:, cut] = lax.dot_general(values, w[cut, :], contract_last, preferred_element_type=f32)
    fetches[3].wait()
    fetches[4].wait()
    fetches[5].wait()
    for at in range(0, rows, 32):
        part = slice(at, at + 32)
        squares = jnp.zeros((32, lanes), f32)
        products = jnp.zeros((32, lanes), f32)
        for cut in cuts(width, lanes):
            wide = x[part, cut].astype(f32)
            squares += wide * wide
            products += wide * back[part, cut] * gain[:, cut]
        scale = lax.rsqrt(jnp.sum(squares, axis=1, keepdims=True) / width + eps_norm)
        pull = scale * jnp.sum(products, axis=1, keepdims=True) / width
        waits = jnp.concatenate(
            [
                lax.broadcasted_iota(jnp.int32, (slots, 1), 0) < jnp.where(receives, counts[m], 0)
                for m in range(at // slots, (at + 32) // slots)
            ],
            axis=0,
        )
        for cut in cuts(width, 2 * lanes):
            unit = x[part, cut].astype(f32) * scale
            here = back[part, cut]
            scaled = gain[:, cut]
            product = (unit * here).reshape(32 // sublanes, sublanes, 2 * lanes).sum(axis=0)
            if at:
                product += gain_part[:, cut]
            gain_part[:, cut] = product
            normed[part, cut] = (unit * scaled).astype(bf16)
            own = scale * (scaled * here - unit * pull)
            whole = (top[part, cut].astype(f32) + own).astype(bf16)
            sent[part, cut] = whole
            addend[part, cut] = jnp.where(waits, own, whole.astype(f32))
    for cut in cuts(width, tile_width):
        packed[:, cut] = lax.dot_general(
            gather, sent[:, cut], contract_rows, preferred_element_type=f32
        ).astype(bf16)
    for cut in cuts(width, tile_width):
        gain_out[:, cut] = jnp.sum(gain_part[:, cut], axis=0, keepdims=True)


def branch_rows(low, room, counts, x, top, v, w, gain):
    rows, width = top.shape
    depth = v.shape[2]
    return pl.pallas_call(
        functools.partial(branch_kernel, low),
        in_specs=[pl.BlockSpec(memory_space=pltpu.HBM)] * 6,
        out_specs=[near] * 3 + [scalar] + [near] * 3,
        out_shape=[
            jax.ShapeDtypeStruct((room, width), bf16),
            jax.ShapeDtypeStruct((rows, width), f32),
            jax.ShapeDtypeStruct((rows, room), bf16),
            pltpu.SMEM((1,), jnp.int32),
            jax.ShapeDtypeStruct((rows, width), bf16),
            jax.ShapeDtypeStruct((rows, depth), bf16),
            jax.ShapeDtypeStruct((1, width), f32),
        ],
        scratch_shapes=[
            pltpu.SMEM(counts.shape, jnp.int32),
            pltpu.VMEM((rows, width), bf16),
            pltpu.VMEM((rows, width), bf16),
            pltpu.VMEM((rows, depth), bf16),
            pltpu.VMEM((width, depth), bf16),
            pltpu.VMEM((1, width), f32),
            pltpu.VMEM((rows, width), f32),
            pltpu.VMEM((sublanes, width), f32),
            pltpu.VMEM((rows, width), bf16),
            pltpu.SemaphoreType.DMA((6,)),
        ],
        compiler_params=roomy,
        cost_estimate=small_cost,
    )(*[far(a) for a in (counts, x, top, v, w, gain)])


def pack_kernel(gather, sent, packed):
    for cut in cuts(sent.shape[1], tile_width):
        packed[:, cut] = lax.dot_general(
            gather[...], sent[:, cut], contract_rows, preferred_element_type=f32
        ).astype(bf16)


def pack(gather, sent):
    return pl.pallas_call(
        pack_kernel,
        in_specs=[near, near],
        out_specs=near,
        out_shape=jax.ShapeDtypeStruct((gather.shape[1], sent.shape[1]), bf16),
        compiler_params=roomy,
        cost_estimate=small_cost,
    )(gather, sent)


def receive_kernel(target, first, factor, scatter, received, addend, more, *refs):
    rows, width = addend.shape
    if first:
        *parts, out_far, more_out, owned_far, out, owned, done = refs
    else:
        previous, out_far, more_out, out, done = refs
    more_out[0] = more[0]
    place = scatter[...]
    writes = []
    if first and parts:
        total_rows(factor, owned, *parts)
        writes.append(pltpu.make_async_copy(owned, owned_far, done.at[width // tile_width]))
        writes[0].start()
    if not first:
        here = (lax.axis_index("section") == target).astype(f32)
        covered = jnp.sum(place.astype(f32), axis=1, keepdims=True) * here > 0.5
    for k, cut in enumerate(cuts(width, tile_width)):
        total = jnp.dot(place, received[:, cut], preferred_element_type=f32) + addend[:, cut]
        if not first:
            total = jnp.where(covered, total, previous[:, cut].astype(f32))
        out[:, cut] = total.astype(bf16)
        write = pltpu.make_async_copy(out.at[:, cut], out_far.at[0, :, cut], done.at[k])
        write.start()
        writes.append(write)
    for write in writes:
        write.wait()


def receive(target, scatter, received, addend, more, previous=None, parts=(), owned=lanes, factor=1.0):
    rows, width = addend.shape
    away = pl.BlockSpec(memory_space=pltpu.HBM)
    first = previous is None
    others = parts if first else [previous]
    outs = [pltpu.HBM((1, rows, width), bf16), pltpu.SMEM(more.shape, more.dtype)]
    scratch = [pltpu.VMEM((rows, width), bf16)]
    if first:
        outs.append(pltpu.HBM((1, owned), f32))
        scratch.append(pltpu.VMEM((1, owned), f32))
    return pl.pallas_call(
        functools.partial(receive_kernel, target, first, factor),
        in_specs=[near, near, near, scalar] + [near] * len(others),
        out_specs=[away, scalar] + [away] * first,
        out_shape=outs,
        scratch_shapes=scratch + [pltpu.SemaphoreType.DMA((width // tile_width + 1,))],
        compiler_params=roomy,
        cost_estimate=small_cost,
    )(scatter, received, addend, more, *others)


def terms_kernel(owned_rows, normed, masked, gain, keep, give, give_low, total):
    width = normed.shape[1]
    values = masked[...]
    gain_rows = width // lanes
    for k in range(gain_rows):
        total[k : k + 1, :] = gain[:, k * lanes : (k + 1) * lanes]
    for at in range(0, width, tile_width):
        total[gain_rows + at : gain_rows + at + tile_width, :] = lax.dot_general(
            normed[:, at : at + tile_width], values, contract_rows, preferred_element_type=f32
        )
    even_core = lax.axis_index("dp") % pair == 0
    padded = keep.shape[1]
    for j in range(keep.shape[0]):
        even = total[2 * j * owned_rows : (2 * j + 1) * owned_rows, :]
        odd = total[(2 * j + 1) * owned_rows : (2 * j + 2) * owned_rows, :]
        if padded > owned_rows:
            blank = jnp.zeros((padded - owned_rows, lanes), f32)
            even = jnp.concatenate([even, blank], axis=0)
            odd = jnp.concatenate([odd, blank], axis=0)
        keep[j] = jnp.where(even_core, even, odd)
        other = jnp.where(even_core, odd, even).astype(bf16)
        give[j] = other[: give.shape[1], :]
        give_low[j] = other[give.shape[1] :, :]


def pair_terms(normed, masked, gain, owned_rows, owners):
    padded = -(-owned_rows // pack_rows) * pack_rows
    cut = padded // 2 // pack_rows * pack_rows
    blocks = owners // pair
    return pl.pallas_call(
        functools.partial(terms_kernel, owned_rows),
        in_specs=[near, near, near],
        out_specs=[near, near, near],
        out_shape=[
            jax.ShapeDtypeStruct((blocks, padded, lanes), f32),
            jax.ShapeDtypeStruct((blocks, cut, lanes), bf16),
            jax.ShapeDtypeStruct((blocks, padded - cut, lanes), bf16),
        ],
        scratch_shapes=[pltpu.VMEM((owners * owned_rows, lanes), f32)],
        compiler_params=roomy,
        cost_estimate=small_cost,
    )(normed, masked, gain)


def merge_kernel(offsets, direct, keep, taken, taken_low, hold, give, *straight):
    chip = lax.axis_index("dp") // pair
    mine, place = chip % 2, chip // 2
    count = keep.shape[0] // 2
    cut = taken.shape[1]

    def total(at, out):
        high = keep[at, :cut, :] + taken[at].astype(f32)
        low = keep[at, cut:, :] + taken_low[at].astype(f32)
        out[:cut, :] = high.astype(out.dtype)
        out[cut:, :] = low.astype(out.dtype)

    for k, offset in enumerate(offsets):
        at = 2 * lax.rem(place + offset, count)
        total(at + mine, hold.at[k])
        total(at + 1 - mine, give.at[k])
    for k, offset in enumerate(direct):
        at = 2 * lax.rem(place + offset, count)
        total(at + mine, straight[2 * k])
        total(at + 1 - mine, straight[2 * k + 1])


def merge_terms(offsets, direct, keep, taken, taken_low):
    block = keep.shape[1:]
    outs = [
        jax.ShapeDtypeStruct((len(offsets),) + block, f32),
        jax.ShapeDtypeStruct((len(offsets),) + block, bf16),
    ] + [jax.ShapeDtypeStruct(block, bf16)] * (2 * len(direct))
    return pl.pallas_call(
        functools.partial(merge_kernel, offsets, direct),
        in_specs=[near, near, near],
        out_specs=[near] * len(outs),
        out_shape=outs,
        compiler_params=roomy,
        cost_estimate=small_cost,
    )(keep, taken, taken_low)


def split_kernel(hold, taken, *parts):
    for k, part in enumerate(parts):
        part[...] = (hold[k] + taken[k].astype(f32)).astype(part.dtype)


def split_terms(part, hold, taken):
    return pl.pallas_call(
        split_kernel,
        in_specs=[near, near],
        out_specs=[near] * len(part),
        out_shape=[jax.ShapeDtypeStruct(hold.shape[1:], bf16 if offset else f32) for offset in part],
        compiler_params=roomy,
        cost_estimate=small_cost,
    )(hold, taken)


def total_rows(factor, out, own, *landed):
    total = own[...]
    for part in landed:
        total += part[...].astype(f32)
    total = total * factor
    for k in range(out.shape[1] // lanes):
        out[:, k * lanes : (k + 1) * lanes] = total[k : k + 1, :]


def plane_parts(owners, keep, *taken):
    quad = 2 * pair
    count = owners // quad
    direct = [count // 2] if count > 2 else []
    offsets = [k for k in range(count) if k not in direct]

    def along(offset, side):
        return [(i, (i + quad * offset) % owners ^ pair * side) for i in range(owners)]

    hold, give, *straight = merge_terms(offsets, direct, keep, *taken)
    across = lax.ppermute(give, "dp", along(0, 1))
    arrived = [
        lax.ppermute(straight[2 * k + side], "dp", along(offset, side))
        for k, offset in enumerate(direct)
        for side in range(2)
    ]
    own, *parts = split_terms(offsets, hold, across)
    for offset, part in zip(offsets[1:], parts):
        arrived.append(lax.ppermute(part, "dp", along(offset, 0)))
    return own, *arrived


def weight_owned(normed, masked, gain, factor):
    owners = lax.axis_size("dp")
    width = normed.shape[1]
    depth = masked.shape[1]
    owned = (width + width * depth) // owners
    if depth != lanes or owned % lanes or owners % (2 * pair):
        weight_term = lax.dot_general(normed, masked, contract_rows, preferred_element_type=f32)
        flat = jnp.concatenate([gain.reshape(-1), weight_term.reshape(-1)]) * factor
        return (), owned, lax.psum_scatter(flat, "dp", scatter_dimension=0, tiled=True)[None, :]
    keep, *give = pair_terms(normed, masked, gain, owned // lanes, owners)
    taken = [lax.ppermute(part, "dp", [(i, i ^ 1) for i in range(owners)]) for part in give]
    return plane_parts(owners, keep, *taken), owned, None


def shards(layer_inputs, top_grad, value_grads, weights, norm_gains, counts):
    rows = layer_inputs.shape[1]
    factor = 1.0 / math.sqrt(rows * lax.axis_size("dp"))
    sections = lax.axis_size("section")
    room = -(-rows * 3 // 4 // pack_rows) * pack_rows
    spare = rows - room
    inputs = (counts, layer_inputs, top_grad, value_grads, weights, norm_gains)
    packed, addend, scatter, more, normed, masked, gain = branch_rows(0, room, *inputs)
    parts, owned_size, owned = weight_owned(normed, masked, gain, factor)
    result = None
    for hop in range(sections - 1):
        target = sections - 2 - hop
        hops = [(target + 1, target), (target, target + 1)]
        before = result
        if hop:
            packed = pack(scatter, before)
        landed = lax.ppermute(packed, "section", hops)
        if hop:
            updated, more = receive(target, scatter, landed, addend, more, before)
        else:
            updated, more, summed = receive(target, scatter, landed, addend, more, None, parts, owned_size, factor)

        def rest(updated):
            packed, addend, scatter, more, *_ = branch_rows(room, spare, *inputs)
            if hop:
                packed = pack(scatter, before)
            landed = lax.ppermute(packed, "section", hops)
            return receive(target, scatter, landed, addend, more, updated[0])[0]

        updated = lax.cond(more.reshape(()) > 0, rest, lambda updated: updated, updated)
        result = updated[0]
    return (result[None], summed if owned is None else owned)


def solution(mesh):
    placed = (
        P("section", "dp", None),
        P("dp", None),
        P("section", "dp", None),
        P("section", None, None),
        P("section", None),
        P("dp"),
    )
    return jax.shard_map(
        shards,
        mesh=mesh,
        in_specs=placed,
        out_specs=(P("section", "dp", None), P("section", "dp")),
        check_vma=False,
    )
```

```python
import functools
import math

import jax
import jax.numpy as jnp
from jax import lax
from jax.experimental import pallas as pl
from jax.experimental.pallas import tpu as pltpu
from jax.sharding import PartitionSpec as P

eps_norm = 1e-05
lanes = 128
sublanes = 8
pack_rows = 16
tile_width = 512
pair = 2
block_rows = 32
pieces = 4
f32 = jnp.float32
bf16 = jnp.bfloat16
contract_last = (((1,), (1,)), ((), ()))
contract_rows = (((0,), (0,)), ((), ()))
small_cost = pl.CostEstimate(flops=1 << 20, bytes_accessed=1 << 16, transcendentals=0)
roomy = pltpu.CompilerParams(vmem_limit_bytes=32 << 20)
near = pl.BlockSpec(memory_space=pltpu.VMEM)
scalar = pl.BlockSpec(memory_space=pltpu.SMEM)


def far(array):
    return pltpu.with_memory_space_constraint(array, pltpu.HBM)


def cuts(width, step):
    return [pl.ds(at, step) for at in range(0, width, step)]


def one_hot(counts, micro_count, slots, low, size):
    slot = lax.broadcasted_iota(jnp.int32, (slots, size), 0)
    column = lax.broadcasted_iota(jnp.int32, (slots, size), 1) + low
    start = jnp.int32(0)
    pieces = []
    for m in range(micro_count):
        hit = (slot < counts[m]) & (slot + start == column)
        pieces.append(jnp.where(hit, 1.0, 0.0))
        start = start + counts[m]
    return jnp.concatenate(pieces, axis=0).astype(bf16)


def branch_kernel(
    low, counts_far, x_far, top_far, v_far, w_far, gain_far,
    packed, addend, scatter, more, normed, masked, gain_out,
    counts, x, top, v, w, gain, back, gain_part, sent, ready,
):
    rows, width = addend.shape
    micro_count = counts.shape[0]
    slots = rows // micro_count
    bands = cuts(width, width // pieces)
    blocks = [pl.ds(at, block_rows) for at in range(0, rows, block_rows)]
    pairs = [(v_far.at[0], v), (counts_far, counts), (gain_far, gain)]
    pairs += [(w_far.at[0, band, :], w.at[band, :]) for band in bands]
    pairs += [(x_far.at[0, part, :], x.at[part, :]) for part in blocks]
    pairs += [(top_far.at[part, :], top.at[part, :]) for part in blocks]
    fetches = [pltpu.make_async_copy(*ends, ready.at[k]) for k, ends in enumerate(pairs)]
    for fetch in fetches:
        fetch.start()
    w_fetch = fetches[3 : 3 + pieces]
    x_fetch = fetches[3 + pieces : 3 + pieces + len(blocks)]
    top_fetch = fetches[3 + pieces + len(blocks) :]
    fetches[0].wait()
    fetches[1].wait()
    slot = lax.broadcasted_iota(jnp.int32, (slots, v.shape[1]), 0)
    for m in range(micro_count):
        piece = v[m * slots : (m + 1) * slots, :]
        masked[m * slots : (m + 1) * slots, :] = jnp.where(slot < counts[m], piece, jnp.zeros_like(piece))
    live = jnp.int32(0)
    for m in range(micro_count):
        live += counts[m]
    more[0] = (live > low + packed.shape[0]).astype(jnp.int32)
    gather = one_hot(counts, micro_count, slots, low, packed.shape[0])
    receives = lax.axis_index("section") < lax.axis_size("section") - 1
    scatter[...] = jnp.where(receives, gather.astype(f32), 0.0).astype(bf16)
    values = masked[...]
    for band in range(pieces):
        w_fetch[band].wait()
        for at in range(band * width // pieces, (band + 1) * width // pieces, tile_width):
            cut = pl.ds(at, tile_width)
            back[:, cut] = lax.dot_general(values, w[cut, :], contract_last, preferred_element_type=f32)
    fetches[2].wait()
    for block, at in enumerate(range(0, rows, block_rows)):
        part = slice(at, at + block_rows)
        x_fetch[block].wait()
        squares = jnp.zeros((block_rows, lanes), f32)
        products = jnp.zeros((block_rows, lanes), f32)
        for cut in cuts(width, lanes):
            wide = x[part, cut].astype(f32)
            squares += wide * wide
            products += wide * back[part, cut] * gain[:, cut]
        scale = lax.rsqrt(jnp.sum(squares, axis=1, keepdims=True) / width + eps_norm)
        pull = scale * jnp.sum(products, axis=1, keepdims=True) / width
        waits = jnp.concatenate(
            [
                lax.broadcasted_iota(jnp.int32, (slots, 1), 0) < jnp.where(receives, counts[m], 0)
                for m in range(at // slots, (at + block_rows) // slots)
            ],
            axis=0,
        )
        top_fetch[block].wait()
        for cut in cuts(width, 2 * lanes):
            unit = x[part, cut].astype(f32) * scale
            here = back[part, cut]
            scaled = gain[:, cut]
            product = (unit * here).reshape(block_rows // sublanes, sublanes, 2 * lanes).sum(axis=0)
            if at:
                product += gain_part[:, cut]
            gain_part[:, cut] = product
            normed[part, cut] = (unit * scaled).astype(bf16)
            own = scale * (scaled * here - unit * pull)
            whole = top[part, cut].astype(f32) + own
            sent[part, cut] = whole.astype(bf16)
            addend[part, cut] = jnp.where(waits, own, whole)
    for cut in cuts(width, tile_width):
        packed[:, cut] = lax.dot_general(
            gather, sent[:, cut], contract_rows, preferred_element_type=f32
        ).astype(bf16)
    for cut in cuts(width, tile_width):
        gain_out[:, cut] = jnp.sum(gain_part[:, cut], axis=0, keepdims=True)


def branch_rows(low, room, counts, x, top, v, w, gain):
    rows, width = top.shape
    depth = v.shape[2]
    return pl.pallas_call(
        functools.partial(branch_kernel, low),
        in_specs=[pl.BlockSpec(memory_space=pltpu.HBM)] * 6,
        out_specs=[near] * 3 + [scalar] + [near] * 3,
        out_shape=[
            jax.ShapeDtypeStruct((room, width), bf16),
            jax.ShapeDtypeStruct((rows, width), f32),
            jax.ShapeDtypeStruct((rows, room), bf16),
            pltpu.SMEM((1,), jnp.int32),
            jax.ShapeDtypeStruct((rows, width), bf16),
            jax.ShapeDtypeStruct((rows, depth), bf16),
            jax.ShapeDtypeStruct((1, width), f32),
        ],
        scratch_shapes=[
            pltpu.SMEM(counts.shape, jnp.int32),
            pltpu.VMEM((rows, width), bf16),
            pltpu.VMEM((rows, width), bf16),
            pltpu.VMEM((rows, depth), bf16),
            pltpu.VMEM((width, depth), bf16),
            pltpu.VMEM((1, width), f32),
            pltpu.VMEM((rows, width), f32),
            pltpu.VMEM((sublanes, width), f32),
            pltpu.VMEM((rows, width), bf16),
            pltpu.SemaphoreType.DMA((3 + pieces + 2 * (rows // block_rows),)),
        ],
        compiler_params=roomy,
        cost_estimate=small_cost,
    )(*[far(a) for a in (counts, x, top, v, w, gain)])


def pack_kernel(gather, sent, packed):
    for cut in cuts(sent.shape[1], tile_width):
        packed[:, cut] = lax.dot_general(
            gather[...], sent[:, cut], contract_rows, preferred_element_type=f32
        ).astype(bf16)


def pack(gather, sent):
    return pl.pallas_call(
        pack_kernel,
        in_specs=[near, near],
        out_specs=near,
        out_shape=jax.ShapeDtypeStruct((gather.shape[1], sent.shape[1]), bf16),
        compiler_params=roomy,
        cost_estimate=small_cost,
    )(gather, sent)


def receive_kernel(target, first, factor, scatter, received, addend, more, *refs):
    rows, width = addend.shape
    if first:
        *parts, out_far, more_out, owned_far, out, owned, done = refs
    else:
        previous, out_far, more_out, out, done = refs
    more_out[0] = more[0]
    place = scatter[...]
    writes = []
    if first and parts:
        total_rows(factor, owned, *parts)
        writes.append(pltpu.make_async_copy(owned, owned_far, done.at[width // tile_width]))
        writes[0].start()
    if not first:
        here = (lax.axis_index("section") == target).astype(f32)
        covered = jnp.sum(place.astype(f32), axis=1, keepdims=True) * here > 0.5
    for k, cut in enumerate(cuts(width, tile_width)):
        total = jnp.dot(place, received[:, cut], preferred_element_type=f32) + addend[:, cut]
        if not first:
            total = jnp.where(covered, total, previous[:, cut].astype(f32))
        out[:, cut] = total.astype(bf16)
        write = pltpu.make_async_copy(out.at[:, cut], out_far.at[0, :, cut], done.at[k])
        write.start()
        writes.append(write)
    for write in writes:
        write.wait()


def receive(target, scatter, received, addend, more, previous=None, parts=(), owned=lanes, factor=1.0):
    rows, width = addend.shape
    away = pl.BlockSpec(memory_space=pltpu.HBM)
    first = previous is None
    others = parts if first else [previous]
    outs = [pltpu.HBM((1, rows, width), bf16), pltpu.SMEM(more.shape, more.dtype)]
    scratch = [pltpu.VMEM((rows, width), bf16)]
    if first:
        outs.append(pltpu.HBM((1, owned), f32))
        scratch.append(pltpu.VMEM((1, owned), f32))
    return pl.pallas_call(
        functools.partial(receive_kernel, target, first, factor),
        in_specs=[near, near, near, scalar] + [near] * len(others),
        out_specs=[away, scalar] + [away] * first,
        out_shape=outs,
        scratch_shapes=scratch + [pltpu.SemaphoreType.DMA((width // tile_width + 1,))],
        compiler_params=roomy,
        cost_estimate=small_cost,
    )(scatter, received, addend, more, *others)


def terms_kernel(owned_rows, normed, masked, gain, keep, give, give_low, total):
    width = normed.shape[1]
    values = masked[...]
    gain_rows = width // lanes
    for k in range(gain_rows):
        total[k : k + 1, :] = gain[:, k * lanes : (k + 1) * lanes]
    for at in range(0, width, tile_width):
        total[gain_rows + at : gain_rows + at + tile_width, :] = lax.dot_general(
            normed[:, at : at + tile_width], values, contract_rows, preferred_element_type=f32
        )
    even_core = lax.axis_index("dp") % pair == 0
    padded = keep.shape[1]
    for j in range(keep.shape[0]):
        even = total[2 * j * owned_rows : (2 * j + 1) * owned_rows, :]
        odd = total[(2 * j + 1) * owned_rows : (2 * j + 2) * owned_rows, :]
        if padded > owned_rows:
            blank = jnp.zeros((padded - owned_rows, lanes), f32)
            even = jnp.concatenate([even, blank], axis=0)
            odd = jnp.concatenate([odd, blank], axis=0)
        keep[j] = jnp.where(even_core, even, odd)
        other = jnp.where(even_core, odd, even).astype(bf16)
        give[j] = other[: give.shape[1], :]
        give_low[j] = other[give.shape[1] :, :]


def pair_terms(normed, masked, gain, owned_rows, owners):
    padded = -(-owned_rows // pack_rows) * pack_rows
    cut = padded // 2 // pack_rows * pack_rows
    blocks = owners // pair
    return pl.pallas_call(
        functools.partial(terms_kernel, owned_rows),
        in_specs=[near, near, near],
        out_specs=[near, near, near],
        out_shape=[
            jax.ShapeDtypeStruct((blocks, padded, lanes), f32),
            jax.ShapeDtypeStruct((blocks, cut, lanes), bf16),
            jax.ShapeDtypeStruct((blocks, padded - cut, lanes), bf16),
        ],
        scratch_shapes=[pltpu.VMEM((owners * owned_rows, lanes), f32)],
        compiler_params=roomy,
        cost_estimate=small_cost,
    )(normed, masked, gain)


def merge_kernel(offsets, direct, keep, taken, taken_low, hold, give, *straight):
    chip = lax.axis_index("dp") // pair
    mine, place = chip % 2, chip // 2
    count = keep.shape[0] // 2
    cut = taken.shape[1]

    def total(at, out):
        high = keep[at, :cut, :] + taken[at].astype(f32)
        low = keep[at, cut:, :] + taken_low[at].astype(f32)
        out[:cut, :] = high.astype(out.dtype)
        out[cut:, :] = low.astype(out.dtype)

    for k, offset in enumerate(offsets):
        at = 2 * lax.rem(place + offset, count)
        total(at + mine, hold.at[k])
        total(at + 1 - mine, give.at[k])
    for k, offset in enumerate(direct):
        at = 2 * lax.rem(place + offset, count)
        total(at + mine, straight[2 * k])
        total(at + 1 - mine, straight[2 * k + 1])


def merge_terms(offsets, direct, keep, taken, taken_low):
    block = keep.shape[1:]
    outs = [
        jax.ShapeDtypeStruct((len(offsets),) + block, f32),
        jax.ShapeDtypeStruct((len(offsets),) + block, bf16),
    ] + [jax.ShapeDtypeStruct(block, bf16)] * (2 * len(direct))
    return pl.pallas_call(
        functools.partial(merge_kernel, offsets, direct),
        in_specs=[near, near, near],
        out_specs=[near] * len(outs),
        out_shape=outs,
        compiler_params=roomy,
        cost_estimate=small_cost,
    )(keep, taken, taken_low)


def split_kernel(hold, taken, *parts):
    for k, part in enumerate(parts):
        part[...] = (hold[k] + taken[k].astype(f32)).astype(part.dtype)


def split_terms(part, hold, taken):
    return pl.pallas_call(
        split_kernel,
        in_specs=[near, near],
        out_specs=[near] * len(part),
        out_shape=[jax.ShapeDtypeStruct(hold.shape[1:], bf16 if offset else f32) for offset in part],
        compiler_params=roomy,
        cost_estimate=small_cost,
    )(hold, taken)


def total_rows(factor, out, own, *landed):
    total = own[...]
    for part in landed:
        total += part[...].astype(f32)
    total = total * factor
    for k in range(out.shape[1] // lanes):
        out[:, k * lanes : (k + 1) * lanes] = total[k : k + 1, :]


def plane_parts(owners, keep, *taken):
    quad = 2 * pair
    count = owners // quad
    direct = [count // 2] if count > 2 else []
    offsets = [k for k in range(count) if k not in direct]

    def along(offset, side):
        return [(i, (i + quad * offset) % owners ^ pair * side) for i in range(owners)]

    hold, give, *straight = merge_terms(offsets, direct, keep, *taken)
    across = lax.ppermute(give, "dp", along(0, 1))
    arrived = [
        lax.ppermute(straight[2 * k + side], "dp", along(offset, side))
        for k, offset in enumerate(direct)
        for side in range(2)
    ]
    own, *parts = split_terms(offsets, hold, across)
    for offset, part in zip(offsets[1:], parts):
        arrived.append(lax.ppermute(part, "dp", along(offset, 0)))
    return own, *arrived


def weight_owned(normed, masked, gain, factor):
    owners = lax.axis_size("dp")
    width = normed.shape[1]
    depth = masked.shape[1]
    owned = (width + width * depth) // owners
    if depth != lanes or owned % lanes or owners % (2 * pair):
        weight_term = lax.dot_general(normed, masked, contract_rows, preferred_element_type=f32)
        flat = jnp.concatenate([gain.reshape(-1), weight_term.reshape(-1)]) * factor
        return (), owned, lax.psum_scatter(flat, "dp", scatter_dimension=0, tiled=True)[None, :]
    keep, *give = pair_terms(normed, masked, gain, owned // lanes, owners)
    taken = [lax.ppermute(part, "dp", [(i, i ^ 1) for i in range(owners)]) for part in give]
    return plane_parts(owners, keep, *taken), owned, None


def shards(layer_inputs, top_grad, value_grads, weights, norm_gains, counts):
    rows = layer_inputs.shape[1]
    factor = 1.0 / math.sqrt(rows * lax.axis_size("dp"))
    sections = lax.axis_size("section")
    room = -(-rows * 3 // 4 // pack_rows) * pack_rows
    spare = rows - room
    inputs = (counts, layer_inputs, top_grad, value_grads, weights, norm_gains)
    packed, addend, scatter, more, normed, masked, gain = branch_rows(0, room, *inputs)
    parts, owned_size, owned = weight_owned(normed, masked, gain, factor)
    result = None
    for hop in range(sections - 1):
        target = sections - 2 - hop
        hops = [(target + 1, target), (target, target + 1)]
        before = result
        if hop:
            packed = pack(scatter, before)
        landed = lax.ppermute(packed, "section", hops)
        if hop:
            updated, more = receive(target, scatter, landed, addend, more, before)
        else:
            updated, more, summed = receive(target, scatter, landed, addend, more, None, parts, owned_size, factor)

        def rest(updated):
            packed, addend, scatter, more, *_ = branch_rows(room, spare, *inputs)
            if hop:
                packed = pack(scatter, before)
            landed = lax.ppermute(packed, "section", hops)
            return receive(target, scatter, landed, addend, more, updated[0])[0]

        updated = lax.cond(more.reshape(()) > 0, rest, lambda updated: updated, updated)
        result = updated[0]
    return (result[None], summed if owned is None else owned)


def solution(mesh):
    placed = (
        P("section", "dp", None),
        P("dp", None),
        P("section", "dp", None),
        P("section", None, None),
        P("section", None),
        P("dp"),
    )
    return jax.shard_map(
        shards,
        mesh=mesh,
        in_specs=placed,
        out_specs=(P("section", "dp", None), P("section", "dp")),
        check_vma=False,
    )
```

```python
import functools
import math

import jax
import jax.numpy as jnp
from jax import lax
from jax.experimental import pallas as pl
from jax.experimental.pallas import tpu as pltpu
from jax.sharding import PartitionSpec as P

eps_norm = 1e-05
lanes = 128
sublanes = 8
pack_rows = 16
tile_width = 512
pair = 2
block_rows = 32
f32 = jnp.float32
bf16 = jnp.bfloat16
contract_last = (((1,), (1,)), ((), ()))
contract_rows = (((0,), (0,)), ((), ()))
small_cost = pl.CostEstimate(flops=1 << 20, bytes_accessed=1 << 16, transcendentals=0)
roomy = pltpu.CompilerParams(vmem_limit_bytes=32 << 20)
near = pl.BlockSpec(memory_space=pltpu.VMEM)
scalar = pl.BlockSpec(memory_space=pltpu.SMEM)


def far(array):
    return pltpu.with_memory_space_constraint(array, pltpu.HBM)


def cuts(width, step):
    return [pl.ds(at, step) for at in range(0, width, step)]


def one_hot(counts, micro_count, slots, low, size):
    slot = lax.broadcasted_iota(jnp.int32, (slots, size), 0)
    column = lax.broadcasted_iota(jnp.int32, (slots, size), 1) + low
    start = jnp.int32(0)
    pieces = []
    for m in range(micro_count):
        hit = (slot < counts[m]) & (slot + start == column)
        pieces.append(jnp.where(hit, 1.0, 0.0))
        start = start + counts[m]
    return jnp.concatenate(pieces, axis=0).astype(bf16)


def branch_kernel(
    low, counts_far, x_far, top_far, v_far, w_far, gain_far,
    packed, addend, scatter, more, normed, masked, gain_out,
    counts, x, top, v, w, gain, back, gain_part, sent, ready,
):
    rows, width = addend.shape
    micro_count = counts.shape[0]
    slots = rows // micro_count
    fetches = [
        pltpu.make_async_copy(v_far.at[0], v, ready.at[0]),
        pltpu.make_async_copy(counts_far, counts, ready.at[1]),
        pltpu.make_async_copy(w_far.at[0], w, ready.at[2]),
        pltpu.make_async_copy(x_far.at[0], x, ready.at[3]),
        pltpu.make_async_copy(gain_far, gain, ready.at[4]),
        pltpu.make_async_copy(top_far, top, ready.at[5]),
    ]
    for fetch in fetches:
        fetch.start()
    fetches[0].wait()
    fetches[1].wait()
    slot = lax.broadcasted_iota(jnp.int32, (slots, v.shape[1]), 0)
    for m in range(micro_count):
        piece = v[m * slots : (m + 1) * slots, :]
        masked[m * slots : (m + 1) * slots, :] = jnp.where(slot < counts[m], piece, jnp.zeros_like(piece))
    live = jnp.int32(0)
    for m in range(micro_count):
        live += counts[m]
    more[0] = (live > low + packed.shape[0]).astype(jnp.int32)
    gather = one_hot(counts, micro_count, slots, low, packed.shape[0])
    receives = lax.axis_index("section") < lax.axis_size("section") - 1
    scatter[...] = jnp.where(receives, gather.astype(f32), 0.0).astype(bf16)
    gather = jnp.transpose(gather.astype(f32)).astype(bf16)
    values = masked[...]
    fetches[2].wait()
    for cut in cuts(width, tile_width):
        back[:, cut] = lax.dot_general(values, w[cut, :], contract_last, preferred_element_type=f32)
    fetches[3].wait()
    fetches[4].wait()
    blocks = [slice(at, at + block_rows) for at in range(0, rows, block_rows)]
    squares, products = [], []
    for part in blocks:
        square = jnp.zeros((block_rows, lanes), f32)
        product = jnp.zeros((block_rows, lanes), f32)
        for cut in cuts(width, lanes):
            wide = x[part, cut].astype(f32)
            square += wide * wide
            product += wide * back[part, cut] * gain[:, cut]
        squares.append(square)
        products.append(product)
    scales = lax.rsqrt(jnp.sum(jnp.concatenate(squares, axis=0), axis=1, keepdims=True) / width + eps_norm)
    pulls = scales * jnp.sum(jnp.concatenate(products, axis=0), axis=1, keepdims=True) / width
    waits = jnp.concatenate(
        [
            lax.broadcasted_iota(jnp.int32, (slots, 1), 0) < jnp.where(receives, counts[m], 0)
            for m in range(micro_count)
        ],
        axis=0,
    )
    fetches[5].wait()
    for part in blocks:
        scale, pull, wait = scales[part], pulls[part], waits[part]
        for cut in cuts(width, 2 * lanes):
            unit = x[part, cut].astype(f32) * scale
            here = back[part, cut]
            scaled = gain[:, cut]
            product = (unit * here).reshape(block_rows // sublanes, sublanes, 2 * lanes).sum(axis=0)
            if part.start:
                product += gain_part[:, cut]
            gain_part[:, cut] = product
            normed[part, cut] = (unit * scaled).astype(bf16)
            own = scale * (scaled * here - unit * pull)
            whole = top[part, cut].astype(f32) + own
            sent[part, cut] = whole.astype(bf16)
            addend[part, cut] = jnp.where(wait, own, whole)
    for cut in cuts(width, tile_width):
        packed[:, cut] = jnp.dot(gather, sent[:, cut], preferred_element_type=f32).astype(bf16)
    for cut in cuts(width, tile_width):
        gain_out[:, cut] = jnp.sum(gain_part[:, cut], axis=0, keepdims=True)


def branch_rows(low, room, counts, x, top, v, w, gain):
    rows, width = top.shape
    depth = v.shape[2]
    return pl.pallas_call(
        functools.partial(branch_kernel, low),
        in_specs=[pl.BlockSpec(memory_space=pltpu.HBM)] * 6,
        out_specs=[near] * 3 + [scalar] + [near] * 3,
        out_shape=[
            jax.ShapeDtypeStruct((room, width), bf16),
            jax.ShapeDtypeStruct((rows, width), f32),
            jax.ShapeDtypeStruct((rows, room), bf16),
            pltpu.SMEM((1,), jnp.int32),
            jax.ShapeDtypeStruct((rows, width), bf16),
            jax.ShapeDtypeStruct((rows, depth), bf16),
            jax.ShapeDtypeStruct((1, width), f32),
        ],
        scratch_shapes=[
            pltpu.SMEM(counts.shape, jnp.int32),
            pltpu.VMEM((rows, width), bf16),
            pltpu.VMEM((rows, width), bf16),
            pltpu.VMEM((rows, depth), bf16),
            pltpu.VMEM((width, depth), bf16),
            pltpu.VMEM((1, width), f32),
            pltpu.VMEM((rows, width), f32),
            pltpu.VMEM((sublanes, width), f32),
            pltpu.VMEM((rows, width), bf16),
            pltpu.SemaphoreType.DMA((6,)),
        ],
        compiler_params=roomy,
        cost_estimate=small_cost,
    )(*[far(a) for a in (counts, x, top, v, w, gain)])


def pack_kernel(gather, sent, packed):
    for cut in cuts(sent.shape[1], tile_width):
        packed[:, cut] = lax.dot_general(
            gather[...], sent[:, cut], contract_rows, preferred_element_type=f32
        ).astype(bf16)


def pack(gather, sent):
    return pl.pallas_call(
        pack_kernel,
        in_specs=[near, near],
        out_specs=near,
        out_shape=jax.ShapeDtypeStruct((gather.shape[1], sent.shape[1]), bf16),
        compiler_params=roomy,
        cost_estimate=small_cost,
    )(gather, sent)


def receive_kernel(target, first, factor, scatter, received, addend, more, *refs):
    rows, width = addend.shape
    if first:
        *parts, out_far, more_out, owned_far, out, owned, done = refs
    else:
        previous, out_far, more_out, out, done = refs
    more_out[0] = more[0]
    place = scatter[...]
    writes = []
    if first and parts:
        total_rows(factor, owned, *parts)
        writes.append(pltpu.make_async_copy(owned, owned_far, done.at[width // tile_width]))
        writes[0].start()
    if not first:
        here = (lax.axis_index("section") == target).astype(f32)
        covered = jnp.sum(place.astype(f32), axis=1, keepdims=True) * here > 0.5
    for k, cut in enumerate(cuts(width, tile_width)):
        total = jnp.dot(place, received[:, cut], preferred_element_type=f32) + addend[:, cut]
        if not first:
            total = jnp.where(covered, total, previous[:, cut].astype(f32))
        out[:, cut] = total.astype(bf16)
        write = pltpu.make_async_copy(out.at[:, cut], out_far.at[0, :, cut], done.at[k])
        write.start()
        writes.append(write)
    for write in writes:
        write.wait()


def receive(target, scatter, received, addend, more, previous=None, parts=(), owned=lanes, factor=1.0):
    rows, width = addend.shape
    away = pl.BlockSpec(memory_space=pltpu.HBM)
    first = previous is None
    others = parts if first else [previous]
    outs = [pltpu.HBM((1, rows, width), bf16), pltpu.SMEM(more.shape, more.dtype)]
    scratch = [pltpu.VMEM((rows, width), bf16)]
    if first:
        outs.append(pltpu.HBM((1, owned), f32))
        scratch.append(pltpu.VMEM((1, owned), f32))
    return pl.pallas_call(
        functools.partial(receive_kernel, target, first, factor),
        in_specs=[near, near, near, scalar] + [near] * len(others),
        out_specs=[away, scalar] + [away] * first,
        out_shape=outs,
        scratch_shapes=scratch + [pltpu.SemaphoreType.DMA((width // tile_width + 1,))],
        compiler_params=roomy,
        cost_estimate=small_cost,
    )(scatter, received, addend, more, *others)


def terms_kernel(owned_rows, normed, masked, gain, keep, give, give_low, total):
    width = normed.shape[1]
    values = masked[...]
    gain_rows = width // lanes
    for k in range(gain_rows):
        total[k : k + 1, :] = gain[:, k * lanes : (k + 1) * lanes]
    for at in range(0, width, tile_width):
        total[gain_rows + at : gain_rows + at + tile_width, :] = lax.dot_general(
            normed[:, at : at + tile_width], values, contract_rows, preferred_element_type=f32
        )
    even_core = lax.axis_index("dp") % pair == 0
    padded = keep.shape[1]
    for j in range(keep.shape[0]):
        even = total[2 * j * owned_rows : (2 * j + 1) * owned_rows, :]
        odd = total[(2 * j + 1) * owned_rows : (2 * j + 2) * owned_rows, :]
        if padded > owned_rows:
            blank = jnp.zeros((padded - owned_rows, lanes), f32)
            even = jnp.concatenate([even, blank], axis=0)
            odd = jnp.concatenate([odd, blank], axis=0)
        keep[j] = jnp.where(even_core, even, odd)
        other = jnp.where(even_core, odd, even).astype(bf16)
        give[j] = other[: give.shape[1], :]
        give_low[j] = other[give.shape[1] :, :]


def pair_terms(normed, masked, gain, owned_rows, owners):
    padded = -(-owned_rows // pack_rows) * pack_rows
    cut = padded // 2 // pack_rows * pack_rows
    blocks = owners // pair
    return pl.pallas_call(
        functools.partial(terms_kernel, owned_rows),
        in_specs=[near, near, near],
        out_specs=[near, near, near],
        out_shape=[
            jax.ShapeDtypeStruct((blocks, padded, lanes), f32),
            jax.ShapeDtypeStruct((blocks, cut, lanes), bf16),
            jax.ShapeDtypeStruct((blocks, padded - cut, lanes), bf16),
        ],
        scratch_shapes=[pltpu.VMEM((owners * owned_rows, lanes), f32)],
        compiler_params=roomy,
        cost_estimate=small_cost,
    )(normed, masked, gain)


def merge_kernel(offsets, direct, keep, taken, taken_low, hold, give, *straight):
    chip = lax.axis_index("dp") // pair
    mine, place = chip % 2, chip // 2
    count = keep.shape[0] // 2
    cut = taken.shape[1]

    def total(at, out):
        high = keep[at, :cut, :] + taken[at].astype(f32)
        low = keep[at, cut:, :] + taken_low[at].astype(f32)
        out[:cut, :] = high.astype(out.dtype)
        out[cut:, :] = low.astype(out.dtype)

    for k, offset in enumerate(offsets):
        at = 2 * lax.rem(place + offset, count)
        total(at + mine, hold.at[k])
        total(at + 1 - mine, give.at[k])
    for k, offset in enumerate(direct):
        at = 2 * lax.rem(place + offset, count)
        total(at + mine, straight[2 * k])
        total(at + 1 - mine, straight[2 * k + 1])


def merge_terms(offsets, direct, keep, taken, taken_low):
    block = keep.shape[1:]
    outs = [
        jax.ShapeDtypeStruct((len(offsets),) + block, f32),
        jax.ShapeDtypeStruct((len(offsets),) + block, bf16),
    ] + [jax.ShapeDtypeStruct(block, bf16)] * (2 * len(direct))
    return pl.pallas_call(
        functools.partial(merge_kernel, offsets, direct),
        in_specs=[near, near, near],
        out_specs=[near] * len(outs),
        out_shape=outs,
        compiler_params=roomy,
        cost_estimate=small_cost,
    )(keep, taken, taken_low)


def split_kernel(hold, taken, *parts):
    for k, part in enumerate(parts):
        part[...] = (hold[k] + taken[k].astype(f32)).astype(part.dtype)


def split_terms(part, hold, taken):
    return pl.pallas_call(
        split_kernel,
        in_specs=[near, near],
        out_specs=[near] * len(part),
        out_shape=[jax.ShapeDtypeStruct(hold.shape[1:], bf16 if offset else f32) for offset in part],
        compiler_params=roomy,
        cost_estimate=small_cost,
    )(hold, taken)


def total_rows(factor, out, own, *landed):
    total = own[...]
    for part in landed:
        total += part[...].astype(f32)
    total = total * factor
    for k in range(out.shape[1] // lanes):
        out[:, k * lanes : (k + 1) * lanes] = total[k : k + 1, :]


def plane_parts(owners, keep, *taken):
    quad = 2 * pair
    count = owners // quad
    direct = [count // 2] if count > 2 else []
    offsets = [k for k in range(count) if k not in direct]

    def along(offset, side):
        return [(i, (i + quad * offset) % owners ^ pair * side) for i in range(owners)]

    hold, give, *straight = merge_terms(offsets, direct, keep, *taken)
    across = lax.ppermute(give, "dp", along(0, 1))
    arrived = [
        lax.ppermute(straight[2 * k + side], "dp", along(offset, side))
        for k, offset in enumerate(direct)
        for side in range(2)
    ]
    own, *parts = split_terms(offsets, hold, across)
    for offset, part in zip(offsets[1:], parts):
        arrived.append(lax.ppermute(part, "dp", along(offset, 0)))
    return own, *arrived


def weight_owned(normed, masked, gain, factor):
    owners = lax.axis_size("dp")
    width = normed.shape[1]
    depth = masked.shape[1]
    owned = (width + width * depth) // owners
    if depth != lanes or owned % lanes or owners % (2 * pair):
        weight_term = lax.dot_general(normed, masked, contract_rows, preferred_element_type=f32)
        flat = jnp.concatenate([gain.reshape(-1), weight_term.reshape(-1)]) * factor
        return (), owned, lax.psum_scatter(flat, "dp", scatter_dimension=0, tiled=True)[None, :]
    keep, *give = pair_terms(normed, masked, gain, owned // lanes, owners)
    taken = [lax.ppermute(part, "dp", [(i, i ^ 1) for i in range(owners)]) for part in give]
    return plane_parts(owners, keep, *taken), owned, None


def shards(layer_inputs, top_grad, value_grads, weights, norm_gains, counts):
    rows = layer_inputs.shape[1]
    factor = 1.0 / math.sqrt(rows * lax.axis_size("dp"))
    sections = lax.axis_size("section")
    room = -(-rows * 3 // 4 // pack_rows) * pack_rows
    spare = rows - room
    inputs = (counts, layer_inputs, top_grad, value_grads, weights, norm_gains)
    packed, addend, scatter, more, normed, masked, gain = branch_rows(0, room, *inputs)
    parts, owned_size, owned = weight_owned(normed, masked, gain, factor)
    result = None
    for hop in range(sections - 1):
        target = sections - 2 - hop
        hops = [(target + 1, target), (target, target + 1)]
        before = result
        if hop:
            packed = pack(scatter, before)
        landed = lax.ppermute(packed, "section", hops)
        if hop:
            updated, more = receive(target, scatter, landed, addend, more, before)
        else:
            updated, more, summed = receive(target, scatter, landed, addend, more, None, parts, owned_size, factor)

        def rest(updated):
            packed, addend, scatter, more, *_ = branch_rows(room, spare, *inputs)
            if hop:
                packed = pack(scatter, before)
            landed = lax.ppermute(packed, "section", hops)
            return receive(target, scatter, landed, addend, more, updated[0])[0]

        updated = lax.cond(more.reshape(()) > 0, rest, lambda updated: updated, updated)
        result = updated[0]
    return (result[None], summed if owned is None else owned)


def solution(mesh):
    placed = (
        P("section", "dp", None),
        P("dp", None),
        P("section", "dp", None),
        P("section", None, None),
        P("section", None),
        P("dp"),
    )
    return jax.shard_map(
        shards,
        mesh=mesh,
        in_specs=placed,
        out_specs=(P("section", "dp", None), P("section", "dp")),
        check_vma=False,
    )
```

```python
import functools
import math

import jax
import jax.numpy as jnp
from jax import lax
from jax.experimental import pallas as pl
from jax.experimental.pallas import tpu as pltpu
from jax.sharding import PartitionSpec as P

eps_norm = 1e-05
lanes = 128
sublanes = 8
pack_rows = 16
tile_width = 512
pair = 2
block_rows = 32
band_width = 256
f32 = jnp.float32
bf16 = jnp.bfloat16
contract_last = (((1,), (1,)), ((), ()))
contract_rows = (((0,), (0,)), ((), ()))
small_cost = pl.CostEstimate(flops=1 << 20, bytes_accessed=1 << 16, transcendentals=0)
roomy = pltpu.CompilerParams(vmem_limit_bytes=32 << 20)
near = pl.BlockSpec(memory_space=pltpu.VMEM)
scalar = pl.BlockSpec(memory_space=pltpu.SMEM)


def far(array):
    return pltpu.with_memory_space_constraint(array, pltpu.HBM)


def cuts(width, step):
    return [pl.ds(at, step) for at in range(0, width, step)]


def one_hot(counts, micro_count, slots, low, size):
    slot = lax.broadcasted_iota(jnp.int32, (slots, size), 0)
    column = lax.broadcasted_iota(jnp.int32, (slots, size), 1) + low
    start = jnp.int32(0)
    pieces = []
    for m in range(micro_count):
        hit = (slot < counts[m]) & (slot + start == column)
        pieces.append(jnp.where(hit, 1.0, 0.0))
        start = start + counts[m]
    return jnp.concatenate(pieces, axis=0).astype(bf16)


def branch_kernel(
    low, counts_far, x_far, top_far, v_far, w_far, gain_far,
    packed, addend, scatter, more, normed, masked, gain_out,
    counts, x, top, v, w, gain, back, sent, ready,
):
    rows, width = addend.shape
    micro_count = counts.shape[0]
    slots = rows // micro_count
    fetches = [
        pltpu.make_async_copy(v_far.at[0], v, ready.at[0]),
        pltpu.make_async_copy(counts_far, counts, ready.at[1]),
        pltpu.make_async_copy(w_far.at[0], w, ready.at[2]),
        pltpu.make_async_copy(x_far.at[0], x, ready.at[3]),
        pltpu.make_async_copy(gain_far, gain, ready.at[4]),
        pltpu.make_async_copy(top_far, top, ready.at[5]),
    ]
    for fetch in fetches:
        fetch.start()
    fetches[0].wait()
    fetches[1].wait()
    slot = lax.broadcasted_iota(jnp.int32, (slots, v.shape[1]), 0)
    for m in range(micro_count):
        piece = v[m * slots : (m + 1) * slots, :]
        masked[m * slots : (m + 1) * slots, :] = jnp.where(slot < counts[m], piece, jnp.zeros_like(piece))
    live = jnp.int32(0)
    for m in range(micro_count):
        live += counts[m]
    more[0] = (live > low + packed.shape[0]).astype(jnp.int32)
    gather = one_hot(counts, micro_count, slots, low, packed.shape[0])
    receives = lax.axis_index("section") < lax.axis_size("section") - 1
    scatter[...] = jnp.where(receives, gather.astype(f32), 0.0).astype(bf16)
    gather = jnp.transpose(gather.astype(f32)).astype(bf16)
    values = masked[...]
    for fetch in fetches[2:5]:
        fetch.wait()
    blocks = [slice(at, at + block_rows) for at in range(0, rows, block_rows)]
    squares = [jnp.zeros((block_rows, lanes), f32) for _ in blocks]
    products = [jnp.zeros((block_rows, lanes), f32) for _ in blocks]
    for tile in range(0, width, tile_width):
        here = lax.dot_general(
            values, w[tile : tile + tile_width, :], contract_last, preferred_element_type=f32
        )
        back[:, tile : tile + tile_width] = here
        for k, part in enumerate(blocks):
            for at in range(0, tile_width, lanes):
                cut = pl.ds(tile + at, lanes)
                wide = x[part, cut].astype(f32)
                squares[k] += wide * wide
                products[k] += wide * here[part, at : at + lanes] * gain[:, cut]
    scales = lax.rsqrt(jnp.sum(jnp.concatenate(squares, axis=0), axis=1, keepdims=True) / width + eps_norm)
    pulls = scales * jnp.sum(jnp.concatenate(products, axis=0), axis=1, keepdims=True) / width
    waits = jnp.concatenate(
        [
            lax.broadcasted_iota(jnp.int32, (slots, 1), 0) < jnp.where(receives, counts[m], 0)
            for m in range(micro_count)
        ],
        axis=0,
    )
    spread = (rows, band_width)
    scales = jnp.broadcast_to(scales, spread)
    pulls = jnp.broadcast_to(pulls, spread)
    waits = jnp.broadcast_to(waits, spread)
    fetches[5].wait()
    for cut in cuts(width, band_width):
        scaled = gain[:, cut]
        partial = jnp.zeros((sublanes, band_width), f32)
        for part in blocks:
            unit = x[part, cut].astype(f32) * scales[part]
            here = back[part, cut]
            partial += (unit * here).reshape(block_rows // sublanes, sublanes, band_width).sum(axis=0)
            normed[part, cut] = (unit * scaled).astype(bf16)
            own = scales[part] * (scaled * here - unit * pulls[part])
            whole = top[part, cut].astype(f32) + own
            sent[part, cut] = whole.astype(bf16)
            addend[part, cut] = jnp.where(waits[part], own, whole)
        gain_out[:, cut] = jnp.sum(partial, axis=0, keepdims=True)
        packed[:, cut] = jnp.dot(gather, sent[:, cut], preferred_element_type=f32).astype(bf16)


def branch_rows(low, room, counts, x, top, v, w, gain):
    rows, width = top.shape
    depth = v.shape[2]
    return pl.pallas_call(
        functools.partial(branch_kernel, low),
        in_specs=[pl.BlockSpec(memory_space=pltpu.HBM)] * 6,
        out_specs=[near] * 3 + [scalar] + [near] * 3,
        out_shape=[
            jax.ShapeDtypeStruct((room, width), bf16),
            jax.ShapeDtypeStruct((rows, width), f32),
            jax.ShapeDtypeStruct((rows, room), bf16),
            pltpu.SMEM((1,), jnp.int32),
            jax.ShapeDtypeStruct((rows, width), bf16),
            jax.ShapeDtypeStruct((rows, depth), bf16),
            jax.ShapeDtypeStruct((1, width), f32),
        ],
        scratch_shapes=[
            pltpu.SMEM(counts.shape, jnp.int32),
            pltpu.VMEM((rows, width), bf16),
            pltpu.VMEM((rows, width), bf16),
            pltpu.VMEM((rows, depth), bf16),
            pltpu.VMEM((width, depth), bf16),
            pltpu.VMEM((1, width), f32),
            pltpu.VMEM((rows, width), f32),
            pltpu.VMEM((rows, width), bf16),
            pltpu.SemaphoreType.DMA((6,)),
        ],
        compiler_params=roomy,
        cost_estimate=small_cost,
    )(*[far(a) for a in (counts, x, top, v, w, gain)])


def pack_kernel(gather, sent, packed):
    for cut in cuts(sent.shape[1], tile_width):
        packed[:, cut] = lax.dot_general(
            gather[...], sent[:, cut], contract_rows, preferred_element_type=f32
        ).astype(bf16)


def pack(gather, sent):
    return pl.pallas_call(
        pack_kernel,
        in_specs=[near, near],
        out_specs=near,
        out_shape=jax.ShapeDtypeStruct((gather.shape[1], sent.shape[1]), bf16),
        compiler_params=roomy,
        cost_estimate=small_cost,
    )(gather, sent)


def receive_kernel(target, first, factor, scatter, received, addend, more, *refs):
    rows, width = addend.shape
    if first:
        *parts, out_far, more_out, owned_far, out, owned, done = refs
    else:
        previous, out_far, more_out, out, done = refs
    more_out[0] = more[0]
    place = scatter[...]
    writes = []
    if first and parts:
        total_rows(factor, owned, *parts)
        writes.append(pltpu.make_async_copy(owned, owned_far, done.at[width // tile_width]))
        writes[0].start()
    if not first:
        here = (lax.axis_index("section") == target).astype(f32)
        covered = jnp.sum(place.astype(f32), axis=1, keepdims=True) * here > 0.5
    for k, cut in enumerate(cuts(width, tile_width)):
        total = jnp.dot(place, received[:, cut], preferred_element_type=f32) + addend[:, cut]
        if not first:
            total = jnp.where(covered, total, previous[:, cut].astype(f32))
        out[:, cut] = total.astype(bf16)
        write = pltpu.make_async_copy(out.at[:, cut], out_far.at[0, :, cut], done.at[k])
        write.start()
        writes.append(write)
    for write in writes:
        write.wait()


def receive(target, scatter, received, addend, more, previous=None, parts=(), owned=lanes, factor=1.0):
    rows, width = addend.shape
    away = pl.BlockSpec(memory_space=pltpu.HBM)
    first = previous is None
    others = parts if first else [previous]
    outs = [pltpu.HBM((1, rows, width), bf16), pltpu.SMEM(more.shape, more.dtype)]
    scratch = [pltpu.VMEM((rows, width), bf16)]
    if first:
        outs.append(pltpu.HBM((1, owned), f32))
        scratch.append(pltpu.VMEM((1, owned), f32))
    return pl.pallas_call(
        functools.partial(receive_kernel, target, first, factor),
        in_specs=[near, near, near, scalar] + [near] * len(others),
        out_specs=[away, scalar] + [away] * first,
        out_shape=outs,
        scratch_shapes=scratch + [pltpu.SemaphoreType.DMA((width // tile_width + 1,))],
        compiler_params=roomy,
        cost_estimate=small_cost,
    )(scatter, received, addend, more, *others)


def terms_kernel(owned_rows, normed, masked, gain, keep, give, give_low, total):
    width = normed.shape[1]
    values = masked[...]
    gain_rows = width // lanes
    for k in range(gain_rows):
        total[k : k + 1, :] = gain[:, k * lanes : (k + 1) * lanes]
    for at in range(0, width, tile_width):
        total[gain_rows + at : gain_rows + at + tile_width, :] = lax.dot_general(
            normed[:, at : at + tile_width], values, contract_rows, preferred_element_type=f32
        )
    even_core = lax.axis_index("dp") % pair == 0
    padded = keep.shape[1]
    for j in range(keep.shape[0]):
        even = total[2 * j * owned_rows : (2 * j + 1) * owned_rows, :]
        odd = total[(2 * j + 1) * owned_rows : (2 * j + 2) * owned_rows, :]
        if padded > owned_rows:
            blank = jnp.zeros((padded - owned_rows, lanes), f32)
            even = jnp.concatenate([even, blank], axis=0)
            odd = jnp.concatenate([odd, blank], axis=0)
        keep[j] = jnp.where(even_core, even, odd)
        other = jnp.where(even_core, odd, even).astype(bf16)
        give[j] = other[: give.shape[1], :]
        give_low[j] = other[give.shape[1] :, :]


def pair_terms(normed, masked, gain, owned_rows, owners):
    padded = -(-owned_rows // pack_rows) * pack_rows
    cut = padded // 2 // pack_rows * pack_rows
    blocks = owners // pair
    return pl.pallas_call(
        functools.partial(terms_kernel, owned_rows),
        in_specs=[near, near, near],
        out_specs=[near, near, near],
        out_shape=[
            jax.ShapeDtypeStruct((blocks, padded, lanes), f32),
            jax.ShapeDtypeStruct((blocks, cut, lanes), bf16),
            jax.ShapeDtypeStruct((blocks, padded - cut, lanes), bf16),
        ],
        scratch_shapes=[pltpu.VMEM((owners * owned_rows, lanes), f32)],
        compiler_params=roomy,
        cost_estimate=small_cost,
    )(normed, masked, gain)


def merge_kernel(offsets, direct, keep, taken, taken_low, hold, give, *straight):
    chip = lax.axis_index("dp") // pair
    mine, place = chip % 2, chip // 2
    count = keep.shape[0] // 2
    cut = taken.shape[1]

    def total(at, out):
        high = keep[at, :cut, :] + taken[at].astype(f32)
        low = keep[at, cut:, :] + taken_low[at].astype(f32)
        out[:cut, :] = high.astype(out.dtype)
        out[cut:, :] = low.astype(out.dtype)

    for k, offset in enumerate(offsets):
        at = 2 * lax.rem(place + offset, count)
        total(at + mine, hold.at[k])
        total(at + 1 - mine, give.at[k])
    for k, offset in enumerate(direct):
        at = 2 * lax.rem(place + offset, count)
        total(at + mine, straight[2 * k])
        total(at + 1 - mine, straight[2 * k + 1])


def merge_terms(offsets, direct, keep, taken, taken_low):
    block = keep.shape[1:]
    outs = [
        jax.ShapeDtypeStruct((len(offsets),) + block, f32),
        jax.ShapeDtypeStruct((len(offsets),) + block, bf16),
    ] + [jax.ShapeDtypeStruct(block, bf16)] * (2 * len(direct))
    return pl.pallas_call(
        functools.partial(merge_kernel, offsets, direct),
        in_specs=[near, near, near],
        out_specs=[near] * len(outs),
        out_shape=outs,
        compiler_params=roomy,
        cost_estimate=small_cost,
    )(keep, taken, taken_low)


def split_kernel(hold, taken, *parts):
    for k, part in enumerate(parts):
        part[...] = (hold[k] + taken[k].astype(f32)).astype(part.dtype)


def split_terms(part, hold, taken):
    return pl.pallas_call(
        split_kernel,
        in_specs=[near, near],
        out_specs=[near] * len(part),
        out_shape=[jax.ShapeDtypeStruct(hold.shape[1:], bf16 if offset else f32) for offset in part],
        compiler_params=roomy,
        cost_estimate=small_cost,
    )(hold, taken)


def total_rows(factor, out, own, *landed):
    total = own[...]
    for part in landed:
        total += part[...].astype(f32)
    total = total * factor
    for k in range(out.shape[1] // lanes):
        out[:, k * lanes : (k + 1) * lanes] = total[k : k + 1, :]


def plane_parts(owners, keep, *taken):
    quad = 2 * pair
    count = owners // quad
    direct = [count // 2] if count > 2 else []
    offsets = [k for k in range(count) if k not in direct]

    def along(offset, side):
        return [(i, (i + quad * offset) % owners ^ pair * side) for i in range(owners)]

    hold, give, *straight = merge_terms(offsets, direct, keep, *taken)
    across = lax.ppermute(give, "dp", along(0, 1))
    arrived = [
        lax.ppermute(straight[2 * k + side], "dp", along(offset, side))
        for k, offset in enumerate(direct)
        for side in range(2)
    ]
    own, *parts = split_terms(offsets, hold, across)
    for offset, part in zip(offsets[1:], parts):
        arrived.append(lax.ppermute(part, "dp", along(offset, 0)))
    return own, *arrived


def weight_owned(normed, masked, gain, factor):
    owners = lax.axis_size("dp")
    width = normed.shape[1]
    depth = masked.shape[1]
    owned = (width + width * depth) // owners
    if depth != lanes or owned % lanes or owners % (2 * pair):
        weight_term = lax.dot_general(normed, masked, contract_rows, preferred_element_type=f32)
        flat = jnp.concatenate([gain.reshape(-1), weight_term.reshape(-1)]) * factor
        return (), owned, lax.psum_scatter(flat, "dp", scatter_dimension=0, tiled=True)[None, :]
    keep, *give = pair_terms(normed, masked, gain, owned // lanes, owners)
    taken = [lax.ppermute(part, "dp", [(i, i ^ 1) for i in range(owners)]) for part in give]
    return plane_parts(owners, keep, *taken), owned, None


def shards(layer_inputs, top_grad, value_grads, weights, norm_gains, counts):
    rows = layer_inputs.shape[1]
    factor = 1.0 / math.sqrt(rows * lax.axis_size("dp"))
    sections = lax.axis_size("section")
    room = -(-rows * 3 // 4 // pack_rows) * pack_rows
    spare = rows - room
    inputs = (counts, layer_inputs, top_grad, value_grads, weights, norm_gains)
    packed, addend, scatter, more, normed, masked, gain = branch_rows(0, room, *inputs)
    parts, owned_size, owned = weight_owned(normed, masked, gain, factor)
    result = None
    for hop in range(sections - 1):
        target = sections - 2 - hop
        hops = [(target + 1, target), (target, target + 1)]
        before = result
        if hop:
            packed = pack(scatter, before)
        landed = lax.ppermute(packed, "section", hops)
        if hop:
            updated, more = receive(target, scatter, landed, addend, more, before)
        else:
            updated, more, summed = receive(target, scatter, landed, addend, more, None, parts, owned_size, factor)

        def rest(updated):
            packed, addend, scatter, more, *_ = branch_rows(room, spare, *inputs)
            if hop:
                packed = pack(scatter, before)
            landed = lax.ppermute(packed, "section", hops)
            return receive(target, scatter, landed, addend, more, updated[0])[0]

        updated = lax.cond(more.reshape(()) > 0, rest, lambda updated: updated, updated)
        result = updated[0]
    return (result[None], summed if owned is None else owned)


def solution(mesh):
    placed = (
        P("section", "dp", None),
        P("dp", None),
        P("section", "dp", None),
        P("section", None, None),
        P("section", None),
        P("dp"),
    )
    return jax.shard_map(
        shards,
        mesh=mesh,
        in_specs=placed,
        out_specs=(P("section", "dp", None), P("section", "dp")),
        check_vma=False,
    )
```

```python
import functools
import math

import jax
import jax.numpy as jnp
from jax import lax
from jax.experimental import pallas as pl
from jax.experimental.pallas import tpu as pltpu
from jax.sharding import PartitionSpec as P

eps_norm = 1e-05
lanes = 128
sublanes = 8
pack_rows = 16
tile_width = 512
pair = 2
block_rows = 32
band_width = 256
f32 = jnp.float32
bf16 = jnp.bfloat16
contract_last = (((1,), (1,)), ((), ()))
contract_rows = (((0,), (0,)), ((), ()))
small_cost = pl.CostEstimate(flops=1 << 20, bytes_accessed=1 << 16, transcendentals=0)
roomy = pltpu.CompilerParams(vmem_limit_bytes=32 << 20)
near = pl.BlockSpec(memory_space=pltpu.VMEM)
scalar = pl.BlockSpec(memory_space=pltpu.SMEM)


def far(array):
    return pltpu.with_memory_space_constraint(array, pltpu.HBM)


def cuts(width, step):
    return [pl.ds(at, step) for at in range(0, width, step)]


def one_hot(counts, micro_count, slots, low, size):
    slot = lax.broadcasted_iota(jnp.int32, (slots, size), 0)
    column = lax.broadcasted_iota(jnp.int32, (slots, size), 1) + low
    start = jnp.int32(0)
    pieces = []
    for m in range(micro_count):
        hit = (slot < counts[m]) & (slot + start == column)
        pieces.append(jnp.where(hit, 1.0, 0.0))
        start = start + counts[m]
    return jnp.concatenate(pieces, axis=0).astype(bf16)


def branch_kernel(
    low, counts_far, x_far, top_far, v_far, w_far, gain_far,
    packed, addend, scatter, more, normed, masked, gain_out,
    counts, x, top, v, w, gain, back, sent, ready,
):
    rows, width = addend.shape
    micro_count = counts.shape[0]
    slots = rows // micro_count
    fetches = [
        pltpu.make_async_copy(v_far.at[0], v, ready.at[0]),
        pltpu.make_async_copy(counts_far, counts, ready.at[1]),
        pltpu.make_async_copy(w_far.at[0], w, ready.at[2]),
        pltpu.make_async_copy(x_far.at[0], x, ready.at[3]),
        pltpu.make_async_copy(gain_far, gain, ready.at[4]),
        pltpu.make_async_copy(top_far, top, ready.at[5]),
    ]
    for fetch in fetches[:5]:
        fetch.start()
    fetches[0].wait()
    fetches[1].wait()
    slot = lax.broadcasted_iota(jnp.int32, (slots, v.shape[1]), 0)
    for m in range(micro_count):
        piece = v[m * slots : (m + 1) * slots, :]
        masked[m * slots : (m + 1) * slots, :] = jnp.where(slot < counts[m], piece, jnp.zeros_like(piece))
    live = jnp.int32(0)
    for m in range(micro_count):
        live += counts[m]
    more[0] = (live > low + packed.shape[0]).astype(jnp.int32)
    gather = one_hot(counts, micro_count, slots, low, packed.shape[0])
    receives = lax.axis_index("section") < lax.axis_size("section") - 1
    scatter[...] = jnp.where(receives, gather.astype(f32), 0.0).astype(bf16)
    gather = jnp.transpose(gather.astype(f32)).astype(bf16)
    values = masked[...]
    fetches[5].start()
    for fetch in fetches[2:5]:
        fetch.wait()
    blocks = [slice(at, at + block_rows) for at in range(0, rows, block_rows)]
    squares = [jnp.zeros((block_rows, lanes), f32) for _ in blocks]
    products = [jnp.zeros((block_rows, lanes), f32) for _ in blocks]
    for tile in range(0, width, tile_width):
        here = lax.dot_general(
            values, w[tile : tile + tile_width, :], contract_last, preferred_element_type=f32
        )
        back[:, tile : tile + tile_width] = here
        for k, part in enumerate(blocks):
            for at in range(0, tile_width, lanes):
                cut = pl.ds(tile + at, lanes)
                wide = x[part, cut].astype(f32)
                squares[k] += wide * wide
                products[k] += wide * here[part, at : at + lanes] * gain[:, cut]
    scales = lax.rsqrt(jnp.sum(jnp.concatenate(squares, axis=0), axis=1, keepdims=True) / width + eps_norm)
    pulls = scales * jnp.sum(jnp.concatenate(products, axis=0), axis=1, keepdims=True) / width
    waits = jnp.concatenate(
        [
            lax.broadcasted_iota(jnp.int32, (slots, 1), 0) < jnp.where(receives, counts[m], 0)
            for m in range(micro_count)
        ],
        axis=0,
    )
    spread = (rows, band_width)
    scales = jnp.broadcast_to(scales, spread)
    pulls = jnp.broadcast_to(pulls, spread)
    waits = jnp.broadcast_to(waits, spread)
    fetches[5].wait()
    for cut in cuts(width, band_width):
        scaled = gain[:, cut]
        partial = jnp.zeros((sublanes, band_width), f32)
        for part in blocks:
            unit = x[part, cut].astype(f32) * scales[part]
            here = back[part, cut]
            partial += (unit * here).reshape(block_rows // sublanes, sublanes, band_width).sum(axis=0)
            normed[part, cut] = (unit * scaled).astype(bf16)
            own = scales[part] * (scaled * here - unit * pulls[part])
            whole = top[part, cut].astype(f32) + own
            sent[part, cut] = whole.astype(bf16)
            addend[part, cut] = jnp.where(waits[part], own, whole)
        gain_out[:, cut] = jnp.sum(partial, axis=0, keepdims=True)
        packed[:, cut] = jnp.dot(gather, sent[:, cut], preferred_element_type=f32).astype(bf16)


def branch_rows(low, room, counts, x, top, v, w, gain):
    rows, width = top.shape
    depth = v.shape[2]
    return pl.pallas_call(
        functools.partial(branch_kernel, low),
        in_specs=[pl.BlockSpec(memory_space=pltpu.HBM)] * 6,
        out_specs=[near] * 3 + [scalar] + [near] * 3,
        out_shape=[
            jax.ShapeDtypeStruct((room, width), bf16),
            jax.ShapeDtypeStruct((rows, width), f32),
            jax.ShapeDtypeStruct((rows, room), bf16),
            pltpu.SMEM((1,), jnp.int32),
            jax.ShapeDtypeStruct((rows, width), bf16),
            jax.ShapeDtypeStruct((rows, depth), bf16),
            jax.ShapeDtypeStruct((1, width), f32),
        ],
        scratch_shapes=[
            pltpu.SMEM(counts.shape, jnp.int32),
            pltpu.VMEM((rows, width), bf16),
            pltpu.VMEM((rows, width), bf16),
            pltpu.VMEM((rows, depth), bf16),
            pltpu.VMEM((width, depth), bf16),
            pltpu.VMEM((1, width), f32),
            pltpu.VMEM((rows, width), f32),
            pltpu.VMEM((rows, width), bf16),
            pltpu.SemaphoreType.DMA((6,)),
        ],
        compiler_params=roomy,
        cost_estimate=small_cost,
    )(*[far(a) for a in (counts, x, top, v, w, gain)])


def pack_kernel(gather, sent, packed):
    for cut in cuts(sent.shape[1], tile_width):
        packed[:, cut] = lax.dot_general(
            gather[...], sent[:, cut], contract_rows, preferred_element_type=f32
        ).astype(bf16)


def pack(gather, sent):
    return pl.pallas_call(
        pack_kernel,
        in_specs=[near, near],
        out_specs=near,
        out_shape=jax.ShapeDtypeStruct((gather.shape[1], sent.shape[1]), bf16),
        compiler_params=roomy,
        cost_estimate=small_cost,
    )(gather, sent)


def receive_kernel(target, first, factor, scatter, received, addend, more, *refs):
    rows, width = addend.shape
    if first:
        *parts, out_far, more_out, owned_far, out, owned, done = refs
    else:
        previous, out_far, more_out, out, done = refs
    more_out[0] = more[0]
    place = scatter[...]
    writes = []
    if first and parts:
        total_rows(factor, owned, *parts)
        writes.append(pltpu.make_async_copy(owned, owned_far, done.at[width // tile_width]))
        writes[0].start()
    if not first:
        here = (lax.axis_index("section") == target).astype(f32)
        covered = jnp.sum(place.astype(f32), axis=1, keepdims=True) * here > 0.5
    for k, cut in enumerate(cuts(width, tile_width)):
        total = jnp.dot(place, received[:, cut], preferred_element_type=f32) + addend[:, cut]
        if not first:
            total = jnp.where(covered, total, previous[:, cut].astype(f32))
        out[:, cut] = total.astype(bf16)
        write = pltpu.make_async_copy(out.at[:, cut], out_far.at[0, :, cut], done.at[k])
        write.start()
        writes.append(write)
    for write in writes:
        write.wait()


def receive(target, scatter, received, addend, more, previous=None, parts=(), owned=lanes, factor=1.0):
    rows, width = addend.shape
    away = pl.BlockSpec(memory_space=pltpu.HBM)
    first = previous is None
    others = parts if first else [previous]
    outs = [pltpu.HBM((1, rows, width), bf16), pltpu.SMEM(more.shape, more.dtype)]
    scratch = [pltpu.VMEM((rows, width), bf16)]
    if first:
        outs.append(pltpu.HBM((1, owned), f32))
        scratch.append(pltpu.VMEM((1, owned), f32))
    return pl.pallas_call(
        functools.partial(receive_kernel, target, first, factor),
        in_specs=[near, near, near, scalar] + [near] * len(others),
        out_specs=[away, scalar] + [away] * first,
        out_shape=outs,
        scratch_shapes=scratch + [pltpu.SemaphoreType.DMA((width // tile_width + 1,))],
        compiler_params=roomy,
        cost_estimate=small_cost,
    )(scatter, received, addend, more, *others)


def terms_kernel(owned_rows, normed, masked, gain, keep, give, give_low, total):
    width = normed.shape[1]
    values = masked[...]
    gain_rows = width // lanes
    for k in range(gain_rows):
        total[k : k + 1, :] = gain[:, k * lanes : (k + 1) * lanes]
    for at in range(0, width, tile_width):
        total[gain_rows + at : gain_rows + at + tile_width, :] = lax.dot_general(
            normed[:, at : at + tile_width], values, contract_rows, preferred_element_type=f32
        )
    even_core = lax.axis_index("dp") % pair == 0
    padded = keep.shape[1]
    for j in range(keep.shape[0]):
        even = total[2 * j * owned_rows : (2 * j + 1) * owned_rows, :]
        odd = total[(2 * j + 1) * owned_rows : (2 * j + 2) * owned_rows, :]
        if padded > owned_rows:
            blank = jnp.zeros((padded - owned_rows, lanes), f32)
            even = jnp.concatenate([even, blank], axis=0)
            odd = jnp.concatenate([odd, blank], axis=0)
        keep[j] = jnp.where(even_core, even, odd)
        other = jnp.where(even_core, odd, even).astype(bf16)
        give[j] = other[: give.shape[1], :]
        give_low[j] = other[give.shape[1] :, :]


def pair_terms(normed, masked, gain, owned_rows, owners):
    padded = -(-owned_rows // pack_rows) * pack_rows
    cut = padded // 2 // pack_rows * pack_rows
    blocks = owners // pair
    return pl.pallas_call(
        functools.partial(terms_kernel, owned_rows),
        in_specs=[near, near, near],
        out_specs=[near, near, near],
        out_shape=[
            jax.ShapeDtypeStruct((blocks, padded, lanes), f32),
            jax.ShapeDtypeStruct((blocks, cut, lanes), bf16),
            jax.ShapeDtypeStruct((blocks, padded - cut, lanes), bf16),
        ],
        scratch_shapes=[pltpu.VMEM((owners * owned_rows, lanes), f32)],
        compiler_params=roomy,
        cost_estimate=small_cost,
    )(normed, masked, gain)


def merge_kernel(offsets, direct, keep, taken, taken_low, hold, give, *straight):
    chip = lax.axis_index("dp") // pair
    mine, place = chip % 2, chip // 2
    count = keep.shape[0] // 2
    cut = taken.shape[1]

    def total(at, out):
        high = keep[at, :cut, :] + taken[at].astype(f32)
        low = keep[at, cut:, :] + taken_low[at].astype(f32)
        out[:cut, :] = high.astype(out.dtype)
        out[cut:, :] = low.astype(out.dtype)

    for k, offset in enumerate(offsets):
        at = 2 * lax.rem(place + offset, count)
        total(at + mine, hold.at[k])
        total(at + 1 - mine, give.at[k])
    for k, offset in enumerate(direct):
        at = 2 * lax.rem(place + offset, count)
        total(at + mine, straight[2 * k])
        total(at + 1 - mine, straight[2 * k + 1])


def merge_terms(offsets, direct, keep, taken, taken_low):
    block = keep.shape[1:]
    outs = [
        jax.ShapeDtypeStruct((len(offsets),) + block, f32),
        jax.ShapeDtypeStruct((len(offsets),) + block, bf16),
    ] + [jax.ShapeDtypeStruct(block, bf16)] * (2 * len(direct))
    return pl.pallas_call(
        functools.partial(merge_kernel, offsets, direct),
        in_specs=[near, near, near],
        out_specs=[near] * len(outs),
        out_shape=outs,
        compiler_params=roomy,
        cost_estimate=small_cost,
    )(keep, taken, taken_low)


def split_kernel(hold, taken, *parts):
    for k, part in enumerate(parts):
        part[...] = (hold[k] + taken[k].astype(f32)).astype(part.dtype)


def split_terms(part, hold, taken):
    return pl.pallas_call(
        split_kernel,
        in_specs=[near, near],
        out_specs=[near] * len(part),
        out_shape=[jax.ShapeDtypeStruct(hold.shape[1:], bf16 if offset else f32) for offset in part],
        compiler_params=roomy,
        cost_estimate=small_cost,
    )(hold, taken)


def total_rows(factor, out, own, *landed):
    total = own[...]
    for part in landed:
        total += part[...].astype(f32)
    total = total * factor
    for k in range(out.shape[1] // lanes):
        out[:, k * lanes : (k + 1) * lanes] = total[k : k + 1, :]


def plane_parts(owners, keep, *taken):
    quad = 2 * pair
    count = owners // quad
    direct = [count // 2] if count > 2 else []
    offsets = [k for k in range(count) if k not in direct]

    def along(offset, side):
        return [(i, (i + quad * offset) % owners ^ pair * side) for i in range(owners)]

    hold, give, *straight = merge_terms(offsets, direct, keep, *taken)
    across = lax.ppermute(give, "dp", along(0, 1))
    arrived = [
        lax.ppermute(straight[2 * k + side], "dp", along(offset, side))
        for k, offset in enumerate(direct)
        for side in range(2)
    ]
    own, *parts = split_terms(offsets, hold, across)
    for offset, part in zip(offsets[1:], parts):
        arrived.append(lax.ppermute(part, "dp", along(offset, 0)))
    return own, *arrived


def weight_owned(normed, masked, gain, factor):
    owners = lax.axis_size("dp")
    width = normed.shape[1]
    depth = masked.shape[1]
    owned = (width + width * depth) // owners
    if depth != lanes or owned % lanes or owners % (2 * pair):
        weight_term = lax.dot_general(normed, masked, contract_rows, preferred_element_type=f32)
        flat = jnp.concatenate([gain.reshape(-1), weight_term.reshape(-1)]) * factor
        return (), owned, lax.psum_scatter(flat, "dp", scatter_dimension=0, tiled=True)[None, :]
    keep, *give = pair_terms(normed, masked, gain, owned // lanes, owners)
    taken = [lax.ppermute(part, "dp", [(i, i ^ 1) for i in range(owners)]) for part in give]
    return plane_parts(owners, keep, *taken), owned, None


def shards(layer_inputs, top_grad, value_grads, weights, norm_gains, counts):
    rows = layer_inputs.shape[1]
    factor = 1.0 / math.sqrt(rows * lax.axis_size("dp"))
    sections = lax.axis_size("section")
    room = -(-rows * 3 // 4 // pack_rows) * pack_rows
    spare = rows - room
    inputs = (counts, layer_inputs, top_grad, value_grads, weights, norm_gains)
    packed, addend, scatter, more, normed, masked, gain = branch_rows(0, room, *inputs)
    parts, owned_size, owned = weight_owned(normed, masked, gain, factor)
    result = None
    for hop in range(sections - 1):
        target = sections - 2 - hop
        hops = [(target + 1, target), (target, target + 1)]
        before = result
        if hop:
            packed = pack(scatter, before)
        landed = lax.ppermute(packed, "section", hops)
        if hop:
            updated, more = receive(target, scatter, landed, addend, more, before)
        else:
            updated, more, summed = receive(target, scatter, landed, addend, more, None, parts, owned_size, factor)

        def rest(updated):
            packed, addend, scatter, more, *_ = branch_rows(room, spare, *inputs)
            if hop:
                packed = pack(scatter, before)
            landed = lax.ppermute(packed, "section", hops)
            return receive(target, scatter, landed, addend, more, updated[0])[0]

        updated = lax.cond(more.reshape(()) > 0, rest, lambda updated: updated, updated)
        result = updated[0]
    return (result[None], summed if owned is None else owned)


def solution(mesh):
    placed = (
        P("section", "dp", None),
        P("dp", None),
        P("section", "dp", None),
        P("section", None, None),
        P("section", None),
        P("dp"),
    )
    return jax.shard_map(
        shards,
        mesh=mesh,
        in_specs=placed,
        out_specs=(P("section", "dp", None), P("section", "dp")),
        check_vma=False,
    )
```

```python
import functools
import math

import jax
import jax.numpy as jnp
from jax import lax
from jax.experimental import pallas as pl
from jax.experimental.pallas import tpu as pltpu
from jax.sharding import PartitionSpec as P

eps_norm = 1e-05
lanes = 128
sublanes = 8
pack_rows = 16
tile_width = 512
pair = 2
block_rows = 32
band_width = 256
f32 = jnp.float32
bf16 = jnp.bfloat16
contract_last = (((1,), (1,)), ((), ()))
contract_rows = (((0,), (0,)), ((), ()))
small_cost = pl.CostEstimate(flops=1 << 20, bytes_accessed=1 << 16, transcendentals=0)
roomy = pltpu.CompilerParams(vmem_limit_bytes=32 << 20)
near = pl.BlockSpec(memory_space=pltpu.VMEM)
scalar = pl.BlockSpec(memory_space=pltpu.SMEM)


def far(array):
    return pltpu.with_memory_space_constraint(array, pltpu.HBM)


def cuts(width, step):
    return [pl.ds(at, step) for at in range(0, width, step)]


def one_hot(counts, micro_count, slots, low, size):
    slot = lax.broadcasted_iota(jnp.int32, (slots, size), 0)
    column = lax.broadcasted_iota(jnp.int32, (slots, size), 1) + low
    start = jnp.int32(0)
    pieces = []
    for m in range(micro_count):
        hit = (slot < counts[m]) & (slot + start == column)
        pieces.append(jnp.where(hit, 1.0, 0.0))
        start = start + counts[m]
    return jnp.concatenate(pieces, axis=0).astype(bf16)


def branch_kernel(
    low, counts_far, x_far, top_far, v_far, w_far, gain_far,
    packed, addend, scatter, more, masked, x, back, scale_out, gain,
    counts, top, v, w, sent, ready,
):
    rows, width = addend.shape
    micro_count = counts.shape[0]
    slots = rows // micro_count
    fetches = [
        pltpu.make_async_copy(v_far.at[0], v, ready.at[0]),
        pltpu.make_async_copy(counts_far, counts, ready.at[1]),
        pltpu.make_async_copy(w_far.at[0], w, ready.at[2]),
        pltpu.make_async_copy(x_far.at[0], x, ready.at[3]),
        pltpu.make_async_copy(gain_far, gain, ready.at[4]),
        pltpu.make_async_copy(top_far, top, ready.at[5]),
    ]
    for fetch in fetches:
        fetch.start()
    fetches[0].wait()
    fetches[1].wait()
    slot = lax.broadcasted_iota(jnp.int32, (slots, v.shape[1]), 0)
    for m in range(micro_count):
        piece = v[m * slots : (m + 1) * slots, :]
        masked[m * slots : (m + 1) * slots, :] = jnp.where(slot < counts[m], piece, jnp.zeros_like(piece))
    live = jnp.int32(0)
    for m in range(micro_count):
        live += counts[m]
    more[0] = (live > low + packed.shape[0]).astype(jnp.int32)
    gather = one_hot(counts, micro_count, slots, low, packed.shape[0])
    receives = lax.axis_index("section") < lax.axis_size("section") - 1
    scatter[...] = jnp.where(receives, gather.astype(f32), 0.0).astype(bf16)
    gather = jnp.transpose(gather.astype(f32)).astype(bf16)
    values = masked[...]
    for fetch in fetches[2:5]:
        fetch.wait()
    blocks = [slice(at, at + block_rows) for at in range(0, rows, block_rows)]
    squares = [jnp.zeros((block_rows, lanes), f32) for _ in blocks]
    products = [jnp.zeros((block_rows, lanes), f32) for _ in blocks]
    for tile in range(0, width, tile_width):
        here = lax.dot_general(
            values, w[tile : tile + tile_width, :], contract_last, preferred_element_type=f32
        )
        back[:, tile : tile + tile_width] = here
        for k, part in enumerate(blocks):
            for at in range(0, tile_width, lanes):
                cut = pl.ds(tile + at, lanes)
                wide = x[part, cut].astype(f32)
                squares[k] += wide * wide
                products[k] += wide * here[part, at : at + lanes] * gain[:, cut]
    scales = lax.rsqrt(jnp.sum(jnp.concatenate(squares, axis=0), axis=1, keepdims=True) / width + eps_norm)
    pulls = scales * jnp.sum(jnp.concatenate(products, axis=0), axis=1, keepdims=True) / width
    waits = jnp.concatenate(
        [
            lax.broadcasted_iota(jnp.int32, (slots, 1), 0) < jnp.where(receives, counts[m], 0)
            for m in range(micro_count)
        ],
        axis=0,
    )
    spread = (rows, band_width)
    scales = jnp.broadcast_to(scales, spread)
    scale_out[...] = scales[:, :lanes]
    pulls = jnp.broadcast_to(pulls, spread)
    waits = jnp.broadcast_to(waits, spread)
    fetches[5].wait()
    for cut in cuts(width, band_width):
        scaled = gain[:, cut]
        for part in blocks:
            unit = x[part, cut].astype(f32) * scales[part]
            here = back[part, cut]
            own = scales[part] * (scaled * here - unit * pulls[part])
            whole = top[part, cut].astype(f32) + own
            sent[part, cut] = whole.astype(bf16)
            addend[part, cut] = jnp.where(waits[part], own, whole)
        packed[:, cut] = jnp.dot(gather, sent[:, cut], preferred_element_type=f32).astype(bf16)


def branch_rows(low, room, counts, x, top, v, w, gain):
    rows, width = top.shape
    depth = v.shape[2]
    return pl.pallas_call(
        functools.partial(branch_kernel, low),
        in_specs=[pl.BlockSpec(memory_space=pltpu.HBM)] * 6,
        out_specs=[near] * 3 + [scalar] + [near] * 5,
        out_shape=[
            jax.ShapeDtypeStruct((room, width), bf16),
            jax.ShapeDtypeStruct((rows, width), f32),
            jax.ShapeDtypeStruct((rows, room), bf16),
            pltpu.SMEM((1,), jnp.int32),
            jax.ShapeDtypeStruct((rows, depth), bf16),
            jax.ShapeDtypeStruct((rows, width), bf16),
            jax.ShapeDtypeStruct((rows, width), f32),
            jax.ShapeDtypeStruct((rows, lanes), f32),
            jax.ShapeDtypeStruct((1, width), f32),
        ],
        scratch_shapes=[
            pltpu.SMEM(counts.shape, jnp.int32),
            pltpu.VMEM((rows, width), bf16),
            pltpu.VMEM((rows, depth), bf16),
            pltpu.VMEM((width, depth), bf16),
            pltpu.VMEM((rows, width), bf16),
            pltpu.SemaphoreType.DMA((6,)),
        ],
        compiler_params=roomy,
        cost_estimate=small_cost,
    )(*[far(a) for a in (counts, x, top, v, w, gain)])


def pack_kernel(gather, sent, packed):
    for cut in cuts(sent.shape[1], tile_width):
        packed[:, cut] = lax.dot_general(
            gather[...], sent[:, cut], contract_rows, preferred_element_type=f32
        ).astype(bf16)


def pack(gather, sent):
    return pl.pallas_call(
        pack_kernel,
        in_specs=[near, near],
        out_specs=near,
        out_shape=jax.ShapeDtypeStruct((gather.shape[1], sent.shape[1]), bf16),
        compiler_params=roomy,
        cost_estimate=small_cost,
    )(gather, sent)


def receive_kernel(target, first, factor, scatter, received, addend, more, *refs):
    rows, width = addend.shape
    if first:
        *parts, out_far, more_out, owned_far, out, owned, done = refs
    else:
        previous, out_far, more_out, out, done = refs
    more_out[0] = more[0]
    place = scatter[...]
    writes = []
    if first and parts:
        total_rows(factor, owned, *parts)
        writes.append(pltpu.make_async_copy(owned, owned_far, done.at[width // tile_width]))
        writes[0].start()
    if not first:
        here = (lax.axis_index("section") == target).astype(f32)
        covered = jnp.sum(place.astype(f32), axis=1, keepdims=True) * here > 0.5
    for k, cut in enumerate(cuts(width, tile_width)):
        total = jnp.dot(place, received[:, cut], preferred_element_type=f32) + addend[:, cut]
        if not first:
            total = jnp.where(covered, total, previous[:, cut].astype(f32))
        out[:, cut] = total.astype(bf16)
        write = pltpu.make_async_copy(out.at[:, cut], out_far.at[0, :, cut], done.at[k])
        write.start()
        writes.append(write)
    for write in writes:
        write.wait()


def receive(target, scatter, received, addend, more, previous=None, parts=(), owned=lanes, factor=1.0):
    rows, width = addend.shape
    away = pl.BlockSpec(memory_space=pltpu.HBM)
    first = previous is None
    others = parts if first else [previous]
    outs = [pltpu.HBM((1, rows, width), bf16), pltpu.SMEM(more.shape, more.dtype)]
    scratch = [pltpu.VMEM((rows, width), bf16)]
    if first:
        outs.append(pltpu.HBM((1, owned), f32))
        scratch.append(pltpu.VMEM((1, owned), f32))
    return pl.pallas_call(
        functools.partial(receive_kernel, target, first, factor),
        in_specs=[near, near, near, scalar] + [near] * len(others),
        out_specs=[away, scalar] + [away] * first,
        out_shape=outs,
        scratch_shapes=scratch + [pltpu.SemaphoreType.DMA((width // tile_width + 1,))],
        compiler_params=roomy,
        cost_estimate=small_cost,
    )(scatter, received, addend, more, *others)


def terms_kernel(owned_rows, masked, x, back, scale, gain, keep, give, give_low, total):
    rows, width = x.shape
    values = masked[...]
    gain_rows = width // lanes
    spread = jnp.concatenate([scale[...]] * (band_width // lanes), axis=1)
    for at in range(0, width, band_width):
        cut = pl.ds(at, band_width)
        unit = x[:, cut].astype(f32) * spread
        summed = (unit * back[:, cut]).reshape(rows // sublanes, sublanes, band_width).sum(axis=0)
        summed = jnp.sum(summed, axis=0, keepdims=True)
        for k in range(0, band_width, lanes):
            spot = (at + k) // lanes
            total[spot : spot + 1, :] = summed[:, k : k + lanes]
        normed = (unit * gain[:, cut]).astype(bf16)
        total[gain_rows + at : gain_rows + at + band_width, :] = lax.dot_general(
            normed, values, contract_rows, preferred_element_type=f32
        )
    even_core = lax.axis_index("dp") % pair == 0
    padded = keep.shape[1]
    for j in range(keep.shape[0]):
        even = total[2 * j * owned_rows : (2 * j + 1) * owned_rows, :]
        odd = total[(2 * j + 1) * owned_rows : (2 * j + 2) * owned_rows, :]
        if padded > owned_rows:
            blank = jnp.zeros((padded - owned_rows, lanes), f32)
            even = jnp.concatenate([even, blank], axis=0)
            odd = jnp.concatenate([odd, blank], axis=0)
        keep[j] = jnp.where(even_core, even, odd)
        other = jnp.where(even_core, odd, even).astype(bf16)
        give[j] = other[: give.shape[1], :]
        give_low[j] = other[give.shape[1] :, :]


def pair_terms(made, owned_rows, owners):
    padded = -(-owned_rows // pack_rows) * pack_rows
    cut = padded // 2 // pack_rows * pack_rows
    blocks = owners // pair
    return pl.pallas_call(
        functools.partial(terms_kernel, owned_rows),
        in_specs=[near] * len(made),
        out_specs=[near, near, near],
        out_shape=[
            jax.ShapeDtypeStruct((blocks, padded, lanes), f32),
            jax.ShapeDtypeStruct((blocks, cut, lanes), bf16),
            jax.ShapeDtypeStruct((blocks, padded - cut, lanes), bf16),
        ],
        scratch_shapes=[pltpu.VMEM((owners * owned_rows, lanes), f32)],
        compiler_params=roomy,
        cost_estimate=small_cost,
    )(*made)


def merge_kernel(offsets, direct, keep, taken, taken_low, hold, give, *straight):
    chip = lax.axis_index("dp") // pair
    mine, place = chip % 2, chip // 2
    count = keep.shape[0] // 2
    cut = taken.shape[1]

    def total(at, out):
        high = keep[at, :cut, :] + taken[at].astype(f32)
        low = keep[at, cut:, :] + taken_low[at].astype(f32)
        out[:cut, :] = high.astype(out.dtype)
        out[cut:, :] = low.astype(out.dtype)

    for k, offset in enumerate(offsets):
        at = 2 * lax.rem(place + offset, count)
        total(at + mine, hold.at[k])
        total(at + 1 - mine, give.at[k])
    for k, offset in enumerate(direct):
        at = 2 * lax.rem(place + offset, count)
        total(at + mine, straight[2 * k])
        total(at + 1 - mine, straight[2 * k + 1])


def merge_terms(offsets, direct, keep, taken, taken_low):
    block = keep.shape[1:]
    outs = [
        jax.ShapeDtypeStruct((len(offsets),) + block, f32),
        jax.ShapeDtypeStruct((len(offsets),) + block, bf16),
    ] + [jax.ShapeDtypeStruct(block, bf16)] * (2 * len(direct))
    return pl.pallas_call(
        functools.partial(merge_kernel, offsets, direct),
        in_specs=[near, near, near],
        out_specs=[near] * len(outs),
        out_shape=outs,
        compiler_params=roomy,
        cost_estimate=small_cost,
    )(keep, taken, taken_low)


def split_kernel(hold, taken, *parts):
    for k, part in enumerate(parts):
        part[...] = (hold[k] + taken[k].astype(f32)).astype(part.dtype)


def split_terms(part, hold, taken):
    return pl.pallas_call(
        split_kernel,
        in_specs=[near, near],
        out_specs=[near] * len(part),
        out_shape=[jax.ShapeDtypeStruct(hold.shape[1:], bf16 if offset else f32) for offset in part],
        compiler_params=roomy,
        cost_estimate=small_cost,
    )(hold, taken)


def total_rows(factor, out, own, *landed):
    total = own[...]
    for part in landed:
        total += part[...].astype(f32)
    total = total * factor
    for k in range(out.shape[1] // lanes):
        out[:, k * lanes : (k + 1) * lanes] = total[k : k + 1, :]


def plane_parts(owners, keep, *taken):
    quad = 2 * pair
    count = owners // quad
    direct = [count // 2] if count > 2 else []
    offsets = [k for k in range(count) if k not in direct]

    def along(offset, side):
        return [(i, (i + quad * offset) % owners ^ pair * side) for i in range(owners)]

    hold, give, *straight = merge_terms(offsets, direct, keep, *taken)
    across = lax.ppermute(give, "dp", along(0, 1))
    arrived = [
        lax.ppermute(straight[2 * k + side], "dp", along(offset, side))
        for k, offset in enumerate(direct)
        for side in range(2)
    ]
    own, *parts = split_terms(offsets, hold, across)
    for offset, part in zip(offsets[1:], parts):
        arrived.append(lax.ppermute(part, "dp", along(offset, 0)))
    return own, *arrived


def weight_owned(made, factor):
    owners = lax.axis_size("dp")
    masked, x, back, scale, gain = made
    width = x.shape[1]
    depth = masked.shape[1]
    owned = (width + width * depth) // owners
    if depth != lanes or owned % lanes or owners % (2 * pair):
        unit = x.astype(f32) * scale[:, :1]
        normed = (unit * gain).astype(bf16)
        weight_term = lax.dot_general(normed, masked, contract_rows, preferred_element_type=f32)
        flat = jnp.concatenate([jnp.sum(unit * back, axis=0), weight_term.reshape(-1)]) * factor
        return (), owned, lax.psum_scatter(flat, "dp", scatter_dimension=0, tiled=True)[None, :]
    keep, *give = pair_terms(made, owned // lanes, owners)
    taken = [lax.ppermute(part, "dp", [(i, i ^ 1) for i in range(owners)]) for part in give]
    return plane_parts(owners, keep, *taken), owned, None


def shards(layer_inputs, top_grad, value_grads, weights, norm_gains, counts):
    rows = layer_inputs.shape[1]
    factor = 1.0 / math.sqrt(rows * lax.axis_size("dp"))
    sections = lax.axis_size("section")
    room = -(-rows * 3 // 4 // pack_rows) * pack_rows
    spare = rows - room
    inputs = (counts, layer_inputs, top_grad, value_grads, weights, norm_gains)
    packed, addend, scatter, more, *made = branch_rows(0, room, *inputs)
    parts, owned_size, owned = weight_owned(made, factor)
    result = None
    for hop in range(sections - 1):
        target = sections - 2 - hop
        hops = [(target + 1, target), (target, target + 1)]
        before = result
        if hop:
            packed = pack(scatter, before)
        landed = lax.ppermute(packed, "section", hops)
        if hop:
            updated, more = receive(target, scatter, landed, addend, more, before)
        else:
            updated, more, summed = receive(target, scatter, landed, addend, more, None, parts, owned_size, factor)

        def rest(updated):
            packed, addend, scatter, more, *_ = branch_rows(room, spare, *inputs)
            if hop:
                packed = pack(scatter, before)
            landed = lax.ppermute(packed, "section", hops)
            return receive(target, scatter, landed, addend, more, updated[0])[0]

        updated = lax.cond(more.reshape(()) > 0, rest, lambda updated: updated, updated)
        result = updated[0]
    return (result[None], summed if owned is None else owned)


def solution(mesh):
    placed = (
        P("section", "dp", None),
        P("dp", None),
        P("section", "dp", None),
        P("section", None, None),
        P("section", None),
        P("dp"),
    )
    return jax.shard_map(
        shards,
        mesh=mesh,
        in_specs=placed,
        out_specs=(P("section", "dp", None), P("section", "dp")),
        check_vma=False,
    )
```

```python
import functools
import math

import jax
import jax.numpy as jnp
from jax import lax
from jax.experimental import pallas as pl
from jax.experimental.pallas import tpu as pltpu
from jax.sharding import PartitionSpec as P

eps_norm = 1e-05
lanes = 128
sublanes = 8
pack_rows = 16
tile_width = 512
pair = 2
block_rows = 32
band_width = 256
f32 = jnp.float32
bf16 = jnp.bfloat16
contract_last = (((1,), (1,)), ((), ()))
contract_rows = (((0,), (0,)), ((), ()))
small_cost = pl.CostEstimate(flops=1 << 20, bytes_accessed=1 << 16, transcendentals=0)
roomy = pltpu.CompilerParams(vmem_limit_bytes=32 << 20)
near = pl.BlockSpec(memory_space=pltpu.VMEM)
scalar = pl.BlockSpec(memory_space=pltpu.SMEM)


def far(array):
    return pltpu.with_memory_space_constraint(array, pltpu.HBM)


def cuts(width, step):
    return [pl.ds(at, step) for at in range(0, width, step)]


def one_hot(counts, micro_count, slots, low, size):
    slot = lax.broadcasted_iota(jnp.int32, (slots, size), 0)
    column = lax.broadcasted_iota(jnp.int32, (slots, size), 1) + low
    start = jnp.int32(0)
    pieces = []
    for m in range(micro_count):
        hit = (slot < counts[m]) & (slot + start == column)
        pieces.append(jnp.where(hit, 1.0, 0.0))
        start = start + counts[m]
    return jnp.concatenate(pieces, axis=0).astype(bf16)


def branch_kernel(
    low, counts_far, x_far, top_far, v_far, w_far, gain_far,
    packed, addend, scatter, more, masked, x, back, scale_out, gain,
    counts, top, v, w, sent, ready,
):
    rows, width = addend.shape
    micro_count = counts.shape[0]
    slots = rows // micro_count
    fetches = [
        pltpu.make_async_copy(v_far.at[0], v, ready.at[0]),
        pltpu.make_async_copy(counts_far, counts, ready.at[1]),
        pltpu.make_async_copy(w_far.at[0], w, ready.at[2]),
        pltpu.make_async_copy(x_far.at[0], x, ready.at[3]),
        pltpu.make_async_copy(gain_far, gain, ready.at[4]),
        pltpu.make_async_copy(top_far, top, ready.at[5]),
    ]
    for fetch in fetches:
        fetch.start()
    fetches[0].wait()
    fetches[1].wait()
    slot = lax.broadcasted_iota(jnp.int32, (slots, v.shape[1]), 0)
    for m in range(micro_count):
        piece = v[m * slots : (m + 1) * slots, :]
        masked[m * slots : (m + 1) * slots, :] = jnp.where(slot < counts[m], piece, jnp.zeros_like(piece))
    live = jnp.int32(0)
    for m in range(micro_count):
        live += counts[m]
    more[0] = (live > low + packed.shape[0]).astype(jnp.int32)
    gather = one_hot(counts, micro_count, slots, low, packed.shape[0])
    receives = lax.axis_index("section") < lax.axis_size("section") - 1
    scatter[...] = jnp.where(receives, gather.astype(f32), 0.0).astype(bf16)
    gather = jnp.transpose(gather.astype(f32)).astype(bf16)
    values = masked[...]
    for fetch in fetches[2:5]:
        fetch.wait()
    blocks = [slice(at, at + block_rows) for at in range(0, rows, block_rows)]
    squares = [jnp.zeros((block_rows, lanes), f32) for _ in blocks]
    products = [jnp.zeros((block_rows, lanes), f32) for _ in blocks]
    for tile in range(0, width, band_width):
        here = lax.dot_general(
            values, w[tile : tile + band_width, :], contract_last, preferred_element_type=f32
        )
        back[:, tile : tile + band_width] = here
        for k, part in enumerate(blocks):
            for at in range(0, band_width, lanes):
                cut = pl.ds(tile + at, lanes)
                wide = x[part, cut].astype(f32)
                squares[k] += wide * wide
                products[k] += wide * here[part, at : at + lanes] * gain[:, cut]
    scales = lax.rsqrt(jnp.sum(jnp.concatenate(squares, axis=0), axis=1, keepdims=True) / width + eps_norm)
    pulls = scales * jnp.sum(jnp.concatenate(products, axis=0), axis=1, keepdims=True) / width
    waits = jnp.concatenate(
        [
            lax.broadcasted_iota(jnp.int32, (slots, 1), 0) < jnp.where(receives, counts[m], 0)
            for m in range(micro_count)
        ],
        axis=0,
    )
    spread = (rows, band_width)
    scales = jnp.broadcast_to(scales, spread)
    scale_out[...] = scales[:, :lanes]
    pulls = jnp.broadcast_to(pulls, spread)
    waits = jnp.broadcast_to(waits, spread)
    fetches[5].wait()
    for cut in cuts(width, band_width):
        scaled = gain[:, cut]
        for part in blocks:
            unit = x[part, cut].astype(f32) * scales[part]
            here = back[part, cut]
            own = scales[part] * (scaled * here - unit * pulls[part])
            whole = top[part, cut].astype(f32) + own
            sent[part, cut] = whole.astype(bf16)
            addend[part, cut] = jnp.where(waits[part], own, whole)
        packed[:, cut] = jnp.dot(gather, sent[:, cut], preferred_element_type=f32).astype(bf16)


def branch_rows(low, room, counts, x, top, v, w, gain):
    rows, width = top.shape
    depth = v.shape[2]
    return pl.pallas_call(
        functools.partial(branch_kernel, low),
        in_specs=[pl.BlockSpec(memory_space=pltpu.HBM)] * 6,
        out_specs=[near] * 3 + [scalar] + [near] * 5,
        out_shape=[
            jax.ShapeDtypeStruct((room, width), bf16),
            jax.ShapeDtypeStruct((rows, width), f32),
            jax.ShapeDtypeStruct((rows, room), bf16),
            pltpu.SMEM((1,), jnp.int32),
            jax.ShapeDtypeStruct((rows, depth), bf16),
            jax.ShapeDtypeStruct((rows, width), bf16),
            jax.ShapeDtypeStruct((rows, width), f32),
            jax.ShapeDtypeStruct((rows, lanes), f32),
            jax.ShapeDtypeStruct((1, width), f32),
        ],
        scratch_shapes=[
            pltpu.SMEM(counts.shape, jnp.int32),
            pltpu.VMEM((rows, width), bf16),
            pltpu.VMEM((rows, depth), bf16),
            pltpu.VMEM((width, depth), bf16),
            pltpu.VMEM((rows, width), bf16),
            pltpu.SemaphoreType.DMA((6,)),
        ],
        compiler_params=roomy,
        cost_estimate=small_cost,
    )(*[far(a) for a in (counts, x, top, v, w, gain)])


def pack_kernel(gather, sent, packed):
    for cut in cuts(sent.shape[1], tile_width):
        packed[:, cut] = lax.dot_general(
            gather[...], sent[:, cut], contract_rows, preferred_element_type=f32
        ).astype(bf16)


def pack(gather, sent):
    return pl.pallas_call(
        pack_kernel,
        in_specs=[near, near],
        out_specs=near,
        out_shape=jax.ShapeDtypeStruct((gather.shape[1], sent.shape[1]), bf16),
        compiler_params=roomy,
        cost_estimate=small_cost,
    )(gather, sent)


def receive_kernel(target, first, factor, scatter, received, addend, more, *refs):
    rows, width = addend.shape
    if first:
        *parts, out_far, more_out, owned_far, out, owned, done = refs
    else:
        previous, out_far, more_out, out, done = refs
    more_out[0] = more[0]
    place = scatter[...]
    writes = []
    if first and parts:
        total_rows(factor, owned, *parts)
        writes.append(pltpu.make_async_copy(owned, owned_far, done.at[width // tile_width]))
        writes[0].start()
    if not first:
        here = (lax.axis_index("section") == target).astype(f32)
        covered = jnp.sum(place.astype(f32), axis=1, keepdims=True) * here > 0.5
    for k, cut in enumerate(cuts(width, tile_width)):
        total = jnp.dot(place, received[:, cut], preferred_element_type=f32) + addend[:, cut]
        if not first:
            total = jnp.where(covered, total, previous[:, cut].astype(f32))
        out[:, cut] = total.astype(bf16)
        write = pltpu.make_async_copy(out.at[:, cut], out_far.at[0, :, cut], done.at[k])
        write.start()
        writes.append(write)
    for write in writes:
        write.wait()


def receive(target, scatter, received, addend, more, previous=None, parts=(), owned=lanes, factor=1.0):
    rows, width = addend.shape
    away = pl.BlockSpec(memory_space=pltpu.HBM)
    first = previous is None
    others = parts if first else [previous]
    outs = [pltpu.HBM((1, rows, width), bf16), pltpu.SMEM(more.shape, more.dtype)]
    scratch = [pltpu.VMEM((rows, width), bf16)]
    if first:
        outs.append(pltpu.HBM((1, owned), f32))
        scratch.append(pltpu.VMEM((1, owned), f32))
    return pl.pallas_call(
        functools.partial(receive_kernel, target, first, factor),
        in_specs=[near, near, near, scalar] + [near] * len(others),
        out_specs=[away, scalar] + [away] * first,
        out_shape=outs,
        scratch_shapes=scratch + [pltpu.SemaphoreType.DMA((width // tile_width + 1,))],
        compiler_params=roomy,
        cost_estimate=small_cost,
    )(scatter, received, addend, more, *others)


def terms_kernel(owned_rows, masked, x, back, scale, gain, keep, give, give_low, total):
    rows, width = x.shape
    values = masked[...]
    gain_rows = width // lanes
    spread = jnp.concatenate([scale[...]] * (band_width // lanes), axis=1)
    for at in range(0, width, band_width):
        cut = pl.ds(at, band_width)
        unit = x[:, cut].astype(f32) * spread
        summed = (unit * back[:, cut]).reshape(rows // sublanes, sublanes, band_width).sum(axis=0)
        summed = jnp.sum(summed, axis=0, keepdims=True)
        for k in range(0, band_width, lanes):
            spot = (at + k) // lanes
            total[spot : spot + 1, :] = summed[:, k : k + lanes]
        normed = (unit * gain[:, cut]).astype(bf16)
        total[gain_rows + at : gain_rows + at + band_width, :] = lax.dot_general(
            normed, values, contract_rows, preferred_element_type=f32
        )
    blocks, padded, _ = keep.shape
    cut = give.shape[1]

    def hand_out(side):
        for j in range(blocks):
            mine = (2 * j + side) * owned_rows
            other = (2 * j + 1 - side) * owned_rows
            keep[j, :owned_rows, :] = total[mine : mine + owned_rows, :]
            give[j] = total[other : other + cut, :].astype(bf16)
            low = total[other + cut : other + owned_rows, :]
            if padded > owned_rows:
                blank = jnp.zeros((padded - owned_rows, lanes), f32)
                keep[j, owned_rows:, :] = blank
                low = jnp.concatenate([low, blank], axis=0)
            give_low[j] = low.astype(bf16)

    side = lax.axis_index("dp") % pair
    for core in range(pair):
        pl.when(side == core)(functools.partial(hand_out, core))


def pair_terms(made, owned_rows, owners):
    padded = -(-owned_rows // pack_rows) * pack_rows
    cut = padded // 2 // pack_rows * pack_rows
    blocks = owners // pair
    return pl.pallas_call(
        functools.partial(terms_kernel, owned_rows),
        in_specs=[near] * len(made),
        out_specs=[near, near, near],
        out_shape=[
            jax.ShapeDtypeStruct((blocks, padded, lanes), f32),
            jax.ShapeDtypeStruct((blocks, cut, lanes), bf16),
            jax.ShapeDtypeStruct((blocks, padded - cut, lanes), bf16),
        ],
        scratch_shapes=[pltpu.VMEM((owners * owned_rows, lanes), f32)],
        compiler_params=roomy,
        cost_estimate=small_cost,
    )(*made)


def merge_kernel(offsets, direct, keep, taken, taken_low, hold, give, *straight):
    chip = lax.axis_index("dp") // pair
    mine, place = chip % 2, chip // 2
    count = keep.shape[0] // 2
    cut = taken.shape[1]

    def total(at, out):
        high = keep[at, :cut, :] + taken[at].astype(f32)
        low = keep[at, cut:, :] + taken_low[at].astype(f32)
        out[:cut, :] = high.astype(out.dtype)
        out[cut:, :] = low.astype(out.dtype)

    for k, offset in enumerate(offsets):
        at = 2 * lax.rem(place + offset, count)
        total(at + mine, hold.at[k])
        total(at + 1 - mine, give.at[k])
    for k, offset in enumerate(direct):
        at = 2 * lax.rem(place + offset, count)
        total(at + mine, straight[2 * k])
        total(at + 1 - mine, straight[2 * k + 1])


def merge_terms(offsets, direct, keep, taken, taken_low):
    block = keep.shape[1:]
    outs = [
        jax.ShapeDtypeStruct((len(offsets),) + block, f32),
        jax.ShapeDtypeStruct((len(offsets),) + block, bf16),
    ] + [jax.ShapeDtypeStruct(block, bf16)] * (2 * len(direct))
    return pl.pallas_call(
        functools.partial(merge_kernel, offsets, direct),
        in_specs=[near, near, near],
        out_specs=[near] * len(outs),
        out_shape=outs,
        compiler_params=roomy,
        cost_estimate=small_cost,
    )(keep, taken, taken_low)


def split_kernel(hold, taken, *parts):
    for k, part in enumerate(parts):
        part[...] = (hold[k] + taken[k].astype(f32)).astype(part.dtype)


def split_terms(part, hold, taken):
    return pl.pallas_call(
        split_kernel,
        in_specs=[near, near],
        out_specs=[near] * len(part),
        out_shape=[jax.ShapeDtypeStruct(hold.shape[1:], bf16 if offset else f32) for offset in part],
        compiler_params=roomy,
        cost_estimate=small_cost,
    )(hold, taken)


def total_rows(factor, out, own, *landed):
    total = own[...]
    for part in landed:
        total += part[...].astype(f32)
    total = total * factor
    for k in range(out.shape[1] // lanes):
        out[:, k * lanes : (k + 1) * lanes] = total[k : k + 1, :]


def plane_parts(owners, keep, *taken):
    quad = 2 * pair
    count = owners // quad
    direct = [count // 2] if count > 2 else []
    offsets = [k for k in range(count) if k not in direct]

    def along(offset, side):
        return [(i, (i + quad * offset) % owners ^ pair * side) for i in range(owners)]

    hold, give, *straight = merge_terms(offsets, direct, keep, *taken)
    across = lax.ppermute(give, "dp", along(0, 1))
    arrived = [
        lax.ppermute(straight[2 * k + side], "dp", along(offset, side))
        for k, offset in enumerate(direct)
        for side in range(2)
    ]
    own, *parts = split_terms(offsets, hold, across)
    for offset, part in zip(offsets[1:], parts):
        arrived.append(lax.ppermute(part, "dp", along(offset, 0)))
    return own, *arrived


def weight_owned(made, factor):
    owners = lax.axis_size("dp")
    masked, x, back, scale, gain = made
    width = x.shape[1]
    depth = masked.shape[1]
    owned = (width + width * depth) // owners
    if depth != lanes or owned % lanes or owners % (2 * pair):
        unit = x.astype(f32) * scale[:, :1]
        normed = (unit * gain).astype(bf16)
        weight_term = lax.dot_general(normed, masked, contract_rows, preferred_element_type=f32)
        flat = jnp.concatenate([jnp.sum(unit * back, axis=0), weight_term.reshape(-1)]) * factor
        return (), owned, lax.psum_scatter(flat, "dp", scatter_dimension=0, tiled=True)[None, :]
    keep, *give = pair_terms(made, owned // lanes, owners)
    taken = [lax.ppermute(part, "dp", [(i, i ^ 1) for i in range(owners)]) for part in give]
    return plane_parts(owners, keep, *taken), owned, None


def shards(layer_inputs, top_grad, value_grads, weights, norm_gains, counts):
    rows = layer_inputs.shape[1]
    factor = 1.0 / math.sqrt(rows * lax.axis_size("dp"))
    sections = lax.axis_size("section")
    room = -(-rows * 3 // 4 // pack_rows) * pack_rows
    spare = rows - room
    inputs = (counts, layer_inputs, top_grad, value_grads, weights, norm_gains)
    packed, addend, scatter, more, *made = branch_rows(0, room, *inputs)
    parts, owned_size, owned = weight_owned(made, factor)
    result = None
    for hop in range(sections - 1):
        target = sections - 2 - hop
        hops = [(target + 1, target), (target, target + 1)]
        before = result
        if hop:
            packed = pack(scatter, before)
        landed = lax.ppermute(packed, "section", hops)
        if hop:
            updated, more = receive(target, scatter, landed, addend, more, before)
        else:
            updated, more, summed = receive(target, scatter, landed, addend, more, None, parts, owned_size, factor)

        def rest(updated):
            packed, addend, scatter, more, *_ = branch_rows(room, spare, *inputs)
            if hop:
                packed = pack(scatter, before)
            landed = lax.ppermute(packed, "section", hops)
            return receive(target, scatter, landed, addend, more, updated[0])[0]

        updated = lax.cond(more.reshape(()) > 0, rest, lambda updated: updated, updated)
        result = updated[0]
    return (result[None], summed if owned is None else owned)


def solution(mesh):
    placed = (
        P("section", "dp", None),
        P("dp", None),
        P("section", "dp", None),
        P("section", None, None),
        P("section", None),
        P("dp"),
    )
    return jax.shard_map(
        shards,
        mesh=mesh,
        in_specs=placed,
        out_specs=(P("section", "dp", None), P("section", "dp")),
        check_vma=False,
    )
```

```python
import functools
import math

import jax
import jax.numpy as jnp
from jax import lax
from jax.experimental import pallas as pl
from jax.experimental.pallas import tpu as pltpu
from jax.sharding import PartitionSpec as P

eps_norm = 1e-05
lanes = 128
sublanes = 8
pack_rows = 16
tile_width = 512
pair = 2
block_rows = 32
band_width = 256
f32 = jnp.float32
bf16 = jnp.bfloat16
contract_last = (((1,), (1,)), ((), ()))
contract_rows = (((0,), (0,)), ((), ()))
small_cost = pl.CostEstimate(flops=1 << 20, bytes_accessed=1 << 16, transcendentals=0)
roomy = pltpu.CompilerParams(vmem_limit_bytes=32 << 20)
near = pl.BlockSpec(memory_space=pltpu.VMEM)
scalar = pl.BlockSpec(memory_space=pltpu.SMEM)


def far(array):
    return pltpu.with_memory_space_constraint(array, pltpu.HBM)


def cuts(width, step):
    return [pl.ds(at, step) for at in range(0, width, step)]


def one_hot(counts, micro_count, slots, low, size):
    slot = lax.broadcasted_iota(jnp.int32, (slots, size), 0)
    column = lax.broadcasted_iota(jnp.int32, (slots, size), 1) + low
    start = jnp.int32(0)
    pieces = []
    for m in range(micro_count):
        hit = (slot < counts[m]) & (slot + start == column)
        pieces.append(jnp.where(hit, 1.0, 0.0))
        start = start + counts[m]
    return jnp.concatenate(pieces, axis=0).astype(bf16)


def branch_kernel(
    low, counts_far, x_far, top_far, v_far, w_far, gain_far,
    packed, addend, scatter, more, masked, x, back, scale_out, gain,
    counts, top, v, w, sent, ready,
):
    rows, width = addend.shape
    micro_count = counts.shape[0]
    slots = rows // micro_count
    fetches = [
        pltpu.make_async_copy(v_far.at[0], v, ready.at[0]),
        pltpu.make_async_copy(counts_far, counts, ready.at[1]),
        pltpu.make_async_copy(w_far.at[0], w, ready.at[2]),
        pltpu.make_async_copy(x_far.at[0], x, ready.at[3]),
        pltpu.make_async_copy(gain_far, gain, ready.at[4]),
        pltpu.make_async_copy(top_far, top, ready.at[5]),
    ]
    for fetch in fetches:
        fetch.start()
    fetches[0].wait()
    fetches[1].wait()
    slot = lax.broadcasted_iota(jnp.int32, (slots, v.shape[1]), 0)
    for m in range(micro_count):
        piece = v[m * slots : (m + 1) * slots, :]
        masked[m * slots : (m + 1) * slots, :] = jnp.where(slot < counts[m], piece, jnp.zeros_like(piece))
    live = jnp.int32(0)
    for m in range(micro_count):
        live += counts[m]
    more[0] = (live > low + packed.shape[0]).astype(jnp.int32)
    gather = one_hot(counts, micro_count, slots, low, packed.shape[0])
    receives = lax.axis_index("section") < lax.axis_size("section") - 1
    scatter[...] = jnp.where(receives, gather.astype(f32), 0.0).astype(bf16)
    gather = jnp.transpose(gather.astype(f32)).astype(bf16)
    values = masked[...]
    for fetch in fetches[2:5]:
        fetch.wait()
    blocks = [slice(at, at + block_rows) for at in range(0, rows, block_rows)]
    squares = [jnp.zeros((block_rows, lanes), f32) for _ in blocks]
    products = [jnp.zeros((block_rows, lanes), f32) for _ in blocks]
    for tile in range(0, width, band_width):
        here = lax.dot_general(
            values, w[tile : tile + band_width, :], contract_last, preferred_element_type=f32
        )
        back[:, tile : tile + band_width] = here
        for k, part in enumerate(blocks):
            for at in range(0, band_width, lanes):
                cut = pl.ds(tile + at, lanes)
                wide = x[part, cut].astype(f32)
                squares[k] += wide * wide
                products[k] += wide * here[part, at : at + lanes] * gain[:, cut]
    scales = lax.rsqrt(jnp.sum(jnp.concatenate(squares, axis=0), axis=1, keepdims=True) / width + eps_norm)
    pulls = scales * jnp.sum(jnp.concatenate(products, axis=0), axis=1, keepdims=True) / width
    waits = jnp.concatenate(
        [
            lax.broadcasted_iota(jnp.int32, (slots, 1), 0) < jnp.where(receives, counts[m], 0)
            for m in range(micro_count)
        ],
        axis=0,
    )
    spread = (rows, band_width)
    scales = jnp.broadcast_to(scales, spread)
    scale_out[...] = scales[:, :lanes]
    pulls = jnp.broadcast_to(pulls, spread)
    waits = jnp.broadcast_to(waits, spread)
    fetches[5].wait()
    for cut in cuts(width, band_width):
        scaled = gain[:, cut]
        for part in blocks:
            unit = x[part, cut].astype(f32) * scales[part]
            here = back[part, cut]
            own = scales[part] * (scaled * here - unit * pulls[part])
            whole = top[part, cut].astype(f32) + own
            sent[part, cut] = whole.astype(bf16)
            addend[part, cut] = jnp.where(waits[part], own, whole)
        packed[:, cut] = jnp.dot(gather, sent[:, cut], preferred_element_type=f32).astype(bf16)


def branch_rows(low, room, counts, x, top, v, w, gain):
    rows, width = top.shape
    depth = v.shape[2]
    return pl.pallas_call(
        functools.partial(branch_kernel, low),
        in_specs=[pl.BlockSpec(memory_space=pltpu.HBM)] * 6,
        out_specs=[near] * 3 + [scalar] + [near] * 5,
        out_shape=[
            jax.ShapeDtypeStruct((room, width), bf16),
            jax.ShapeDtypeStruct((rows, width), f32),
            jax.ShapeDtypeStruct((rows, room), bf16),
            pltpu.SMEM((1,), jnp.int32),
            jax.ShapeDtypeStruct((rows, depth), bf16),
            jax.ShapeDtypeStruct((rows, width), bf16),
            jax.ShapeDtypeStruct((rows, width), f32),
            jax.ShapeDtypeStruct((rows, lanes), f32),
            jax.ShapeDtypeStruct((1, width), f32),
        ],
        scratch_shapes=[
            pltpu.SMEM(counts.shape, jnp.int32),
            pltpu.VMEM((rows, width), bf16),
            pltpu.VMEM((rows, depth), bf16),
            pltpu.VMEM((width, depth), bf16),
            pltpu.VMEM((rows, width), bf16),
            pltpu.SemaphoreType.DMA((6,)),
        ],
        compiler_params=roomy,
        cost_estimate=small_cost,
    )(*[far(a) for a in (counts, x, top, v, w, gain)])


def pack_kernel(gather, sent, packed):
    for cut in cuts(sent.shape[1], tile_width):
        packed[:, cut] = lax.dot_general(
            gather[...], sent[:, cut], contract_rows, preferred_element_type=f32
        ).astype(bf16)


def pack(gather, sent):
    return pl.pallas_call(
        pack_kernel,
        in_specs=[near, near],
        out_specs=near,
        out_shape=jax.ShapeDtypeStruct((gather.shape[1], sent.shape[1]), bf16),
        compiler_params=roomy,
        cost_estimate=small_cost,
    )(gather, sent)


def receive_kernel(target, first, factor, scatter, received, addend, more, *refs):
    rows, width = addend.shape
    if first:
        *parts, out_far, more_out, owned_far, out, owned, done = refs
    else:
        previous, out_far, more_out, out, done = refs
    more_out[0] = more[0]
    place = scatter[...]
    writes = []
    if first and parts:
        total_rows(factor, owned, *parts)
        writes.append(pltpu.make_async_copy(owned, owned_far, done.at[width // tile_width]))
        writes[0].start()
    if not first:
        here = (lax.axis_index("section") == target).astype(f32)
        covered = jnp.sum(place.astype(f32), axis=1, keepdims=True) * here > 0.5
    for k, cut in enumerate(cuts(width, tile_width)):
        total = jnp.dot(place, received[:, cut], preferred_element_type=f32) + addend[:, cut]
        if not first:
            total = jnp.where(covered, total, previous[:, cut].astype(f32))
        out[:, cut] = total.astype(bf16)
        write = pltpu.make_async_copy(out.at[:, cut], out_far.at[0, :, cut], done.at[k])
        write.start()
        writes.append(write)
    for write in writes:
        write.wait()


def receive(target, scatter, received, addend, more, previous=None, parts=(), owned=lanes, factor=1.0):
    rows, width = addend.shape
    away = pl.BlockSpec(memory_space=pltpu.HBM)
    first = previous is None
    others = parts if first else [previous]
    outs = [pltpu.HBM((1, rows, width), bf16), pltpu.SMEM(more.shape, more.dtype)]
    scratch = [pltpu.VMEM((rows, width), bf16)]
    if first:
        outs.append(pltpu.HBM((1, owned), f32))
        scratch.append(pltpu.VMEM((1, owned), f32))
    return pl.pallas_call(
        functools.partial(receive_kernel, target, first, factor),
        in_specs=[near, near, near, scalar] + [near] * len(others),
        out_specs=[away, scalar] + [away] * first,
        out_shape=outs,
        scratch_shapes=scratch + [pltpu.SemaphoreType.DMA((width // tile_width + 1,))],
        compiler_params=roomy,
        cost_estimate=small_cost,
    )(scatter, received, addend, more, *others)


def terms_kernel(owned_rows, masked, x, back, scale, gain, keep, give, give_low, total):
    rows, width = x.shape
    values = masked[...]
    gain_rows = width // lanes
    spread = jnp.concatenate([scale[...]] * (band_width // lanes), axis=1)
    for at in range(0, width, band_width):
        cut = pl.ds(at, band_width)
        unit = x[:, cut].astype(f32) * spread
        summed = (unit * back[:, cut]).reshape(rows // sublanes, sublanes, band_width).sum(axis=0)
        summed = jnp.sum(summed, axis=0, keepdims=True)
        for k in range(0, band_width, lanes):
            spot = (at + k) // lanes
            total[spot : spot + 1, :] = summed[:, k : k + lanes]
        normed = (unit * gain[:, cut]).astype(bf16)
        total[gain_rows + at : gain_rows + at + band_width, :] = lax.dot_general(
            normed, values, contract_rows, preferred_element_type=f32
        )
    blocks, padded, _ = keep.shape
    cut = give.shape[1]

    def hand_out(side):
        for j in range(blocks):
            mine = (2 * j + side) * owned_rows
            other = (2 * j + 1 - side) * owned_rows
            keep[j, :owned_rows, :] = total[mine : mine + owned_rows, :]
            give[j] = total[other : other + cut, :].astype(bf16)
            low = total[other + cut : other + owned_rows, :]
            if padded > owned_rows:
                blank = jnp.zeros((padded - owned_rows, lanes), f32)
                keep[j, owned_rows:, :] = blank
                low = jnp.concatenate([low, blank], axis=0)
            give_low[j] = low.astype(bf16)

    side = lax.axis_index("dp") % pair
    for core in range(pair):
        pl.when(side == core)(functools.partial(hand_out, core))


def pair_terms(made, owned_rows, owners):
    padded = -(-owned_rows // pack_rows) * pack_rows
    cut = padded // 2 // pack_rows * pack_rows
    blocks = owners // pair
    return pl.pallas_call(
        functools.partial(terms_kernel, owned_rows),
        in_specs=[near] * len(made),
        out_specs=[near, near, near],
        out_shape=[
            jax.ShapeDtypeStruct((blocks, padded, lanes), f32),
            jax.ShapeDtypeStruct((blocks, cut, lanes), bf16),
            jax.ShapeDtypeStruct((blocks, padded - cut, lanes), bf16),
        ],
        scratch_shapes=[pltpu.VMEM((owners * owned_rows, lanes), f32)],
        compiler_params=roomy,
        cost_estimate=small_cost,
    )(*made)


def merge_kernel(offsets, direct, keep, taken, taken_low, hold, give, *straight):
    chip = lax.axis_index("dp") // pair
    mine, place = chip % 2, chip // 2
    count = keep.shape[0] // 2
    cut = taken.shape[1]

    def total(at, out):
        high = keep[at, :cut, :] + taken[at].astype(f32)
        low = keep[at, cut:, :] + taken_low[at].astype(f32)
        out[:cut, :] = high.astype(out.dtype)
        out[cut:, :] = low.astype(out.dtype)

    for k, offset in enumerate(offsets):
        at = 2 * lax.rem(place + offset, count)
        total(at + mine, hold.at[k])
        total(at + 1 - mine, give.at[k])
    for k, offset in enumerate(direct):
        at = 2 * lax.rem(place + offset, count)
        total(at + mine, straight[2 * k])
        total(at + 1 - mine, straight[2 * k + 1])


def merge_terms(offsets, direct, keep, taken, taken_low):
    block = keep.shape[1:]
    outs = [
        jax.ShapeDtypeStruct((len(offsets),) + block, f32),
        jax.ShapeDtypeStruct((len(offsets),) + block, bf16),
    ] + [jax.ShapeDtypeStruct(block, bf16)] * (2 * len(direct))
    return pl.pallas_call(
        functools.partial(merge_kernel, offsets, direct),
        in_specs=[near, near, near],
        out_specs=[near] * len(outs),
        out_shape=outs,
        compiler_params=roomy,
        cost_estimate=small_cost,
    )(keep, taken, taken_low)


def split_kernel(hold, taken, *parts):
    for k, part in enumerate(parts):
        part[...] = (hold[k] + taken[k].astype(f32)).astype(part.dtype)


def split_terms(part, hold, taken):
    return pl.pallas_call(
        split_kernel,
        in_specs=[near, near],
        out_specs=[near] * len(part),
        out_shape=[jax.ShapeDtypeStruct(hold.shape[1:], bf16 if offset else f32) for offset in part],
        compiler_params=roomy,
        cost_estimate=small_cost,
    )(hold, taken)


def total_rows(factor, out, own, *landed):
    total = own[...]
    for part in landed:
        total += part[...].astype(f32)
    total = total * factor
    for k in range(out.shape[1] // lanes):
        out[:, k * lanes : (k + 1) * lanes] = total[k : k + 1, :]


def plane_parts(owners, keep, *taken):
    quad = 2 * pair
    count = owners // quad
    direct = [1] if count > 2 else []
    offsets = [k for k in range(count) if k not in direct]

    def along(offset, side):
        return [(i, (i + quad * offset) % owners ^ pair * side) for i in range(owners)]

    hold, give, *straight = merge_terms(offsets, direct, keep, *taken)
    across = lax.ppermute(give, "dp", along(0, 1))
    arrived = [
        lax.ppermute(straight[2 * k + side], "dp", along(offset, side))
        for k, offset in enumerate(direct)
        for side in range(2)
    ]
    own, *parts = split_terms(offsets, hold, across)
    for offset, part in zip(offsets[1:], parts):
        arrived.append(lax.ppermute(part, "dp", along(offset, 0)))
    return own, *arrived


def weight_owned(made, factor):
    owners = lax.axis_size("dp")
    masked, x, back, scale, gain = made
    width = x.shape[1]
    depth = masked.shape[1]
    owned = (width + width * depth) // owners
    if depth != lanes or owned % lanes or owners % (2 * pair):
        unit = x.astype(f32) * scale[:, :1]
        normed = (unit * gain).astype(bf16)
        weight_term = lax.dot_general(normed, masked, contract_rows, preferred_element_type=f32)
        flat = jnp.concatenate([jnp.sum(unit * back, axis=0), weight_term.reshape(-1)]) * factor
        return (), owned, lax.psum_scatter(flat, "dp", scatter_dimension=0, tiled=True)[None, :]
    keep, *give = pair_terms(made, owned // lanes, owners)
    taken = [lax.ppermute(part, "dp", [(i, i ^ 1) for i in range(owners)]) for part in give]
    return plane_parts(owners, keep, *taken), owned, None


def shards(layer_inputs, top_grad, value_grads, weights, norm_gains, counts):
    rows = layer_inputs.shape[1]
    factor = 1.0 / math.sqrt(rows * lax.axis_size("dp"))
    sections = lax.axis_size("section")
    room = -(-rows * 3 // 4 // pack_rows) * pack_rows
    spare = rows - room
    inputs = (counts, layer_inputs, top_grad, value_grads, weights, norm_gains)
    packed, addend, scatter, more, *made = branch_rows(0, room, *inputs)
    parts, owned_size, owned = weight_owned(made, factor)
    result = None
    for hop in range(sections - 1):
        target = sections - 2 - hop
        hops = [(target + 1, target), (target, target + 1)]
        before = result
        if hop:
            packed = pack(scatter, before)
        landed = lax.ppermute(packed, "section", hops)
        if hop:
            updated, more = receive(target, scatter, landed, addend, more, before)
        else:
            updated, more, summed = receive(target, scatter, landed, addend, more, None, parts, owned_size, factor)

        def rest(updated):
            packed, addend, scatter, more, *_ = branch_rows(room, spare, *inputs)
            if hop:
                packed = pack(scatter, before)
            landed = lax.ppermute(packed, "section", hops)
            return receive(target, scatter, landed, addend, more, updated[0])[0]

        updated = lax.cond(more.reshape(()) > 0, rest, lambda updated: updated, updated)
        result = updated[0]
    return (result[None], summed if owned is None else owned)


def solution(mesh):
    placed = (
        P("section", "dp", None),
        P("dp", None),
        P("section", "dp", None),
        P("section", None, None),
        P("section", None),
        P("dp"),
    )
    return jax.shard_map(
        shards,
        mesh=mesh,
        in_specs=placed,
        out_specs=(P("section", "dp", None), P("section", "dp")),
        check_vma=False,
    )
```

```python
import functools
import math

import jax
import jax.numpy as jnp
from jax import lax
from jax.experimental import pallas as pl
from jax.experimental.pallas import tpu as pltpu
from jax.sharding import PartitionSpec as P

eps_norm = 1e-05
lanes = 128
sublanes = 8
pack_rows = 16
tile_width = 512
pair = 2
block_rows = 32
band_width = 256
f32 = jnp.float32
bf16 = jnp.bfloat16
contract_last = (((1,), (1,)), ((), ()))
contract_rows = (((0,), (0,)), ((), ()))
small_cost = pl.CostEstimate(flops=1 << 20, bytes_accessed=1 << 16, transcendentals=0)
roomy = pltpu.CompilerParams(vmem_limit_bytes=32 << 20)
near = pl.BlockSpec(memory_space=pltpu.VMEM)
scalar = pl.BlockSpec(memory_space=pltpu.SMEM)


def far(array):
    return pltpu.with_memory_space_constraint(array, pltpu.HBM)


def cuts(width, step):
    return [pl.ds(at, step) for at in range(0, width, step)]


def one_hot(counts, micro_count, slots, low, size):
    slot = lax.broadcasted_iota(jnp.int32, (slots, size), 0)
    column = lax.broadcasted_iota(jnp.int32, (slots, size), 1) + low
    start = jnp.int32(0)
    pieces = []
    for m in range(micro_count):
        hit = (slot < counts[m]) & (slot + start == column)
        pieces.append(jnp.where(hit, 1.0, 0.0))
        start = start + counts[m]
    return jnp.concatenate(pieces, axis=0).astype(bf16)


def branch_kernel(
    low, counts_far, x_far, top_far, v_far, w_far, gain_far,
    packed, addend, scatter, more, masked, x, back, scale_out, gain,
    counts, top, v, w, sent, ready,
):
    rows, width = addend.shape
    micro_count = counts.shape[0]
    slots = rows // micro_count
    fetches = [
        pltpu.make_async_copy(v_far.at[0], v, ready.at[0]),
        pltpu.make_async_copy(counts_far, counts, ready.at[1]),
        pltpu.make_async_copy(w_far.at[0], w, ready.at[2]),
        pltpu.make_async_copy(x_far.at[0], x, ready.at[3]),
        pltpu.make_async_copy(gain_far, gain, ready.at[4]),
        pltpu.make_async_copy(top_far, top, ready.at[5]),
    ]
    for fetch in fetches:
        fetch.start()
    fetches[0].wait()
    fetches[1].wait()
    slot = lax.broadcasted_iota(jnp.int32, (slots, v.shape[1]), 0)
    for m in range(micro_count):
        piece = v[m * slots : (m + 1) * slots, :]
        masked[m * slots : (m + 1) * slots, :] = jnp.where(slot < counts[m], piece, jnp.zeros_like(piece))
    live = jnp.int32(0)
    for m in range(micro_count):
        live += counts[m]
    more[0] = (live > low + packed.shape[0]).astype(jnp.int32)
    gather = one_hot(counts, micro_count, slots, low, packed.shape[0])
    receives = lax.axis_index("section") < lax.axis_size("section") - 1
    scatter[...] = jnp.where(receives, gather.astype(f32), 0.0).astype(bf16)
    gather = jnp.transpose(gather.astype(f32)).astype(bf16)
    values = masked[...]
    for fetch in fetches[2:5]:
        fetch.wait()
    blocks = [slice(at, at + block_rows) for at in range(0, rows, block_rows)]
    squares = [jnp.zeros((block_rows, lanes), f32) for _ in blocks]
    products = [jnp.zeros((block_rows, lanes), f32) for _ in blocks]
    for tile in range(0, width, band_width):
        here = lax.dot_general(
            values, w[tile : tile + band_width, :], contract_last, preferred_element_type=f32
        )
        back[:, tile : tile + band_width] = here
        for k, part in enumerate(blocks):
            for at in range(0, band_width, lanes):
                cut = pl.ds(tile + at, lanes)
                wide = x[part, cut].astype(f32)
                squares[k] += wide * wide
                products[k] += wide * here[part, at : at + lanes] * gain[:, cut]
    scales = lax.rsqrt(jnp.sum(jnp.concatenate(squares, axis=0), axis=1, keepdims=True) / width + eps_norm)
    pulls = scales * jnp.sum(jnp.concatenate(products, axis=0), axis=1, keepdims=True) / width
    waits = jnp.concatenate(
        [
            lax.broadcasted_iota(jnp.int32, (slots, 1), 0) < jnp.where(receives, counts[m], 0)
            for m in range(micro_count)
        ],
        axis=0,
    )
    spread = (rows, lanes)
    scales = jnp.broadcast_to(scales, spread)
    scale_out[...] = scales
    pulls = jnp.broadcast_to(scales[:, :1] * pulls, spread)
    waits = jnp.broadcast_to(waits, spread)
    fetches[5].wait()
    for band in cuts(width, band_width):
        for part in blocks:
            scale, pull, wait = scales[part], pulls[part], waits[part]
            for at in range(0, band_width, lanes):
                cut = pl.ds(band.start + at, lanes)
                unit = x[part, cut].astype(f32) * scale
                own = scale * (gain[:, cut] * back[part, cut]) - unit * pull
                whole = top[part, cut].astype(f32) + own
                sent[part, cut] = whole.astype(bf16)
                addend[part, cut] = jnp.where(wait, own, whole)
        packed[:, band] = jnp.dot(gather, sent[:, band], preferred_element_type=f32).astype(bf16)


def branch_rows(low, room, counts, x, top, v, w, gain):
    rows, width = top.shape
    depth = v.shape[2]
    return pl.pallas_call(
        functools.partial(branch_kernel, low),
        in_specs=[pl.BlockSpec(memory_space=pltpu.HBM)] * 6,
        out_specs=[near] * 3 + [scalar] + [near] * 5,
        out_shape=[
            jax.ShapeDtypeStruct((room, width), bf16),
            jax.ShapeDtypeStruct((rows, width), f32),
            jax.ShapeDtypeStruct((rows, room), bf16),
            pltpu.SMEM((1,), jnp.int32),
            jax.ShapeDtypeStruct((rows, depth), bf16),
            jax.ShapeDtypeStruct((rows, width), bf16),
            jax.ShapeDtypeStruct((rows, width), f32),
            jax.ShapeDtypeStruct((rows, lanes), f32),
            jax.ShapeDtypeStruct((1, width), f32),
        ],
        scratch_shapes=[
            pltpu.SMEM(counts.shape, jnp.int32),
            pltpu.VMEM((rows, width), bf16),
            pltpu.VMEM((rows, depth), bf16),
            pltpu.VMEM((width, depth), bf16),
            pltpu.VMEM((rows, width), bf16),
            pltpu.SemaphoreType.DMA((6,)),
        ],
        compiler_params=roomy,
        cost_estimate=small_cost,
    )(*[far(a) for a in (counts, x, top, v, w, gain)])


def pack_kernel(gather, sent, packed):
    for cut in cuts(sent.shape[1], tile_width):
        packed[:, cut] = lax.dot_general(
            gather[...], sent[:, cut], contract_rows, preferred_element_type=f32
        ).astype(bf16)


def pack(gather, sent):
    return pl.pallas_call(
        pack_kernel,
        in_specs=[near, near],
        out_specs=near,
        out_shape=jax.ShapeDtypeStruct((gather.shape[1], sent.shape[1]), bf16),
        compiler_params=roomy,
        cost_estimate=small_cost,
    )(gather, sent)


def receive_kernel(target, first, factor, scatter, received, addend, more, *refs):
    rows, width = addend.shape
    if first:
        *parts, out_far, more_out, owned_far, out, owned, done = refs
    else:
        previous, out_far, more_out, out, done = refs
    more_out[0] = more[0]
    place = scatter[...]
    writes = []
    if first and parts:
        total_rows(factor, owned, *parts)
        writes.append(pltpu.make_async_copy(owned, owned_far, done.at[width // tile_width]))
        writes[0].start()
    if not first:
        here = (lax.axis_index("section") == target).astype(f32)
        covered = jnp.sum(place.astype(f32), axis=1, keepdims=True) * here > 0.5
    for k, cut in enumerate(cuts(width, tile_width)):
        total = jnp.dot(place, received[:, cut], preferred_element_type=f32) + addend[:, cut]
        if not first:
            total = jnp.where(covered, total, previous[:, cut].astype(f32))
        out[:, cut] = total.astype(bf16)
        write = pltpu.make_async_copy(out.at[:, cut], out_far.at[0, :, cut], done.at[k])
        write.start()
        writes.append(write)
    for write in writes:
        write.wait()


def receive(target, scatter, received, addend, more, previous=None, parts=(), owned=lanes, factor=1.0):
    rows, width = addend.shape
    away = pl.BlockSpec(memory_space=pltpu.HBM)
    first = previous is None
    others = parts if first else [previous]
    outs = [pltpu.HBM((1, rows, width), bf16), pltpu.SMEM(more.shape, more.dtype)]
    scratch = [pltpu.VMEM((rows, width), bf16)]
    if first:
        outs.append(pltpu.HBM((1, owned), f32))
        scratch.append(pltpu.VMEM((1, owned), f32))
    return pl.pallas_call(
        functools.partial(receive_kernel, target, first, factor),
        in_specs=[near, near, near, scalar] + [near] * len(others),
        out_specs=[away, scalar] + [away] * first,
        out_shape=outs,
        scratch_shapes=scratch + [pltpu.SemaphoreType.DMA((width // tile_width + 1,))],
        compiler_params=roomy,
        cost_estimate=small_cost,
    )(scatter, received, addend, more, *others)


def terms_kernel(owned_rows, masked, x, back, scale, gain, keep, give, give_low, total):
    rows, width = x.shape
    values = masked[...]
    gain_rows = width // lanes
    spread = jnp.concatenate([scale[...]] * (band_width // lanes), axis=1)
    for at in range(0, width, band_width):
        cut = pl.ds(at, band_width)
        unit = x[:, cut].astype(f32) * spread
        summed = (unit * back[:, cut]).reshape(rows // sublanes, sublanes, band_width).sum(axis=0)
        summed = jnp.sum(summed, axis=0, keepdims=True)
        for k in range(0, band_width, lanes):
            spot = (at + k) // lanes
            total[spot : spot + 1, :] = summed[:, k : k + lanes]
        normed = (unit * gain[:, cut]).astype(bf16)
        total[gain_rows + at : gain_rows + at + band_width, :] = lax.dot_general(
            normed, values, contract_rows, preferred_element_type=f32
        )
    blocks, padded, _ = keep.shape
    cut = give.shape[1]

    def hand_out(side):
        for j in range(blocks):
            mine = (2 * j + side) * owned_rows
            other = (2 * j + 1 - side) * owned_rows
            keep[j, :owned_rows, :] = total[mine : mine + owned_rows, :]
            give[j] = total[other : other + cut, :].astype(bf16)
            low = total[other + cut : other + owned_rows, :]
            if padded > owned_rows:
                blank = jnp.zeros((padded - owned_rows, lanes), f32)
                keep[j, owned_rows:, :] = blank
                low = jnp.concatenate([low, blank], axis=0)
            give_low[j] = low.astype(bf16)

    side = lax.axis_index("dp") % pair
    for core in range(pair):
        pl.when(side == core)(functools.partial(hand_out, core))


def pair_terms(made, owned_rows, owners):
    padded = -(-owned_rows // pack_rows) * pack_rows
    cut = padded // 2 // pack_rows * pack_rows
    blocks = owners // pair
    return pl.pallas_call(
        functools.partial(terms_kernel, owned_rows),
        in_specs=[near] * len(made),
        out_specs=[near, near, near],
        out_shape=[
            jax.ShapeDtypeStruct((blocks, padded, lanes), f32),
            jax.ShapeDtypeStruct((blocks, cut, lanes), bf16),
            jax.ShapeDtypeStruct((blocks, padded - cut, lanes), bf16),
        ],
        scratch_shapes=[pltpu.VMEM((owners * owned_rows, lanes), f32)],
        compiler_params=roomy,
        cost_estimate=small_cost,
    )(*made)


def merge_kernel(offsets, direct, keep, taken, taken_low, hold, give, *straight):
    chip = lax.axis_index("dp") // pair
    mine, place = chip % 2, chip // 2
    count = keep.shape[0] // 2
    cut = taken.shape[1]

    def total(at, out):
        high = keep[at, :cut, :] + taken[at].astype(f32)
        low = keep[at, cut:, :] + taken_low[at].astype(f32)
        out[:cut, :] = high.astype(out.dtype)
        out[cut:, :] = low.astype(out.dtype)

    for k, offset in enumerate(offsets):
        at = 2 * lax.rem(place + offset, count)
        total(at + mine, hold.at[k])
        total(at + 1 - mine, give.at[k])
    for k, offset in enumerate(direct):
        at = 2 * lax.rem(place + offset, count)
        total(at + mine, straight[2 * k])
        total(at + 1 - mine, straight[2 * k + 1])


def merge_terms(offsets, direct, keep, taken, taken_low):
    block = keep.shape[1:]
    outs = [
        jax.ShapeDtypeStruct((len(offsets),) + block, f32),
        jax.ShapeDtypeStruct((len(offsets),) + block, bf16),
    ] + [jax.ShapeDtypeStruct(block, bf16)] * (2 * len(direct))
    return pl.pallas_call(
        functools.partial(merge_kernel, offsets, direct),
        in_specs=[near, near, near],
        out_specs=[near] * len(outs),
        out_shape=outs,
        compiler_params=roomy,
        cost_estimate=small_cost,
    )(keep, taken, taken_low)


def split_kernel(hold, taken, *parts):
    for k, part in enumerate(parts):
        part[...] = (hold[k] + taken[k].astype(f32)).astype(part.dtype)


def split_terms(part, hold, taken):
    return pl.pallas_call(
        split_kernel,
        in_specs=[near, near],
        out_specs=[near] * len(part),
        out_shape=[jax.ShapeDtypeStruct(hold.shape[1:], bf16 if offset else f32) for offset in part],
        compiler_params=roomy,
        cost_estimate=small_cost,
    )(hold, taken)


def total_rows(factor, out, own, *landed):
    total = own[...]
    for part in landed:
        total += part[...].astype(f32)
    total = total * factor
    for k in range(out.shape[1] // lanes):
        out[:, k * lanes : (k + 1) * lanes] = total[k : k + 1, :]


def plane_parts(owners, keep, *taken):
    quad = 2 * pair
    count = owners // quad
    direct = [count // 2] if count > 2 else []
    offsets = [k for k in range(count) if k not in direct]

    def along(offset, side):
        return [(i, (i + quad * offset) % owners ^ pair * side) for i in range(owners)]

    hold, give, *straight = merge_terms(offsets, direct, keep, *taken)
    across = lax.ppermute(give, "dp", along(0, 1))
    arrived = [
        lax.ppermute(straight[2 * k + side], "dp", along(offset, side))
        for k, offset in enumerate(direct)
        for side in range(2)
    ]
    own, *parts = split_terms(offsets, hold, across)
    for offset, part in zip(offsets[1:], parts):
        arrived.append(lax.ppermute(part, "dp", along(offset, 0)))
    return own, *arrived


def weight_owned(made, factor):
    owners = lax.axis_size("dp")
    masked, x, back, scale, gain = made
    width = x.shape[1]
    depth = masked.shape[1]
    owned = (width + width * depth) // owners
    if depth != lanes or owned % lanes or owners % (2 * pair):
        unit = x.astype(f32) * scale[:, :1]
        normed = (unit * gain).astype(bf16)
        weight_term = lax.dot_general(normed, masked, contract_rows, preferred_element_type=f32)
        flat = jnp.concatenate([jnp.sum(unit * back, axis=0), weight_term.reshape(-1)]) * factor
        return (), owned, lax.psum_scatter(flat, "dp", scatter_dimension=0, tiled=True)[None, :]
    keep, *give = pair_terms(made, owned // lanes, owners)
    taken = [lax.ppermute(part, "dp", [(i, i ^ 1) for i in range(owners)]) for part in give]
    return plane_parts(owners, keep, *taken), owned, None


def shards(layer_inputs, top_grad, value_grads, weights, norm_gains, counts):
    rows = layer_inputs.shape[1]
    factor = 1.0 / math.sqrt(rows * lax.axis_size("dp"))
    sections = lax.axis_size("section")
    room = -(-rows * 3 // 4 // pack_rows) * pack_rows
    spare = rows - room
    inputs = (counts, layer_inputs, top_grad, value_grads, weights, norm_gains)
    packed, addend, scatter, more, *made = branch_rows(0, room, *inputs)
    parts, owned_size, owned = weight_owned(made, factor)
    result = None
    for hop in range(sections - 1):
        target = sections - 2 - hop
        hops = [(target + 1, target), (target, target + 1)]
        before = result
        if hop:
            packed = pack(scatter, before)
        landed = lax.ppermute(packed, "section", hops)
        if hop:
            updated, more = receive(target, scatter, landed, addend, more, before)
        else:
            updated, more, summed = receive(target, scatter, landed, addend, more, None, parts, owned_size, factor)

        def rest(updated):
            packed, addend, scatter, more, *_ = branch_rows(room, spare, *inputs)
            if hop:
                packed = pack(scatter, before)
            landed = lax.ppermute(packed, "section", hops)
            return receive(target, scatter, landed, addend, more, updated[0])[0]

        updated = lax.cond(more.reshape(()) > 0, rest, lambda updated: updated, updated)
        result = updated[0]
    return (result[None], summed if owned is None else owned)


def solution(mesh):
    placed = (
        P("section", "dp", None),
        P("dp", None),
        P("section", "dp", None),
        P("section", None, None),
        P("section", None),
        P("dp"),
    )
    return jax.shard_map(
        shards,
        mesh=mesh,
        in_specs=placed,
        out_specs=(P("section", "dp", None), P("section", "dp")),
        check_vma=False,
    )
```

```python
import functools
import math

import jax
import jax.numpy as jnp
from jax import lax
from jax.experimental import pallas as pl
from jax.experimental.pallas import tpu as pltpu
from jax.sharding import PartitionSpec as P

eps_norm = 1e-05
lanes = 128
sublanes = 8
pack_rows = 16
tile_width = 512
pair = 2
block_rows = 32
band_width = 256
f32 = jnp.float32
bf16 = jnp.bfloat16
contract_last = (((1,), (1,)), ((), ()))
contract_rows = (((0,), (0,)), ((), ()))
small_cost = pl.CostEstimate(flops=1 << 20, bytes_accessed=1 << 16, transcendentals=0)
roomy = pltpu.CompilerParams(vmem_limit_bytes=32 << 20)
near = pl.BlockSpec(memory_space=pltpu.VMEM)
scalar = pl.BlockSpec(memory_space=pltpu.SMEM)


def far(array):
    return pltpu.with_memory_space_constraint(array, pltpu.HBM)


def cuts(width, step):
    return [pl.ds(at, step) for at in range(0, width, step)]


def one_hot(counts, micro_count, slots, low, size):
    slot = lax.broadcasted_iota(jnp.int32, (slots, size), 0)
    column = lax.broadcasted_iota(jnp.int32, (slots, size), 1) + low
    start = jnp.int32(0)
    pieces = []
    for m in range(micro_count):
        hit = (slot < counts[m]) & (slot + start == column)
        pieces.append(jnp.where(hit, 1.0, 0.0))
        start = start + counts[m]
    return jnp.concatenate(pieces, axis=0).astype(bf16)


def branch_kernel(
    low, counts_far, x_far, top_far, v_far, w_far, gain_far,
    packed, addend, scatter, more, masked, x, back, scale_out, gain,
    counts, top, v, w, sent, ready,
):
    rows, width = addend.shape
    micro_count = counts.shape[0]
    slots = rows // micro_count
    fetches = [
        pltpu.make_async_copy(v_far.at[0], v, ready.at[0]),
        pltpu.make_async_copy(counts_far, counts, ready.at[1]),
        pltpu.make_async_copy(w_far.at[0], w, ready.at[2]),
        pltpu.make_async_copy(x_far.at[0], x, ready.at[3]),
        pltpu.make_async_copy(gain_far, gain, ready.at[4]),
        pltpu.make_async_copy(top_far, top, ready.at[5]),
    ]
    for fetch in fetches:
        fetch.start()
    fetches[0].wait()
    fetches[1].wait()
    slot = lax.broadcasted_iota(jnp.int32, (slots, v.shape[1]), 0)
    for m in range(micro_count):
        piece = v[m * slots : (m + 1) * slots, :]
        masked[m * slots : (m + 1) * slots, :] = jnp.where(slot < counts[m], piece, jnp.zeros_like(piece))
    live = jnp.int32(0)
    for m in range(micro_count):
        live += counts[m]
    more[0] = (live > low + packed.shape[0]).astype(jnp.int32)
    gather = one_hot(counts, micro_count, slots, low, packed.shape[0])
    receives = lax.axis_index("section") < lax.axis_size("section") - 1
    scatter[...] = jnp.where(receives, gather.astype(f32), 0.0).astype(bf16)
    gather = jnp.transpose(gather.astype(f32)).astype(bf16)
    values = masked[...]
    for fetch in fetches[2:5]:
        fetch.wait()
    blocks = [slice(at, at + block_rows) for at in range(0, rows, block_rows)]
    squares = [jnp.zeros((block_rows, lanes), f32) for _ in blocks]
    products = [jnp.zeros((block_rows, lanes), f32) for _ in blocks]
    for tile in range(0, width, band_width):
        here = lax.dot_general(
            values, w[tile : tile + band_width, :], contract_last, preferred_element_type=f32
        )
        back[:, tile : tile + band_width] = here
        for k, part in enumerate(blocks):
            for at in range(0, band_width, lanes):
                cut = pl.ds(tile + at, lanes)
                wide = x[part, cut].astype(f32)
                squares[k] += wide * wide
                products[k] += wide * here[part, at : at + lanes] * gain[:, cut]
    scales = lax.rsqrt(jnp.sum(jnp.concatenate(squares, axis=0), axis=1, keepdims=True) / width + eps_norm)
    pulls = scales * jnp.sum(jnp.concatenate(products, axis=0), axis=1, keepdims=True) / width
    waits = jnp.concatenate(
        [
            lax.broadcasted_iota(jnp.int32, (slots, 1), 0) < jnp.where(receives, counts[m], 0)
            for m in range(micro_count)
        ],
        axis=0,
    )
    spread = (rows, tile_width)
    scales = jnp.broadcast_to(scales, spread)
    scale_out[...] = scales[:, :lanes]
    pulls = jnp.broadcast_to(pulls, spread)
    waits = jnp.broadcast_to(waits, spread)
    fetches[5].wait()
    for cut in cuts(width, tile_width):
        scaled = gain[:, cut]
        for part in blocks:
            unit = x[part, cut].astype(f32) * scales[part]
            here = back[part, cut]
            own = scales[part] * (scaled * here - unit * pulls[part])
            whole = top[part, cut].astype(f32) + own
            sent[part, cut] = whole.astype(bf16)
            addend[part, cut] = jnp.where(waits[part], own, whole)
        packed[:, cut] = jnp.dot(gather, sent[:, cut], preferred_element_type=f32).astype(bf16)


def branch_rows(low, room, counts, x, top, v, w, gain):
    rows, width = top.shape
    depth = v.shape[2]
    return pl.pallas_call(
        functools.partial(branch_kernel, low),
        in_specs=[pl.BlockSpec(memory_space=pltpu.HBM)] * 6,
        out_specs=[near] * 3 + [scalar] + [near] * 5,
        out_shape=[
            jax.ShapeDtypeStruct((room, width), bf16),
            jax.ShapeDtypeStruct((rows, width), f32),
            jax.ShapeDtypeStruct((rows, room), bf16),
            pltpu.SMEM((1,), jnp.int32),
            jax.ShapeDtypeStruct((rows, depth), bf16),
            jax.ShapeDtypeStruct((rows, width), bf16),
            jax.ShapeDtypeStruct((rows, width), f32),
            jax.ShapeDtypeStruct((rows, lanes), f32),
            jax.ShapeDtypeStruct((1, width), f32),
        ],
        scratch_shapes=[
            pltpu.SMEM(counts.shape, jnp.int32),
            pltpu.VMEM((rows, width), bf16),
            pltpu.VMEM((rows, depth), bf16),
            pltpu.VMEM((width, depth), bf16),
            pltpu.VMEM((rows, width), bf16),
            pltpu.SemaphoreType.DMA((6,)),
        ],
        compiler_params=roomy,
        cost_estimate=small_cost,
    )(*[far(a) for a in (counts, x, top, v, w, gain)])


def pack_kernel(gather, sent, packed):
    for cut in cuts(sent.shape[1], tile_width):
        packed[:, cut] = lax.dot_general(
            gather[...], sent[:, cut], contract_rows, preferred_element_type=f32
        ).astype(bf16)


def pack(gather, sent):
    return pl.pallas_call(
        pack_kernel,
        in_specs=[near, near],
        out_specs=near,
        out_shape=jax.ShapeDtypeStruct((gather.shape[1], sent.shape[1]), bf16),
        compiler_params=roomy,
        cost_estimate=small_cost,
    )(gather, sent)


def receive_kernel(target, first, factor, scatter, received, addend, more, *refs):
    rows, width = addend.shape
    if first:
        *parts, out_far, more_out, owned_far, out, owned, done = refs
    else:
        previous, out_far, more_out, out, done = refs
    more_out[0] = more[0]
    place = scatter[...]
    writes = []
    if first and parts:
        total_rows(factor, owned, *parts)
        writes.append(pltpu.make_async_copy(owned, owned_far, done.at[width // tile_width]))
        writes[0].start()
    if not first:
        here = (lax.axis_index("section") == target).astype(f32)
        covered = jnp.sum(place.astype(f32), axis=1, keepdims=True) * here > 0.5
    for k, cut in enumerate(cuts(width, tile_width)):
        total = jnp.dot(place, received[:, cut], preferred_element_type=f32) + addend[:, cut]
        if not first:
            total = jnp.where(covered, total, previous[:, cut].astype(f32))
        out[:, cut] = total.astype(bf16)
        write = pltpu.make_async_copy(out.at[:, cut], out_far.at[0, :, cut], done.at[k])
        write.start()
        writes.append(write)
    for write in writes:
        write.wait()


def receive(target, scatter, received, addend, more, previous=None, parts=(), owned=lanes, factor=1.0):
    rows, width = addend.shape
    away = pl.BlockSpec(memory_space=pltpu.HBM)
    first = previous is None
    others = parts if first else [previous]
    outs = [pltpu.HBM((1, rows, width), bf16), pltpu.SMEM(more.shape, more.dtype)]
    scratch = [pltpu.VMEM((rows, width), bf16)]
    if first:
        outs.append(pltpu.HBM((1, owned), f32))
        scratch.append(pltpu.VMEM((1, owned), f32))
    return pl.pallas_call(
        functools.partial(receive_kernel, target, first, factor),
        in_specs=[near, near, near, scalar] + [near] * len(others),
        out_specs=[away, scalar] + [away] * first,
        out_shape=outs,
        scratch_shapes=scratch + [pltpu.SemaphoreType.DMA((width // tile_width + 1,))],
        compiler_params=roomy,
        cost_estimate=small_cost,
    )(scatter, received, addend, more, *others)


def terms_kernel(owned_rows, masked, x, back, scale, gain, keep, give, give_low, total):
    rows, width = x.shape
    values = masked[...]
    gain_rows = width // lanes
    spread = jnp.concatenate([scale[...]] * (band_width // lanes), axis=1)
    for at in range(0, width, band_width):
        cut = pl.ds(at, band_width)
        unit = x[:, cut].astype(f32) * spread
        summed = (unit * back[:, cut]).reshape(rows // sublanes, sublanes, band_width).sum(axis=0)
        summed = jnp.sum(summed, axis=0, keepdims=True)
        for k in range(0, band_width, lanes):
            spot = (at + k) // lanes
            total[spot : spot + 1, :] = summed[:, k : k + lanes]
        normed = (unit * gain[:, cut]).astype(bf16)
        total[gain_rows + at : gain_rows + at + band_width, :] = lax.dot_general(
            normed, values, contract_rows, preferred_element_type=f32
        )
    blocks, padded, _ = keep.shape
    cut = give.shape[1]

    def hand_out(side):
        for j in range(blocks):
            mine = (2 * j + side) * owned_rows
            other = (2 * j + 1 - side) * owned_rows
            keep[j, :owned_rows, :] = total[mine : mine + owned_rows, :]
            give[j] = total[other : other + cut, :].astype(bf16)
            low = total[other + cut : other + owned_rows, :]
            if padded > owned_rows:
                blank = jnp.zeros((padded - owned_rows, lanes), f32)
                keep[j, owned_rows:, :] = blank
                low = jnp.concatenate([low, blank], axis=0)
            give_low[j] = low.astype(bf16)

    side = lax.axis_index("dp") % pair
    for core in range(pair):
        pl.when(side == core)(functools.partial(hand_out, core))


def pair_terms(made, owned_rows, owners):
    padded = -(-owned_rows // pack_rows) * pack_rows
    cut = padded // 2 // pack_rows * pack_rows
    blocks = owners // pair
    return pl.pallas_call(
        functools.partial(terms_kernel, owned_rows),
        in_specs=[near] * len(made),
        out_specs=[near, near, near],
        out_shape=[
            jax.ShapeDtypeStruct((blocks, padded, lanes), f32),
            jax.ShapeDtypeStruct((blocks, cut, lanes), bf16),
            jax.ShapeDtypeStruct((blocks, padded - cut, lanes), bf16),
        ],
        scratch_shapes=[pltpu.VMEM((owners * owned_rows, lanes), f32)],
        compiler_params=roomy,
        cost_estimate=small_cost,
    )(*made)


def merge_kernel(offsets, direct, keep, taken, taken_low, hold, give, *straight):
    chip = lax.axis_index("dp") // pair
    mine, place = chip % 2, chip // 2
    count = keep.shape[0] // 2
    cut = taken.shape[1]

    def total(at, out):
        high = keep[at, :cut, :] + taken[at].astype(f32)
        low = keep[at, cut:, :] + taken_low[at].astype(f32)
        out[:cut, :] = high.astype(out.dtype)
        out[cut:, :] = low.astype(out.dtype)

    for k, offset in enumerate(offsets):
        at = 2 * lax.rem(place + offset, count)
        total(at + mine, hold.at[k])
        total(at + 1 - mine, give.at[k])
    for k, offset in enumerate(direct):
        at = 2 * lax.rem(place + offset, count)
        total(at + mine, straight[2 * k])
        total(at + 1 - mine, straight[2 * k + 1])


def merge_terms(offsets, direct, keep, taken, taken_low):
    block = keep.shape[1:]
    outs = [
        jax.ShapeDtypeStruct((len(offsets),) + block, f32),
        jax.ShapeDtypeStruct((len(offsets),) + block, bf16),
    ] + [jax.ShapeDtypeStruct(block, bf16)] * (2 * len(direct))
    return pl.pallas_call(
        functools.partial(merge_kernel, offsets, direct),
        in_specs=[near, near, near],
        out_specs=[near] * len(outs),
        out_shape=outs,
        compiler_params=roomy,
        cost_estimate=small_cost,
    )(keep, taken, taken_low)


def split_kernel(hold, taken, *parts):
    for k, part in enumerate(parts):
        part[...] = (hold[k] + taken[k].astype(f32)).astype(part.dtype)


def split_terms(part, hold, taken):
    return pl.pallas_call(
        split_kernel,
        in_specs=[near, near],
        out_specs=[near] * len(part),
        out_shape=[jax.ShapeDtypeStruct(hold.shape[1:], bf16 if offset else f32) for offset in part],
        compiler_params=roomy,
        cost_estimate=small_cost,
    )(hold, taken)


def total_rows(factor, out, own, *landed):
    total = own[...]
    for part in landed:
        total += part[...].astype(f32)
    total = total * factor
    for k in range(out.shape[1] // lanes):
        out[:, k * lanes : (k + 1) * lanes] = total[k : k + 1, :]


def plane_parts(owners, keep, *taken):
    quad = 2 * pair
    count = owners // quad
    direct = [count // 2] if count > 2 else []
    offsets = [k for k in range(count) if k not in direct]

    def along(offset, side):
        return [(i, (i + quad * offset) % owners ^ pair * side) for i in range(owners)]

    hold, give, *straight = merge_terms(offsets, direct, keep, *taken)
    across = lax.ppermute(give, "dp", along(0, 1))
    arrived = [
        lax.ppermute(straight[2 * k + side], "dp", along(offset, side))
        for k, offset in enumerate(direct)
        for side in range(2)
    ]
    own, *parts = split_terms(offsets, hold, across)
    for offset, part in zip(offsets[1:], parts):
        arrived.append(lax.ppermute(part, "dp", along(offset, 0)))
    return own, *arrived


def weight_owned(made, factor):
    owners = lax.axis_size("dp")
    masked, x, back, scale, gain = made
    width = x.shape[1]
    depth = masked.shape[1]
    owned = (width + width * depth) // owners
    if depth != lanes or owned % lanes or owners % (2 * pair):
        unit = x.astype(f32) * scale[:, :1]
        normed = (unit * gain).astype(bf16)
        weight_term = lax.dot_general(normed, masked, contract_rows, preferred_element_type=f32)
        flat = jnp.concatenate([jnp.sum(unit * back, axis=0), weight_term.reshape(-1)]) * factor
        return (), owned, lax.psum_scatter(flat, "dp", scatter_dimension=0, tiled=True)[None, :]
    keep, *give = pair_terms(made, owned // lanes, owners)
    taken = [lax.ppermute(part, "dp", [(i, i ^ 1) for i in range(owners)]) for part in give]
    return plane_parts(owners, keep, *taken), owned, None


def shards(layer_inputs, top_grad, value_grads, weights, norm_gains, counts):
    rows = layer_inputs.shape[1]
    factor = 1.0 / math.sqrt(rows * lax.axis_size("dp"))
    sections = lax.axis_size("section")
    room = -(-rows * 3 // 4 // pack_rows) * pack_rows
    spare = rows - room
    inputs = (counts, layer_inputs, top_grad, value_grads, weights, norm_gains)
    packed, addend, scatter, more, *made = branch_rows(0, room, *inputs)
    parts, owned_size, owned = weight_owned(made, factor)
    result = None
    for hop in range(sections - 1):
        target = sections - 2 - hop
        hops = [(target + 1, target), (target, target + 1)]
        before = result
        if hop:
            packed = pack(scatter, before)
        landed = lax.ppermute(packed, "section", hops)
        if hop:
            updated, more = receive(target, scatter, landed, addend, more, before)
        else:
            updated, more, summed = receive(target, scatter, landed, addend, more, None, parts, owned_size, factor)

        def rest(updated):
            packed, addend, scatter, more, *_ = branch_rows(room, spare, *inputs)
            if hop:
                packed = pack(scatter, before)
            landed = lax.ppermute(packed, "section", hops)
            return receive(target, scatter, landed, addend, more, updated[0])[0]

        updated = lax.cond(more.reshape(()) > 0, rest, lambda updated: updated, updated)
        result = updated[0]
    return (result[None], summed if owned is None else owned)


def solution(mesh):
    placed = (
        P("section", "dp", None),
        P("dp", None),
        P("section", "dp", None),
        P("section", None, None),
        P("section", None),
        P("dp"),
    )
    return jax.shard_map(
        shards,
        mesh=mesh,
        in_specs=placed,
        out_specs=(P("section", "dp", None), P("section", "dp")),
        check_vma=False,
    )
```

```python
import functools
import math

import jax
import jax.numpy as jnp
from jax import lax
from jax.experimental import pallas as pl
from jax.experimental.pallas import tpu as pltpu
from jax.sharding import PartitionSpec as P

eps_norm = 1e-05
lanes = 128
sublanes = 8
pack_rows = 16
tile_width = 512
pair = 2
block_rows = 32
band_width = 256
f32 = jnp.float32
bf16 = jnp.bfloat16
contract_last = (((1,), (1,)), ((), ()))
contract_rows = (((0,), (0,)), ((), ()))
small_cost = pl.CostEstimate(flops=1 << 20, bytes_accessed=1 << 16, transcendentals=0)
roomy = pltpu.CompilerParams(vmem_limit_bytes=32 << 20)
near = pl.BlockSpec(memory_space=pltpu.VMEM)
scalar = pl.BlockSpec(memory_space=pltpu.SMEM)


def far(array):
    return pltpu.with_memory_space_constraint(array, pltpu.HBM)


def cuts(width, step):
    return [pl.ds(at, step) for at in range(0, width, step)]


def one_hot(counts, micro_count, slots, low, size):
    slot = lax.broadcasted_iota(jnp.int32, (slots, size), 0)
    column = lax.broadcasted_iota(jnp.int32, (slots, size), 1) + low
    start = jnp.int32(0)
    pieces = []
    for m in range(micro_count):
        hit = (slot < counts[m]) & (slot + start == column)
        pieces.append(jnp.where(hit, 1.0, 0.0))
        start = start + counts[m]
    return jnp.concatenate(pieces, axis=0).astype(bf16)


def branch_kernel(
    low, counts_far, x_far, top_far, v_far, w_far, gain_far,
    packed, addend, scatter, more, masked, x, back, scale_out, gain,
    counts, top, v, w, sent, ready,
):
    rows, width = addend.shape
    micro_count = counts.shape[0]
    slots = rows // micro_count
    fetches = [
        pltpu.make_async_copy(v_far.at[0], v, ready.at[0]),
        pltpu.make_async_copy(counts_far, counts, ready.at[1]),
        pltpu.make_async_copy(w_far.at[0], w, ready.at[2]),
        pltpu.make_async_copy(x_far.at[0], x, ready.at[3]),
        pltpu.make_async_copy(gain_far, gain, ready.at[4]),
        pltpu.make_async_copy(top_far, top, ready.at[5]),
    ]
    for fetch in fetches:
        fetch.start()
    fetches[0].wait()
    fetches[1].wait()
    slot = lax.broadcasted_iota(jnp.int32, (slots, v.shape[1]), 0)
    for m in range(micro_count):
        piece = v[m * slots : (m + 1) * slots, :]
        masked[m * slots : (m + 1) * slots, :] = jnp.where(slot < counts[m], piece, jnp.zeros_like(piece))
    live = jnp.int32(0)
    for m in range(micro_count):
        live += counts[m]
    more[0] = (live > low + packed.shape[0]).astype(jnp.int32)
    gather = one_hot(counts, micro_count, slots, low, packed.shape[0])
    receives = lax.axis_index("section") < lax.axis_size("section") - 1
    scatter[...] = jnp.where(receives, gather.astype(f32), 0.0).astype(bf16)
    gather = jnp.transpose(gather.astype(f32)).astype(bf16)
    values = masked[...]
    for fetch in fetches[2:5]:
        fetch.wait()
    blocks = [slice(at, at + block_rows) for at in range(0, rows, block_rows)]
    squares = [jnp.zeros((block_rows, lanes), f32) for _ in blocks]
    products = [jnp.zeros((block_rows, lanes), f32) for _ in blocks]
    for tile in range(0, width, band_width):
        here = lax.dot_general(
            values, w[tile : tile + band_width, :], contract_last, preferred_element_type=f32
        )
        back[:, tile : tile + band_width] = here
        for k, part in enumerate(blocks):
            for at in range(0, band_width, lanes):
                cut = pl.ds(tile + at, lanes)
                wide = x[part, cut].astype(f32)
                squares[k] += wide * wide
                products[k] += wide * here[part, at : at + lanes] * gain[:, cut]
    scales = lax.rsqrt(jnp.sum(jnp.concatenate(squares, axis=0), axis=1, keepdims=True) / width + eps_norm)
    pulls = scales * jnp.sum(jnp.concatenate(products, axis=0), axis=1, keepdims=True) / width
    waits = jnp.concatenate(
        [
            lax.broadcasted_iota(jnp.int32, (slots, 1), 0) < jnp.where(receives, counts[m], 0)
            for m in range(micro_count)
        ],
        axis=0,
    )
    spread = (rows, band_width)
    scales = jnp.broadcast_to(scales, spread)
    scale_out[...] = scales[:, :lanes]
    pulls = jnp.broadcast_to(pulls, spread)
    waits = jnp.broadcast_to(waits, spread)
    fetches[5].wait()
    for cut in cuts(width, band_width):
        scaled = gain[:, cut]
        for part in blocks:
            unit = x[part, cut].astype(f32) * scales[part]
            here = back[part, cut]
            own = scales[part] * (scaled * here - unit * pulls[part])
            whole = top[part, cut].astype(f32) + own
            sent[part, cut] = whole.astype(bf16)
            addend[part, cut] = jnp.where(waits[part], own, whole)
        packed[:, cut] = jnp.dot(gather, sent[:, cut], preferred_element_type=f32).astype(bf16)


def branch_rows(low, room, counts, x, top, v, w, gain):
    rows, width = top.shape
    depth = v.shape[2]
    return pl.pallas_call(
        functools.partial(branch_kernel, low),
        in_specs=[pl.BlockSpec(memory_space=pltpu.HBM)] * 6,
        out_specs=[near] * 3 + [scalar] + [near] * 5,
        out_shape=[
            jax.ShapeDtypeStruct((room, width), bf16),
            jax.ShapeDtypeStruct((rows, width), f32),
            jax.ShapeDtypeStruct((rows, room), bf16),
            pltpu.SMEM((1,), jnp.int32),
            jax.ShapeDtypeStruct((rows, depth), bf16),
            jax.ShapeDtypeStruct((rows, width), bf16),
            jax.ShapeDtypeStruct((rows, width), f32),
            jax.ShapeDtypeStruct((rows, lanes), f32),
            jax.ShapeDtypeStruct((1, width), f32),
        ],
        scratch_shapes=[
            pltpu.SMEM(counts.shape, jnp.int32),
            pltpu.VMEM((rows, width), bf16),
            pltpu.VMEM((rows, depth), bf16),
            pltpu.VMEM((width, depth), bf16),
            pltpu.VMEM((rows, width), bf16),
            pltpu.SemaphoreType.DMA((6,)),
        ],
        compiler_params=roomy,
        cost_estimate=small_cost,
    )(*[far(a) for a in (counts, x, top, v, w, gain)])


def pack_kernel(gather, sent, packed):
    for cut in cuts(sent.shape[1], tile_width):
        packed[:, cut] = lax.dot_general(
            gather[...], sent[:, cut], contract_rows, preferred_element_type=f32
        ).astype(bf16)


def pack(gather, sent):
    return pl.pallas_call(
        pack_kernel,
        in_specs=[near, near],
        out_specs=near,
        out_shape=jax.ShapeDtypeStruct((gather.shape[1], sent.shape[1]), bf16),
        compiler_params=roomy,
        cost_estimate=small_cost,
    )(gather, sent)


def receive_kernel(target, first, factor, scatter, received, addend, more, *refs):
    rows, width = addend.shape
    if first:
        *parts, out_far, more_out, owned_far, out, owned, done = refs
    else:
        previous, out_far, more_out, out, done = refs
    more_out[0] = more[0]
    place = scatter[...]
    writes = []
    if not first:
        here = (lax.axis_index("section") == target).astype(f32)
        covered = jnp.sum(place.astype(f32), axis=1, keepdims=True) * here > 0.5
    for k, cut in enumerate(cuts(width, tile_width)):
        total = jnp.dot(place, received[:, cut], preferred_element_type=f32) + addend[:, cut]
        if not first:
            total = jnp.where(covered, total, previous[:, cut].astype(f32))
        out[:, cut] = total.astype(bf16)
        write = pltpu.make_async_copy(out.at[:, cut], out_far.at[0, :, cut], done.at[k])
        write.start()
        writes.append(write)
    if first and parts:
        total_rows(factor, owned, *parts)
        writes.append(pltpu.make_async_copy(owned, owned_far, done.at[width // tile_width]))
        writes[-1].start()
    for write in writes:
        write.wait()


def receive(target, scatter, received, addend, more, previous=None, parts=(), owned=lanes, factor=1.0):
    rows, width = addend.shape
    away = pl.BlockSpec(memory_space=pltpu.HBM)
    first = previous is None
    others = parts if first else [previous]
    outs = [pltpu.HBM((1, rows, width), bf16), pltpu.SMEM(more.shape, more.dtype)]
    scratch = [pltpu.VMEM((rows, width), bf16)]
    if first:
        outs.append(pltpu.HBM((1, owned), f32))
        scratch.append(pltpu.VMEM((1, owned), f32))
    return pl.pallas_call(
        functools.partial(receive_kernel, target, first, factor),
        in_specs=[near, near, near, scalar] + [near] * len(others),
        out_specs=[away, scalar] + [away] * first,
        out_shape=outs,
        scratch_shapes=scratch + [pltpu.SemaphoreType.DMA((width // tile_width + 1,))],
        compiler_params=roomy,
        cost_estimate=small_cost,
    )(scatter, received, addend, more, *others)


def terms_kernel(owned_rows, masked, x, back, scale, gain, keep, give, give_low, total):
    rows, width = x.shape
    values = masked[...]
    gain_rows = width // lanes
    spread = jnp.concatenate([scale[...]] * (band_width // lanes), axis=1)
    for at in range(0, width, band_width):
        cut = pl.ds(at, band_width)
        unit = x[:, cut].astype(f32) * spread
        summed = (unit * back[:, cut]).reshape(rows // sublanes, sublanes, band_width).sum(axis=0)
        summed = jnp.sum(summed, axis=0, keepdims=True)
        for k in range(0, band_width, lanes):
            spot = (at + k) // lanes
            total[spot : spot + 1, :] = summed[:, k : k + lanes]
        normed = (unit * gain[:, cut]).astype(bf16)
        total[gain_rows + at : gain_rows + at + band_width, :] = lax.dot_general(
            normed, values, contract_rows, preferred_element_type=f32
        )
    blocks, padded, _ = keep.shape
    cut = give.shape[1]

    def hand_out(side):
        for j in range(blocks):
            mine = (2 * j + side) * owned_rows
            other = (2 * j + 1 - side) * owned_rows
            keep[j, :owned_rows, :] = total[mine : mine + owned_rows, :]
            give[j] = total[other : other + cut, :].astype(bf16)
            low = total[other + cut : other + owned_rows, :]
            if padded > owned_rows:
                blank = jnp.zeros((padded - owned_rows, lanes), f32)
                keep[j, owned_rows:, :] = blank
                low = jnp.concatenate([low, blank], axis=0)
            give_low[j] = low.astype(bf16)

    side = lax.axis_index("dp") % pair
    for core in range(pair):
        pl.when(side == core)(functools.partial(hand_out, core))


def pair_terms(made, owned_rows, owners):
    padded = -(-owned_rows // pack_rows) * pack_rows
    cut = padded // 2 // pack_rows * pack_rows
    blocks = owners // pair
    return pl.pallas_call(
        functools.partial(terms_kernel, owned_rows),
        in_specs=[near] * len(made),
        out_specs=[near, near, near],
        out_shape=[
            jax.ShapeDtypeStruct((blocks, padded, lanes), f32),
            jax.ShapeDtypeStruct((blocks, cut, lanes), bf16),
            jax.ShapeDtypeStruct((blocks, padded - cut, lanes), bf16),
        ],
        scratch_shapes=[pltpu.VMEM((owners * owned_rows, lanes), f32)],
        compiler_params=roomy,
        cost_estimate=small_cost,
    )(*made)


def merge_kernel(offsets, direct, keep, taken, taken_low, hold, give, *straight):
    chip = lax.axis_index("dp") // pair
    mine, place = chip % 2, chip // 2
    count = keep.shape[0] // 2
    cut = taken.shape[1]

    def total(at, out):
        high = keep[at, :cut, :] + taken[at].astype(f32)
        low = keep[at, cut:, :] + taken_low[at].astype(f32)
        out[:cut, :] = high.astype(out.dtype)
        out[cut:, :] = low.astype(out.dtype)

    for k, offset in enumerate(offsets):
        at = 2 * lax.rem(place + offset, count)
        total(at + mine, hold.at[k])
        total(at + 1 - mine, give.at[k])
    for k, offset in enumerate(direct):
        at = 2 * lax.rem(place + offset, count)
        total(at + mine, straight[2 * k])
        total(at + 1 - mine, straight[2 * k + 1])


def merge_terms(offsets, direct, keep, taken, taken_low):
    block = keep.shape[1:]
    outs = [
        jax.ShapeDtypeStruct((len(offsets),) + block, f32),
        jax.ShapeDtypeStruct((len(offsets),) + block, bf16),
    ] + [jax.ShapeDtypeStruct(block, bf16)] * (2 * len(direct))
    return pl.pallas_call(
        functools.partial(merge_kernel, offsets, direct),
        in_specs=[near, near, near],
        out_specs=[near] * len(outs),
        out_shape=outs,
        compiler_params=roomy,
        cost_estimate=small_cost,
    )(keep, taken, taken_low)


def split_kernel(hold, taken, *parts):
    for k, part in enumerate(parts):
        part[...] = (hold[k] + taken[k].astype(f32)).astype(part.dtype)


def split_terms(part, hold, taken):
    return pl.pallas_call(
        split_kernel,
        in_specs=[near, near],
        out_specs=[near] * len(part),
        out_shape=[jax.ShapeDtypeStruct(hold.shape[1:], bf16 if offset else f32) for offset in part],
        compiler_params=roomy,
        cost_estimate=small_cost,
    )(hold, taken)


def total_rows(factor, out, own, *landed):
    total = own[...]
    for part in landed:
        total += part[...].astype(f32)
    total = total * factor
    for k in range(out.shape[1] // lanes):
        out[:, k * lanes : (k + 1) * lanes] = total[k : k + 1, :]


def plane_parts(owners, keep, *taken):
    quad = 2 * pair
    count = owners // quad
    direct = [count // 2] if count > 2 else []
    offsets = [k for k in range(count) if k not in direct]

    def along(offset, side):
        return [(i, (i + quad * offset) % owners ^ pair * side) for i in range(owners)]

    hold, give, *straight = merge_terms(offsets, direct, keep, *taken)
    across = lax.ppermute(give, "dp", along(0, 1))
    arrived = [
        lax.ppermute(straight[2 * k + side], "dp", along(offset, side))
        for k, offset in enumerate(direct)
        for side in range(2)
    ]
    own, *parts = split_terms(offsets, hold, across)
    for offset, part in zip(offsets[1:], parts):
        arrived.append(lax.ppermute(part, "dp", along(offset, 0)))
    return own, *arrived


def weight_owned(made, factor):
    owners = lax.axis_size("dp")
    masked, x, back, scale, gain = made
    width = x.shape[1]
    depth = masked.shape[1]
    owned = (width + width * depth) // owners
    if depth != lanes or owned % lanes or owners % (2 * pair):
        unit = x.astype(f32) * scale[:, :1]
        normed = (unit * gain).astype(bf16)
        weight_term = lax.dot_general(normed, masked, contract_rows, preferred_element_type=f32)
        flat = jnp.concatenate([jnp.sum(unit * back, axis=0), weight_term.reshape(-1)]) * factor
        return (), owned, lax.psum_scatter(flat, "dp", scatter_dimension=0, tiled=True)[None, :]
    keep, *give = pair_terms(made, owned // lanes, owners)
    taken = [lax.ppermute(part, "dp", [(i, i ^ 1) for i in range(owners)]) for part in give]
    return plane_parts(owners, keep, *taken), owned, None


def shards(layer_inputs, top_grad, value_grads, weights, norm_gains, counts):
    rows = layer_inputs.shape[1]
    factor = 1.0 / math.sqrt(rows * lax.axis_size("dp"))
    sections = lax.axis_size("section")
    room = -(-rows * 3 // 4 // pack_rows) * pack_rows
    spare = rows - room
    inputs = (counts, layer_inputs, top_grad, value_grads, weights, norm_gains)
    packed, addend, scatter, more, *made = branch_rows(0, room, *inputs)
    parts, owned_size, owned = weight_owned(made, factor)
    result = None
    for hop in range(sections - 1):
        target = sections - 2 - hop
        hops = [(target + 1, target), (target, target + 1)]
        before = result
        if hop:
            packed = pack(scatter, before)
        landed = lax.ppermute(packed, "section", hops)
        if hop:
            updated, more = receive(target, scatter, landed, addend, more, before)
        else:
            updated, more, summed = receive(target, scatter, landed, addend, more, None, parts, owned_size, factor)

        def rest(updated):
            packed, addend, scatter, more, *_ = branch_rows(room, spare, *inputs)
            if hop:
                packed = pack(scatter, before)
            landed = lax.ppermute(packed, "section", hops)
            return receive(target, scatter, landed, addend, more, updated[0])[0]

        updated = lax.cond(more.reshape(()) > 0, rest, lambda updated: updated, updated)
        result = updated[0]
    return (result[None], summed if owned is None else owned)


def solution(mesh):
    placed = (
        P("section", "dp", None),
        P("dp", None),
        P("section", "dp", None),
        P("section", None, None),
        P("section", None),
        P("dp"),
    )
    return jax.shard_map(
        shards,
        mesh=mesh,
        in_specs=placed,
        out_specs=(P("section", "dp", None), P("section", "dp")),
        check_vma=False,
    )
```
